128 devices in a mesh: pipe: 2 (over core), shard: 64 (over y, x, z).
Axes of the slice: x: 4, y: 4, z: 4, core: 2. Of those that a mesh axis runs over, the one named last changes fastest.
Arguments:
- latents: bfloat16 [2, 128, 256, 384], P(None, 'shard'), may hold values from -6 to 6
- conditions: bfloat16 [2, 128, 384], P(None, 'shard'), may hold values from -6 to 6
- cotangent: bfloat16 [2, 128, 256, 384], P(None, 'shard'), may hold values from -6 to 6
- w_qkv: bfloat16 [2, 384, 1152], P('pipe', 'shard'), may hold values from -0.3125 to 0.3125
- b_qv: bfloat16 [2, 768], P('pipe', 'shard'), may hold values from -3 to 3
- w_proj: bfloat16 [2, 384, 384], P('pipe', 'shard'), may hold values from -0.875 to 0.875
- b_proj: bfloat16 [2, 384], P('pipe', 'shard'), may hold values from -3 to 3
- w_fc1: bfloat16 [2, 384, 1536], P('pipe', 'shard'), may hold values from -0.3125 to 0.3125
- b_fc1: bfloat16 [2, 1536], P('pipe', 'shard'), may hold values from -3 to 3
- w_fc2: bfloat16 [2, 1536, 384], P('pipe', 'shard'), may hold values from -0.21875 to 0.21875
- b_fc2: bfloat16 [2, 384], P('pipe', 'shard'), may hold values from -3 to 3
- w_ada: bfloat16 [2, 384, 2304], P('pipe', 'shard'), may hold values from -0.4375 to 0.4375
- b_ada: bfloat16 [2, 2304], P('pipe', 'shard'), may hold values from -3 to 3
Outputs:
- section_outputs: bfloat16 [2, 2, 128, 256, 384], P('pipe', None, 'shard')
- input_grads: bfloat16 [2, 2, 128, 256, 384], P('pipe', None, 'shard')
- cond_grad: float32 [2, 128, 384], P(None, 'shard')
- grad_w_qkv: float32 [2, 384, 1152], P('pipe', 'shard')
- grad_b_qv: float32 [2, 768], P('pipe', 'shard')
- grad_w_proj: float32 [2, 384, 384], P('pipe', 'shard')
- grad_b_proj: float32 [2, 384], P('pipe', 'shard')
- grad_w_fc1: float32 [2, 384, 1536], P('pipe', 'shard')
- grad_b_fc1: float32 [2, 1536], P('pipe', 'shard')
- grad_w_fc2: float32 [2, 1536, 384], P('pipe', 'shard')
- grad_b_fc2: float32 [2, 384], P('pipe', 'shard')
- grad_w_ada: float32 [2, 384, 2304], P('pipe', 'shard')
- grad_b_ada: float32 [2, 2304], P('pipe', 'shard')
The draws below stay inside these ranges and needn't reach their ends.
All inputs are finite; a program needn't handle non-finite values.
Results may differ from the reference program's by a relative error of at most 0.018.
The reference program's roundings to bfloat16 on the way count: a program that leaves them out, or rounds other values in their place, can miss the bound.
Values may be sent and summed in bfloat16 or wider, within the bound.
No kernel may reach another device: no remote copies, remote signals or barrier semaphores. Data moves between devices by JAX's collectives and lax.ppermute only.
A program may use at most 192 MiB of HBM per device.

```python
import jax
import jax.numpy as jnp
from jax import lax

D = 384
HEADS = 6
HEAD = 64
FF = 1536
SEQ = 256
MICRO = 2
LATENTS = 128
N_PIPE = 2


def clipped_normal(key, shape):
    values = jax.random.normal(key, shape, jnp.float32)
    return jnp.clip(values, -6.0, 6.0)


def draw_latents(key, part):
    key = jax.random.fold_in(key, 11)
    return clipped_normal(key, (MICRO, LATENTS, SEQ, D)).astype(jnp.bfloat16)


def draw_conditions(key, part):
    key = jax.random.fold_in(key, 12)
    return clipped_normal(key, (MICRO, LATENTS, D)).astype(jnp.bfloat16)


def draw_cotangent(key, part):
    key = jax.random.fold_in(key, 13)
    return clipped_normal(key, (MICRO, LATENTS, SEQ, D)).astype(jnp.bfloat16)


def steps_of(rng, shape, pieces, smallest, high):
    loudness, own = 1.0, jax.random.fold_in(rng, 6)
    for position, blocks in pieces:
        steps = jnp.exp(jax.random.uniform(jax.random.fold_in(own, position), (blocks,), jnp.float32, smallest / len(pieces), high / len(pieces)))
        loudness = loudness * jnp.repeat(steps, shape[position] // blocks).reshape([-1 if axis == position else 1 for axis in range(len(shape))])
    return loudness


def scatter_about(stream_key, dims, width, reach, pieces=(), held_as=jnp.bfloat16):
    gain = steps_of(stream_key, dims, pieces, -0.22, 0.18) if pieces else 1.0
    result = jax.random.normal(stream_key, dims, jnp.float32) * width * gain
    return jnp.minimum(jnp.maximum(result, -reach), reach).astype(held_as)


def setup_inputs(seed: int = 0) -> dict:
    streams_of = jax.random.split(jax.random.key(seed), 14)
    latents = draw_latents(jax.random.fold_in(streams_of[13], 71), 0)
    conditions = draw_conditions(jax.random.fold_in(streams_of[13], 71), 0)
    cotangent = draw_cotangent(jax.random.fold_in(streams_of[13], 71), 0)
    w_qkv = scatter_about(streams_of[3], (N_PIPE, D, 3 * D), D ** -0.5, 0.3125, ((0, 2), (1, 64)))
    b_qv = scatter_about(streams_of[4], (N_PIPE, 2 * D), 0.5, 3.0, ((0, 2), (1, 64)))
    w_proj = scatter_about(streams_of[5], (N_PIPE, D, D), (D // 8) ** -0.5, 0.875, ((0, 2), (1, 64)))
    b_proj = scatter_about(streams_of[6], (N_PIPE, D), 0.5, 3.0, ((0, 2), (1, 64)))
    w_fc1 = scatter_about(streams_of[7], (N_PIPE, D, FF), D ** -0.5, 0.3125, ((0, 2), (1, 64)))
    b_fc1 = scatter_about(streams_of[8], (N_PIPE, FF), 0.5, 3.0, ((0, 2), (1, 64)))
    w_fc2 = scatter_about(streams_of[9], (N_PIPE, FF, D), (FF // 2) ** -0.5, 0.21875, ((0, 2), (1, 64)))
    b_fc2 = scatter_about(streams_of[10], (N_PIPE, D), 0.5, 3.0, ((0, 2), (1, 64)))
    w_ada = scatter_about(streams_of[11], (N_PIPE, D, 6 * D), (D // 2) ** -0.5, 0.4375, ((0, 2), (1, 64)))
    b_ada = scatter_about(streams_of[12], (N_PIPE, 6 * D), 0.5, 3.0, ((0, 2), (1, 64)))
    return {"latents": latents, "conditions": conditions, "cotangent": cotangent, "w_qkv": w_qkv, "b_qv": b_qv, "w_proj": w_proj, "b_proj": b_proj, "w_fc1": w_fc1, "b_fc1": b_fc1, "w_fc2": w_fc2, "b_fc2": b_fc2, "w_ada": w_ada, "b_ada": b_ada}


@jax.custom_vjp
def reduced_precision(v):
    return lax.optimization_barrier(v.astype(jnp.bfloat16)).astype(jnp.float32)

@jax.custom_vjp
def low_back(v):
    return v

def low_keep(v):
    return (reduced_precision(v), None)

def low_pass(kept, grad):
    return (grad,)

def back_keep(v):
    return (v, None)

def back_low(kept, grad):
    return (reduced_precision(grad),)
reduced_precision.defvjp(low_keep, low_pass)
low_back.defvjp(back_keep, back_low)
EPSILON = 1e-06

def matmul_high(left, right):
    return jnp.matmul(left, right, precision=lax.Precision.HIGHEST)

def norm_rows(values):
    centre = values - lax.optimization_barrier(jnp.mean(values, axis=-1, keepdims=True))
    spread = lax.optimization_barrier(jnp.mean(centre * centre, axis=-1, keepdims=True))
    return centre * lax.rsqrt(spread + EPSILON)

def gelu_tanh(values):
    return jax.nn.gelu(values, approximate=True)

def diffusion_transformer_block(hidden_state, conditions, model_weights):
    w_qkv, b_qv, w_proj, b_proj, w_fc1, b_fc1, w_fc2, b_fc2, w_ada, b_ada = model_weights
    groups, length, features = hidden_state.shape
    modulation = low_back(matmul_high(reduced_precision(jax.nn.silu(conditions)), w_ada) + b_ada)
    shift_one, scale_one, gate_one, shift_two, scale_two, gate_two = jnp.split(modulation[:, None, :], 6, axis=-1)
    attn_in = reduced_precision(norm_rows(hidden_state) * (1.0 + scale_one) + shift_one)
    qkv_bias = jnp.concatenate([b_qv[:features], jnp.zeros((features,), jnp.float32), b_qv[features:]])
    qkv_all = reduced_precision(low_back(matmul_high(attn_in, w_qkv) + qkv_bias))
    queries, keys_all, values_all = [portion.reshape(groups, length, HEADS, HEAD) for portion in jnp.split(qkv_all, 3, axis=-1)]
    scores = jnp.einsum('gqhe,gkhe->ghqk', queries, keys_all, precision=lax.Precision.HIGHEST) * HEAD ** (-0.5)
    scores = low_back(scores)
    shifted = jnp.exp(scores - lax.optimization_barrier(jnp.max(scores, axis=-1, keepdims=True)))
    probabilities = reduced_precision(shifted / lax.optimization_barrier(jnp.sum(shifted, axis=-1, keepdims=True)))
    attended = jnp.einsum('ghqk,gkhe->gqhe', probabilities, values_all, precision=lax.Precision.HIGHEST)
    attended = reduced_precision(low_back(attended.reshape(groups, length, features)))
    branch_attn = low_back(matmul_high(attended, w_proj) + b_proj)
    middle = hidden_state + gate_one * branch_attn
    mlp_in = reduced_precision(norm_rows(middle) * (1.0 + scale_two) + shift_two)
    pre_act = low_back(matmul_high(mlp_in, w_fc1) + b_fc1)
    activated = reduced_precision(gelu_tanh(pre_act))
    branch_mlp = low_back(matmul_high(activated, w_fc2) + b_fc2)
    return middle + gate_two * branch_mlp

def chain(latents_in, conditions, offset, model_weights):
    leading_section_weights = tuple((member[0] for member in model_weights))
    trailing_section_weights = tuple((member[1] for member in model_weights))
    section_input = low_back(latents_in)
    passed_along = diffusion_transformer_block(section_input, conditions, leading_section_weights)
    sent_rows = reduced_precision(passed_along)
    arrived_rows = low_back(sent_rows) + offset
    emitted_rows = reduced_precision(diffusion_transformer_block(arrived_rows, conditions, trailing_section_weights))
    return (emitted_rows, sent_rows)

def reference(latents, conditions, cotangent, w_qkv, b_qv, w_proj, b_proj, w_fc1, b_fc1, w_fc2, b_fc2, w_ada, b_ada):
    model_weights = tuple((member.astype(jnp.float32) for member in (w_qkv, b_qv, w_proj, b_proj, w_fc1, b_fc1, w_fc2, b_fc2, w_ada, b_ada)))
    latent_total = MICRO * LATENTS
    group_size = 16

    def regroup(array):
        return array.astype(jnp.float32).reshape((latent_total // group_size, group_size) + array.shape[2:])

    def one_group(totals, batch_items):
        lat_group, cond_group, cot_group = batch_items
        offset = jnp.zeros_like(lat_group)
        emitted_rows, pullback, sent_rows = jax.vjp(chain, lat_group, cond_group, offset, model_weights, has_aux=True)
        grad_in, grad_cond, grad_mid, grad_params = pullback(cot_group)
        totals = tuple((former + latter for former, latter in zip(totals, grad_params)))
        return (totals, (sent_rows.astype(jnp.bfloat16), emitted_rows.astype(jnp.bfloat16), grad_in.astype(jnp.bfloat16), grad_mid.astype(jnp.bfloat16), grad_cond))
    zeros = tuple((jnp.zeros_like(member) for member in model_weights))
    totals, stacked = lax.scan(one_group, zeros, (regroup(latents), regroup(conditions), regroup(cotangent)))
    shape_rows = (MICRO, LATENTS, SEQ, D)
    passed_along = stacked[0].reshape(shape_rows)
    emitted_rows = stacked[1].reshape(shape_rows)
    grad_in = stacked[2].reshape(shape_rows)
    grad_mid = stacked[3].reshape(shape_rows)
    cond_grad = stacked[4].reshape(MICRO, LATENTS, D)
    section_outputs = jnp.stack([passed_along, emitted_rows])
    input_grads = jnp.stack([grad_in, grad_mid])
    return (section_outputs, input_grads, cond_grad, totals[0], totals[1], totals[2], totals[3], totals[4], totals[5], totals[6], totals[7], totals[8], totals[9])
```

```python
import functools

import jax
import jax.numpy as jnp
from jax import lax
from jax.experimental import pallas as pl
from jax.experimental.pallas import tpu as pltpu
from jax.sharding import PartitionSpec as P

F = jnp.float32
B = jnp.bfloat16
D = 384
HEADS = 6
HEAD = 64
FF = 1536
SEQ = 256
EPS = 1e-06
CHIPS = 64
ROWS = 512
EXP = 512

C_QKV, C_PROJ, C_FC1, C_ADA, C_FC2, C_END = 0, 1152, 1536, 3072, 5376, 6528
SPARE = 6
K0 = 0.7978845608028654
K1 = 0.044715

NN = (1, 0)
NT = (1, 1)
TN = (0, 0)


def dot(a, b, dims=NN):
    return lax.dot_general(a, b, (((dims[0],), (dims[1],)), ((), ())), preferred_element_type=F)


def selector():
    row = lax.broadcasted_iota(jnp.int32, (EXP, D), 0)
    col = lax.broadcasted_iota(jnp.int32, (EXP, D), 1)
    r = row & 7
    return ((col == (row >> 3) * 6 + r) & (r < 6)).astype(F).astype(B)


def row_kind(shape, dim, kind):
    return (lax.broadcasted_iota(jnp.int32, shape, dim) & 7) == kind


def stats(v):
    centre = v - jnp.mean(v, axis=-1, keepdims=True)
    inv = lax.rsqrt(jnp.mean(centre * centre, axis=-1, keepdims=True) + EPS)
    return centre * inv, inv


def norm_back(g, n, inv):
    mg = jnp.mean(g, axis=-1, keepdims=True)
    mgn = jnp.mean(g * n, axis=-1, keepdims=True)
    return inv * (g - mg - n * mgn)


def head_masks():
    lane = lax.broadcasted_iota(jnp.int32, (1, 128), 1)
    low = (lane < HEAD).astype(F)
    return low.astype(B), (1.0 - low).astype(B)


def unpack(g, sel, w):
    sel[...] = selector()

    def step(i, _):
        at = pl.multiple_of(i * 256, 256)
        w["main"][:, pl.ds(at, 256)] = dot(sel[...], g[:, pl.ds(at, 256)], TN).astype(B)
        return 0

    lax.fori_loop(0, C_ADA // 256, step, 0)
    pick = row_kind((8, EXP), 1, 6).astype(F).astype(B)
    w["bias"][...] = dot(pick, g[:, :C_ADA])
    pick7 = row_kind((8, EXP), 1, 7).astype(F).astype(B)
    w["bias2"][...] = dot(pick7, g[:, C_PROJ:C_FC1])

    def step2(i, _):
        at = pl.multiple_of(i * 128, 128)
        parts = [
            g[pl.ds(at, 128), C_FC2 + a * D : C_FC2 + (a + 1) * D].astype(F).reshape(16, 8, D)
            for a in range(3)
        ]
        whole = jnp.concatenate(parts, axis=1).reshape(D, D).astype(B)
        w["fc2"][pl.ds(pl.multiple_of(i * D, D), D), :] = whole
        return 0

    lax.fori_loop(0, 4, step2, 0)


def modulate(cond, g, sel, mod):
    c = cond[...]
    act = (c * jax.nn.sigmoid(c)).astype(B)
    wide = dot(act, sel[...], NT)
    wide = jnp.where(row_kind((8, EXP), 1, 6), 1.0, wide).astype(B)
    mod[...] = dot(wide, g[:, C_ADA:C_FC2])


def forward(x, w, mod, k, y):
    main, bias, fc2 = w["main"], w["bias"], w["fc2"]

    def ln_in(i, _):
        rows = pl.ds(pl.multiple_of(i * 128, 128), 128)
        lat = pl.ds(i // 2, 1)
        n, _ = stats(x[rows, :].astype(F))
        k["ain"][rows, :] = (n * (1.0 + mod[lat, D : 2 * D]) + mod[lat, :D]).astype(B)
        return 0

    lax.fori_loop(0, 4, ln_in, 0)

    for c in range(3):
        cs = slice(c * D, (c + 1) * D)
        k["qkv"][:, cs] = (dot(k["ain"][...], main[:, cs]) + bias[0:1, cs]).astype(B)

    low, high = head_masks()

    def attend(i, _):
        rows = pl.ds(pl.multiple_of((i // 3) * SEQ, SEQ), SEQ)
        at = (i % 3) * 128
        q = k["qkv"][rows, pl.ds(pl.multiple_of(at, 128), 128)]
        key = k["qkv"][rows, pl.ds(pl.multiple_of(D + at, 128), 128)]
        v = k["qkv"][rows, pl.ds(pl.multiple_of(2 * D + at, 128), 128)]
        total = None
        for h, m in enumerate((low, high)):
            s = dot(key, q * m, NT) * 0.125
            top = jnp.max(s, axis=0, keepdims=True)
            e = jnp.exp(s - top)
            t = jnp.sum(e, axis=0, keepdims=True)
            p = (e * (1.0 / t)).astype(B)
            k["lse"][i, h : h + 1, :] = top + jnp.log(t)
            part = dot(p, v * m, TN)
            total = part if total is None else total + part
        k["att"][rows, pl.ds(pl.multiple_of(at, 128), 128)] = total.astype(B)
        return 0

    lax.fori_loop(0, 6, attend, 0)

    def mid(i, _):
        rows = pl.ds(pl.multiple_of(i * 128, 128), 128)
        lat = pl.ds(i // 2, 1)
        o = dot(k["att"][rows, :], main[:, C_PROJ:C_FC1]) + bias[0:1, C_PROJ:C_FC1]
        x1 = x[rows, :].astype(F) + mod[lat, 2 * D : 3 * D] * o
        k["o"][rows, :] = o
        k["x1"][rows, :] = x1
        n, _ = stats(x1)
        k["min"][rows, :] = (n * (1.0 + mod[lat, 4 * D : 5 * D]) + mod[lat, 3 * D : 4 * D]).astype(B)
        return 0

    lax.fori_loop(0, 4, mid, 0)

    def mlp(i, _):
        at = pl.multiple_of(i * 256, 256)
        cs = pl.ds(at, 256)
        ws = pl.ds(pl.multiple_of(C_FC1 + at, 256), 256)
        z = dot(k["min"][...], main[:, ws]) + bias[0:1, ws]
        zz = z * z
        t = jnp.tanh(z * (K0 + K0 * K1 * zz))
        half = 0.5 + 0.5 * t
        k["act"][:, cs] = (z * half).astype(B)
        k["slope"][:, cs] = half + (0.5 * z) * (1.0 - t * t) * (K0 + 3.0 * K0 * K1 * zz)
        return 0

    lax.fori_loop(0, 6, mlp, 0)

    def out(i, _):
        rows = pl.ds(pl.multiple_of(i * 128, 128), 128)
        lat = pl.ds(i // 2, 1)
        f = dot(k["act"][rows, :], fc2[...]) + w["bias2"][0:1, :]
        k["f"][rows, :] = f
        y[rows, :] = (k["x1"][rows, :] + mod[lat, 5 * D : 6 * D] * f).astype(B)
        return 0

    lax.fori_loop(0, 4, out, 0)


def token_sum(v):
    return jnp.sum(v, axis=0, keepdims=True)


def spread(sel, v, ones):
    wide = dot(sel[...], v, NT)
    return jnp.where(row_kind((EXP, 1), 0, 6), 1.0, wide).astype(B) if ones else wide.astype(B)


def backward(grad, x, cond, g, sel, w, mod, k, t, dx, dc, put):
    main, fc2 = w["main"], w["fc2"]
    dmod = t["dmod"]
    dmod[...] = jnp.zeros_like(dmod)

    def add_mod(lat, piece, v):
        cs = slice(piece * D, (piece + 1) * D)
        dmod[lat, cs] = dmod[lat, cs] + v

    t["db2"][...] = jnp.zeros_like(t["db2"])

    def start(i, _):
        rows = pl.ds(pl.multiple_of(i * 128, 128), 128)
        lat = pl.ds(i // 2, 1)
        gr = grad[rows, :].astype(F)
        df = (gr * mod[lat, 5 * D : 6 * D]).astype(B)
        t["df"][rows, :] = df
        add_mod(lat, 5, token_sum(gr * k["f"][rows, :]))
        t["db2"][0:1, :] = t["db2"][0:1, :] + token_sum(df.astype(F))
        return 0

    lax.fori_loop(0, 4, start, 0)

    def dmlp(i, _):
        cs = pl.ds(pl.multiple_of(i * 256, 256), 256)
        da = dot(t["df"][...], fc2[cs, :], NT)
        t["dz"][:, cs] = (da * k["slope"][:, cs]).astype(B)
        return 0

    lax.fori_loop(0, 6, dmlp, 0)

    t["wide"][...] = spread(sel, k["min"][...], True)

    def dw1(i, _):
        at = pl.multiple_of(i * 256, 256)
        put(pl.ds(0, EXP), pl.ds(pl.multiple_of(C_FC1 + at, 256), 256), dot(t["wide"][...], t["dz"][:, pl.ds(at, 256)]).astype(B))
        return 0

    lax.fori_loop(0, 6, dw1, 0)

    for c in range(4):
        part = dot(k["act"][:, c * D : (c + 1) * D], t["df"][...], TN).reshape(16, 24, D)
        for a in range(3):
            put(
                slice(c * 128, (c + 1) * 128),
                slice(C_FC2 + a * D, C_FC2 + (a + 1) * D),
                part[:, 8 * a : 8 * a + 8, :].reshape(128, D).astype(B),
            )

    def dmid(i, _):
        rows = pl.ds(pl.multiple_of(i * 128, 128), 128)
        lat = pl.ds(i // 2, 1)
        dmin = dot(t["dz"][rows, :], main[:, C_FC1:C_ADA], NT)
        n, inv = stats(k["x1"][rows, :])
        add_mod(lat, 4, token_sum(dmin * n))
        add_mod(lat, 3, token_sum(dmin))
        d1 = grad[rows, :].astype(F) + norm_back(dmin * (1.0 + mod[lat, 4 * D : 5 * D]), n, inv)
        t["dx1"][rows, :] = d1
        do = (d1 * mod[lat, 2 * D : 3 * D]).astype(B)
        add_mod(lat, 2, token_sum(d1 * k["o"][rows, :]))
        t["df"][rows, :] = do
        t["datt"][rows, :] = dot(do, main[:, C_PROJ:C_FC1], NT).astype(B)
        return 0

    lax.fori_loop(0, 4, dmid, 0)

    t["wide"][...] = spread(sel, k["att"][...], True)
    dp = dot(t["wide"][...], t["df"][...])
    dp = jnp.where(row_kind((EXP, 1), 0, 7), t["db2"][0:1, :], dp)
    put(slice(0, EXP), slice(C_PROJ, C_FC1), dp.astype(B))

    low, high = head_masks()

    def dattend(i, _):
        rows = pl.ds(pl.multiple_of((i // 3) * SEQ, SEQ), SEQ)
        at = (i % 3) * 128
        qs = pl.ds(pl.multiple_of(at, 128), 128)
        ks = pl.ds(pl.multiple_of(D + at, 128), 128)
        vs = pl.ds(pl.multiple_of(2 * D + at, 128), 128)
        q = k["qkv"][rows, qs]
        key = k["qkv"][rows, ks]
        v = k["qkv"][rows, vs]
        da = t["datt"][rows, qs]
        dq = dk = dv = None
        for h, m in enumerate((low, high)):
            qm = q * m
            dam = da * m
            s = dot(key, qm, NT) * 0.125
            p = jnp.exp(s - k["lse"][i, h : h + 1, :])
            dp = dot(v, dam, NT)
            ds = (p * (dp - jnp.sum(p * dp, axis=0, keepdims=True))).astype(B)
            v1 = dot(p.astype(B), dam)
            k1 = dot(ds, qm)
            q1 = dot(ds, key * m, TN)
            dv = v1 if dv is None else dv + v1
            dk = k1 if dk is None else dk + k1
            dq = q1 if dq is None else dq + q1
        t["dqkv"][rows, qs] = (dq * 0.125).astype(B)
        t["dqkv"][rows, ks] = (dk * 0.125).astype(B)
        t["dqkv"][rows, vs] = dv.astype(B)
        return 0

    lax.fori_loop(0, 6, dattend, 0)

    t["wide"][...] = spread(sel, k["ain"][...], True)

    def dwq(i, _):
        cs = pl.ds(pl.multiple_of(i * 384, 128), 384)
        put(pl.ds(0, EXP), cs, dot(t["wide"][...], t["dqkv"][:, cs]).astype(B))
        return 0

    lax.fori_loop(0, 3, dwq, 0)

    def dlast(i, _):
        rows = pl.ds(pl.multiple_of(i * 128, 128), 128)
        lat = pl.ds(i // 2, 1)
        dain = dot(t["dqkv"][rows, :], main[:, C_QKV:C_PROJ], NT)
        n, inv = stats(x[rows, :].astype(F))
        add_mod(lat, 1, token_sum(dain * n))
        add_mod(lat, 0, token_sum(dain))
        back = norm_back(dain * (1.0 + mod[lat, D : 2 * D]), n, inv)
        dx[rows, :] = (t["dx1"][rows, :] + back).astype(B)
        return 0

    lax.fori_loop(0, 4, dlast, 0)

    dm = dmod[...].astype(B)
    c = cond[...]
    sig = jax.nn.sigmoid(c)
    act = (c * sig).astype(B)
    live = lax.broadcasted_iota(jnp.int32, (8, 1), 0) < 2
    dm = jnp.where(live, dm.astype(F), 0.0)
    wide = dot(sel[...], act, NT)
    wide = jnp.where(row_kind((EXP, 1), 0, 6), 1.0, wide).astype(B)
    for i in range(3):
        at = i * 768
        put(slice(0, EXP), slice(C_ADA + at, C_ADA + at + 768), dot(wide, dm[:, at : at + 768].astype(B)).astype(B))
    dwide = dot(dm.astype(B), g[:, C_ADA:C_FC2], NT)
    dact = lax.dot_general(
        dwide, sel[...].astype(F), (((1,), (0,)), ((), ())), precision=lax.Precision.HIGHEST, preferred_element_type=F
    )
    dc[...] = dact * (sig * (1.0 + c * (1.0 - sig)))


KEEP = (
    ("ain", (ROWS, D), B),
    ("qkv", (ROWS, 3 * D), B),
    ("lse", (6, 8, SEQ), F),
    ("att", (ROWS, D), B),
    ("o", (ROWS, D), F),
    ("x1", (ROWS, D), F),
    ("min", (ROWS, D), B),
    ("slope", (ROWS, FF), F),
    ("act", (ROWS, FF), B),
    ("f", (ROWS, D), F),
)
WEIGHTS = (("main", (D, C_ADA), B), ("bias", (8, C_ADA), F), ("bias2", (8, D), F), ("fc2", (FF, D), B))
TEMPS = (
    ("dmod", (8, 6 * D), F),
    ("db2", (8, D), F),
    ("df", (ROWS, D), B),
    ("dz", (ROWS, FF), B),
    ("wide", (EXP, ROWS), B),
    ("dx1", (ROWS, D), F),
    ("datt", (ROWS, D), B),
    ("dqkv", (ROWS, 3 * D), B),
)
SEL = (("sel", (EXP, D), B),)
MOD = (("mod", (8, 6 * D), F),)


def buffers(table):
    return [pltpu.VMEM(shape, dtype) for _, shape, dtype in table]


def shapes(table):
    return [jax.ShapeDtypeStruct(shape, dtype) for _, shape, dtype in table]


def named(table, refs):
    return {name: ref for (name, _, _), ref in zip(table, refs)}


def fetch(pick, first, second, into, sem, cols=None):
    def go(ref):
        src = ref if cols is None else ref.at[:, cols[0] : cols[1]]
        copy = pltpu.make_async_copy(src, into, sem)
        copy.start()
        copy.wait()

    @pl.when(pick)
    def _():
        go(first)

    @pl.when(jnp.logical_not(pick))
    def _():
        go(second)


def front_kernel(core, own, other, x, cond, *refs):
    n_keep, n_w = len(KEEP), len(WEIGHTS)
    y = refs[0]
    k = named(KEEP, refs[1 : 1 + n_keep])
    w = named(WEIGHTS, refs[1 + n_keep : 1 + n_keep + n_w])
    mod, g, sel, sem = refs[1 + n_keep + n_w :]
    fetch(core[0] == 0, own, other, g, sem)
    unpack(g, sel, w)
    modulate(cond, g, sel, mod)
    forward(x, w, mod, k, y)


def turn_kernel(core, own, other, x, cond, grad, y, dx, dc, pack, *refs):
    n_keep, n_w, n_t = len(KEEP), len(WEIGHTS), len(TEMPS)
    k = named(KEEP, refs[:n_keep])
    w = named(WEIGHTS, refs[n_keep : n_keep + n_w])
    t = named(TEMPS, refs[n_keep + n_w : n_keep + n_w + n_t])
    mod, g, sel, sem = refs[n_keep + n_w + n_t :]
    fetch(core[0] == 1, own, other, g, sem)
    unpack(g, sel, w)
    modulate(cond, g, sel, mod)
    forward(x, w, mod, k, y)

    def put(rows, cols, value):
        pack[rows, cols] = value

    backward(grad, x, cond, g, sel, w, mod, k, t, dx, dc, put)


def back_kernel(core, own, other, x, cond, grad, *refs):
    n_keep, n_w, n_t = len(KEEP), len(WEIGHTS), len(TEMPS)
    k = named(KEEP, refs[:n_keep])
    w = named(WEIGHTS, refs[n_keep : n_keep + n_w])
    mod, dx, dc, pack = refs[n_keep + n_w : n_keep + n_w + 4]
    refs = refs[n_keep + n_w + 4 :]
    t = named(TEMPS, refs[:n_t])
    g, sel, sem = refs[n_t:]
    sel[...] = selector()
    fetch(core[0] == 0, own, other, g.at[:, C_ADA:C_FC2], sem, (C_ADA, C_FC2))

    def put(rows, cols, value):
        pack[rows, cols] = value

    backward(grad, x, cond, g, sel, w, mod, k, t, dx, dc, put)


VM = pl.BlockSpec(memory_space=pltpu.VMEM)
ANY = pl.BlockSpec(memory_space=pl.ANY)
SM = pl.BlockSpec(memory_space=pltpu.SMEM)
PARAMS = pltpu.CompilerParams(vmem_limit_bytes=60 * 1024 * 1024)
G_BUF = pltpu.VMEM((EXP, C_END), B)
SEL_BUF = pltpu.VMEM((EXP, D), B)
SEM = pltpu.SemaphoreType.DMA
ROWS_OUT = jax.ShapeDtypeStruct((ROWS, D), B)
COND_OUT = jax.ShapeDtypeStruct((8, D), F)
PACK_OUT = jax.ShapeDtypeStruct((EXP, C_END), B)


def front(core, own, other, x, cond):
    outs = [ROWS_OUT] + shapes(KEEP) + shapes(WEIGHTS) + shapes(MOD)
    return pl.pallas_call(
        front_kernel,
        out_shape=outs,
        in_specs=[SM, ANY, ANY, VM, VM],
        out_specs=[VM] * len(outs),
        scratch_shapes=[G_BUF, SEL_BUF, SEM],
        compiler_params=PARAMS,
        name="front",
    )(core, own, other, x, cond)


def turn(core, own, other, x, cond, grad):
    return pl.pallas_call(
        turn_kernel,
        out_shape=[ROWS_OUT, ROWS_OUT, COND_OUT, PACK_OUT],
        in_specs=[SM, ANY, ANY, VM, VM, VM],
        out_specs=[VM] * 4,
        scratch_shapes=buffers(KEEP) + buffers(WEIGHTS) + buffers(TEMPS) + buffers(MOD) + [G_BUF, SEL_BUF, SEM],
        compiler_params=PARAMS,
        name="turn",
    )(core, own, other, x, cond, grad)


def back(core, own, other, x, cond, grad, kept):
    return pl.pallas_call(
        back_kernel,
        out_shape=[ROWS_OUT, COND_OUT, PACK_OUT],
        in_specs=[SM, ANY, ANY, VM, VM, VM] + [VM] * len(kept),
        out_specs=[VM] * 3,
        scratch_shapes=buffers(TEMPS) + [G_BUF, SEL_BUF, SEM],
        compiler_params=PARAMS,
        name="back",
    )(core, own, other, x, cond, grad, *kept)


def line_up(j, w_qkv, b_qv, w_proj, b_proj, w_fc1, b_fc1, w_fc2, b_fc2, w_ada, b_ada):
    main = jnp.concatenate([w_qkv, w_proj, w_fc1, w_ada], axis=1)
    line = jnp.zeros((C_FC2,), B)
    at_qv = jnp.where(j < 32, 12 * j, 12 * j + D)
    line = lax.dynamic_update_slice(line, b_qv, (at_qv,))
    line = lax.dynamic_update_slice(line, b_proj, (C_PROJ + 6 * j,))
    line = lax.dynamic_update_slice(line, b_fc1, (C_FC1 + 24 * j,))
    line = lax.dynamic_update_slice(line, b_ada, (C_ADA + 36 * j,))
    spare = lax.dynamic_update_slice(jnp.zeros((C_FC2,), B), b_fc2, (C_PROJ + 6 * j,))
    top = jnp.concatenate([main, line[None], spare[None]], axis=0)
    return jnp.concatenate([top, w_fc2[:8], w_fc2[8:16], w_fc2[16:]], axis=1)


def swap(x):
    return lax.ppermute(x, "pipe", [(0, 1), (1, 0)])


def to_all(block):
    copies = jnp.broadcast_to(block[None], (CHIPS, *block.shape))
    return lax.all_to_all(copies, "shard", 0, 0, tiled=True).reshape(EXP, block.shape[1])


def shards(latents, conditions, cotangent, w_qkv, b_qv, w_proj, b_proj, w_fc1, b_fc1, w_fc2, b_fc2, w_ada, b_ada):
    p = lax.axis_index("pipe")
    j = lax.axis_index("shard")
    first = p == 0
    core = p.reshape(1).astype(jnp.int32)
    own = to_all(line_up(j, w_qkv[0], b_qv[0], w_proj[0], b_proj[0], w_fc1[0], b_fc1[0], w_fc2[0], b_fc2[0], w_ada[0], b_ada[0]))
    other = swap(own)
    x = lax.dynamic_index_in_dim(latents, p, 0, keepdims=False).reshape(ROWS, D)
    cot = lax.dynamic_index_in_dim(cotangent, p, 0, keepdims=False).reshape(ROWS, D)
    cond = lax.dynamic_index_in_dim(conditions, p, 0, keepdims=False).astype(F)
    cond = jnp.concatenate([cond, jnp.zeros((6, D), F)], axis=0)

    h, *kept = front(core, own, other, x, cond)
    y, dx1, dc1, pack1 = turn(core, own, other, h, cond, cot)
    dx0, dc0, pack0 = back(core, own, other, x, cond, dx1, kept)

    def pair(for_first, for_second):
        keep = jnp.where(first, for_first, for_second)
        came = swap(jnp.where(first, for_second, for_first))
        both = jnp.where(first, jnp.stack([keep, came]), jnp.stack([came, keep]))
        return both.reshape(1, 2, 2, SEQ, D)

    section_outputs = pair(h, y)
    input_grads = pair(dx0, dx1)
    dc = (dc0 + dc1)[:2]
    dc_other = swap(dc)
    cond_grad = jnp.where(first, jnp.stack([dc, dc_other]), jnp.stack([dc_other, dc]))

    mine = jnp.where(first, pack0, pack1)
    came = swap(jnp.where(first, pack1, pack0))
    total = (mine.astype(F) + came.astype(F)).astype(B).reshape(CHIPS, 8, C_END)
    parts = lax.all_to_all(total, "shard", 0, 0, tiled=True)
    done = jnp.sum(parts.astype(F), axis=0)

    rows = done[:6]
    at_qv = jnp.where(j < 32, 12 * j, 12 * j + D)
    line = done[6]
    outs = (
        rows[:, C_QKV:C_PROJ],
        lax.dynamic_slice(line, (at_qv,), (12,)),
        rows[:, C_PROJ:C_FC1],
        lax.dynamic_slice(line, (C_PROJ + 6 * j,), (6,)),
        rows[:, C_FC1:C_ADA],
        lax.dynamic_slice(line, (C_FC1 + 24 * j,), (24,)),
        done[:, C_FC2:].reshape(8, 3, D).transpose(1, 0, 2).reshape(24, D),
        lax.dynamic_slice(done[7], (C_PROJ + 6 * j,), (6,)),
        rows[:, C_ADA:C_FC2],
        lax.dynamic_slice(line, (C_ADA + 36 * j,), (36,)),
    )
    return (section_outputs, input_grads, cond_grad) + tuple(o[None] for o in outs)


def solution(mesh):
    rows = P(None, "shard", None, None)
    wide = P("pipe", "shard", None)
    thin = P("pipe", "shard")
    both = P("pipe", None, "shard", None, None)
    pairs = (wide, thin) * 5
    return jax.shard_map(
        shards,
        mesh=mesh,
        in_specs=(rows, P(None, "shard", None), rows) + pairs,
        out_specs=(both, both, P(None, "shard", None)) + pairs,
        check_vma=False,
    )
```

```python
import functools

import jax
import jax.numpy as jnp
from jax import lax
from jax.experimental import pallas as pl
from jax.experimental.pallas import tpu as pltpu
from jax.sharding import PartitionSpec as P

F = jnp.float32
B = jnp.bfloat16
D = 384
HEADS = 6
HEAD = 64
FF = 1536
SEQ = 256
EPS = 1e-06
CHIPS = 64
ROWS = 512
EXP = 512

C_QKV, C_PROJ, C_FC1, C_ADA, C_FC2, C_END = 0, 1152, 1536, 3072, 5376, 6528
HALF = 3328
SPARE = 6
K0 = 0.7978845608028654
K1 = 0.044715

NN = (1, 0)
NT = (1, 1)
TN = (0, 0)


def dot(a, b, dims=NN):
    return lax.dot_general(a, b, (((dims[0],), (dims[1],)), ((), ())), preferred_element_type=F)


def selector():
    row = lax.broadcasted_iota(jnp.int32, (EXP, D), 0)
    col = lax.broadcasted_iota(jnp.int32, (EXP, D), 1)
    r = row & 7
    return ((col == (row >> 3) * 6 + r) & (r < 6)).astype(F).astype(B)


def row_kind(shape, dim, kind):
    return (lax.broadcasted_iota(jnp.int32, shape, dim) & 7) == kind


def stats(v):
    centre = v - jnp.mean(v, axis=-1, keepdims=True)
    inv = lax.rsqrt(jnp.mean(centre * centre, axis=-1, keepdims=True) + EPS)
    return centre * inv, inv


def norm_back(g, n, inv):
    mg = jnp.mean(g, axis=-1, keepdims=True)
    mgn = jnp.mean(g * n, axis=-1, keepdims=True)
    return inv * (g - mg - n * mgn)


def head_masks():
    lane = lax.broadcasted_iota(jnp.int32, (1, 128), 1)
    low = (lane < HEAD).astype(F)
    return low.astype(B), (1.0 - low).astype(B)


def unpack(g, sel, w):
    sel[...] = selector()

    def step(i, _):
        at = pl.multiple_of(i * 256, 256)
        w["main"][:, pl.ds(at, 256)] = dot(sel[...], g[:, pl.ds(at, 256)], TN).astype(B)
        return 0

    lax.fori_loop(0, C_ADA // 256, step, 0)
    pick = row_kind((8, EXP), 1, 6).astype(F).astype(B)
    w["bias"][...] = dot(pick, g[:, :C_ADA])
    pick7 = row_kind((8, EXP), 1, 7).astype(F).astype(B)
    w["bias2"][...] = dot(pick7, g[:, C_PROJ:C_FC1])

    def step2(i, _):
        at = pl.multiple_of(i * 128, 128)
        parts = [
            g[pl.ds(at, 128), C_FC2 + a * D : C_FC2 + (a + 1) * D].astype(F).reshape(16, 8, D)
            for a in range(3)
        ]
        whole = jnp.concatenate(parts, axis=1).reshape(D, D).astype(B)
        w["fc2"][pl.ds(pl.multiple_of(i * D, D), D), :] = whole
        return 0

    lax.fori_loop(0, 4, step2, 0)


def modulate(cond, g, sel, mod):
    c = cond[...]
    act = (c * jax.nn.sigmoid(c)).astype(B)
    wide = dot(act, sel[...], NT)
    wide = jnp.where(row_kind((8, EXP), 1, 6), 1.0, wide).astype(B)
    mod[...] = dot(wide, g[:, C_ADA:C_FC2])


def forward(x, w, mod, k, y):
    main, bias, fc2 = w["main"], w["bias"], w["fc2"]

    def ln_in(i, _):
        rows = pl.ds(pl.multiple_of(i * 128, 128), 128)
        lat = pl.ds(i // 2, 1)
        n, _ = stats(x[rows, :].astype(F))
        k["ain"][rows, :] = (n * (1.0 + mod[lat, D : 2 * D]) + mod[lat, :D]).astype(B)
        return 0

    lax.fori_loop(0, 4, ln_in, 0)

    for c in range(3):
        cs = slice(c * D, (c + 1) * D)
        k["qkv"][:, cs] = (dot(k["ain"][...], main[:, cs]) + bias[0:1, cs]).astype(B)

    low, high = head_masks()

    def attend(i, _):
        rows = pl.ds(pl.multiple_of((i // 3) * SEQ, SEQ), SEQ)
        at = (i % 3) * 128
        q = k["qkv"][rows, pl.ds(pl.multiple_of(at, 128), 128)]
        key = k["qkv"][rows, pl.ds(pl.multiple_of(D + at, 128), 128)]
        v = k["qkv"][rows, pl.ds(pl.multiple_of(2 * D + at, 128), 128)]
        total = None
        for h, m in enumerate((low, high)):
            s = dot(key, q * m, NT) * 0.125
            top = jnp.max(s, axis=0, keepdims=True)
            e = jnp.exp(s - top)
            t = jnp.sum(e, axis=0, keepdims=True)
            p = (e * (1.0 / t)).astype(B)
            k["lse"][i, h : h + 1, :] = top + jnp.log(t)
            part = dot(p, v * m, TN)
            total = part if total is None else total + part
        k["att"][rows, pl.ds(pl.multiple_of(at, 128), 128)] = total.astype(B)
        return 0

    lax.fori_loop(0, 6, attend, 0)

    def mid(i, _):
        rows = pl.ds(pl.multiple_of(i * 128, 128), 128)
        lat = pl.ds(i // 2, 1)
        o = dot(k["att"][rows, :], main[:, C_PROJ:C_FC1]) + bias[0:1, C_PROJ:C_FC1]
        x1 = x[rows, :].astype(F) + mod[lat, 2 * D : 3 * D] * o
        k["o"][rows, :] = o
        k["x1"][rows, :] = x1
        n, _ = stats(x1)
        k["min"][rows, :] = (n * (1.0 + mod[lat, 4 * D : 5 * D]) + mod[lat, 3 * D : 4 * D]).astype(B)
        return 0

    lax.fori_loop(0, 4, mid, 0)

    def mlp(i, _):
        at = pl.multiple_of(i * 256, 256)
        cs = pl.ds(at, 256)
        ws = pl.ds(pl.multiple_of(C_FC1 + at, 256), 256)
        z = dot(k["min"][...], main[:, ws]) + bias[0:1, ws]
        zz = z * z
        t = jnp.tanh(z * (K0 + K0 * K1 * zz))
        half = 0.5 + 0.5 * t
        k["act"][:, cs] = (z * half).astype(B)
        k["slope"][:, cs] = half + (0.5 * z) * (1.0 - t * t) * (K0 + 3.0 * K0 * K1 * zz)
        return 0

    lax.fori_loop(0, 6, mlp, 0)

    def out(i, _):
        rows = pl.ds(pl.multiple_of(i * 128, 128), 128)
        lat = pl.ds(i // 2, 1)
        f = dot(k["act"][rows, :], fc2[...]) + w["bias2"][0:1, :]
        k["f"][rows, :] = f
        y[rows, :] = (k["x1"][rows, :] + mod[lat, 5 * D : 6 * D] * f).astype(B)
        return 0

    lax.fori_loop(0, 4, out, 0)


def token_sum(v):
    return jnp.sum(v, axis=0, keepdims=True)


def spread(sel, v, ones):
    wide = dot(sel[...], v, NT)
    return jnp.where(row_kind((EXP, 1), 0, 6), 1.0, wide).astype(B) if ones else wide.astype(B)


def backward(grad, x, cond, g, sel, w, mod, k, t, dx, dc, put):
    main, fc2 = w["main"], w["fc2"]
    dmod = t["dmod"]
    dmod[...] = jnp.zeros_like(dmod)

    def add_mod(lat, piece, v):
        cs = slice(piece * D, (piece + 1) * D)
        dmod[lat, cs] = dmod[lat, cs] + v

    t["db2"][...] = jnp.zeros_like(t["db2"])

    def start(i, _):
        rows = pl.ds(pl.multiple_of(i * 128, 128), 128)
        lat = pl.ds(i // 2, 1)
        gr = grad[rows, :].astype(F)
        df = (gr * mod[lat, 5 * D : 6 * D]).astype(B)
        t["df"][rows, :] = df
        add_mod(lat, 5, token_sum(gr * k["f"][rows, :]))
        t["db2"][0:1, :] = t["db2"][0:1, :] + token_sum(df.astype(F))
        return 0

    lax.fori_loop(0, 4, start, 0)

    def dmlp(i, _):
        cs = pl.ds(pl.multiple_of(i * 256, 256), 256)
        da = dot(t["df"][...], fc2[cs, :], NT)
        t["dz"][:, cs] = (da * k["slope"][:, cs]).astype(B)
        return 0

    lax.fori_loop(0, 6, dmlp, 0)

    t["wide"][...] = spread(sel, k["min"][...], True)

    def dw1(i, _):
        at = pl.multiple_of(i * 256, 256)
        put(0, pl.ds(0, EXP), pl.ds(pl.multiple_of(C_FC1 + at, 256), 256), dot(t["wide"][...], t["dz"][:, pl.ds(at, 256)]).astype(B))
        return 0

    lax.fori_loop(0, 6, dw1, 0)

    for c in range(4):
        part = dot(k["act"][:, c * D : (c + 1) * D], t["df"][...], TN).reshape(16, 24, D)
        for a in range(3):
            put(
                1,
                slice(c * 128, (c + 1) * 128),
                slice(C_FC2 - HALF + a * D, C_FC2 - HALF + (a + 1) * D),
                part[:, 8 * a : 8 * a + 8, :].reshape(128, D).astype(B),
            )

    def dmid(i, _):
        rows = pl.ds(pl.multiple_of(i * 128, 128), 128)
        lat = pl.ds(i // 2, 1)
        dmin = dot(t["dz"][rows, :], main[:, C_FC1:C_ADA], NT)
        n, inv = stats(k["x1"][rows, :])
        add_mod(lat, 4, token_sum(dmin * n))
        add_mod(lat, 3, token_sum(dmin))
        d1 = grad[rows, :].astype(F) + norm_back(dmin * (1.0 + mod[lat, 4 * D : 5 * D]), n, inv)
        t["dx1"][rows, :] = d1
        do = (d1 * mod[lat, 2 * D : 3 * D]).astype(B)
        add_mod(lat, 2, token_sum(d1 * k["o"][rows, :]))
        t["df"][rows, :] = do
        t["datt"][rows, :] = dot(do, main[:, C_PROJ:C_FC1], NT).astype(B)
        return 0

    lax.fori_loop(0, 4, dmid, 0)

    t["wide"][...] = spread(sel, k["att"][...], True)
    dp = dot(t["wide"][...], t["df"][...])
    dp = jnp.where(row_kind((EXP, 1), 0, 7), t["db2"][0:1, :], dp)
    put(0, slice(0, EXP), slice(C_PROJ, C_FC1), dp.astype(B))

    low, high = head_masks()

    def dattend(i, _):
        rows = pl.ds(pl.multiple_of((i // 3) * SEQ, SEQ), SEQ)
        at = (i % 3) * 128
        qs = pl.ds(pl.multiple_of(at, 128), 128)
        ks = pl.ds(pl.multiple_of(D + at, 128), 128)
        vs = pl.ds(pl.multiple_of(2 * D + at, 128), 128)
        q = k["qkv"][rows, qs]
        key = k["qkv"][rows, ks]
        v = k["qkv"][rows, vs]
        da = t["datt"][rows, qs]
        dq = dk = dv = None
        for h, m in enumerate((low, high)):
            qm = q * m
            dam = da * m
            s = dot(key, qm, NT) * 0.125
            p = jnp.exp(s - k["lse"][i, h : h + 1, :])
            dp = dot(v, dam, NT)
            ds = (p * (dp - jnp.sum(p * dp, axis=0, keepdims=True))).astype(B)
            v1 = dot(p.astype(B), dam)
            k1 = dot(ds, qm)
            q1 = dot(ds, key * m, TN)
            dv = v1 if dv is None else dv + v1
            dk = k1 if dk is None else dk + k1
            dq = q1 if dq is None else dq + q1
        t["dqkv"][rows, qs] = (dq * 0.125).astype(B)
        t["dqkv"][rows, ks] = (dk * 0.125).astype(B)
        t["dqkv"][rows, vs] = dv.astype(B)
        return 0

    lax.fori_loop(0, 6, dattend, 0)

    t["wide"][...] = spread(sel, k["ain"][...], True)

    def dwq(i, _):
        cs = pl.ds(pl.multiple_of(i * 384, 128), 384)
        put(0, pl.ds(0, EXP), cs, dot(t["wide"][...], t["dqkv"][:, cs]).astype(B))
        return 0

    lax.fori_loop(0, 3, dwq, 0)

    def dlast(i, _):
        rows = pl.ds(pl.multiple_of(i * 128, 128), 128)
        lat = pl.ds(i // 2, 1)
        dain = dot(t["dqkv"][rows, :], main[:, C_QKV:C_PROJ], NT)
        n, inv = stats(x[rows, :].astype(F))
        add_mod(lat, 1, token_sum(dain * n))
        add_mod(lat, 0, token_sum(dain))
        back = norm_back(dain * (1.0 + mod[lat, D : 2 * D]), n, inv)
        dx[rows, :] = (t["dx1"][rows, :] + back).astype(B)
        return 0

    lax.fori_loop(0, 4, dlast, 0)

    dm = dmod[...].astype(B)
    c = cond[...]
    sig = jax.nn.sigmoid(c)
    act = (c * sig).astype(B)
    live = lax.broadcasted_iota(jnp.int32, (8, 1), 0) < 2
    dm = jnp.where(live, dm.astype(F), 0.0)
    wide = dot(sel[...], act, NT)
    wide = jnp.where(row_kind((EXP, 1), 0, 6), 1.0, wide).astype(B)
    for i in range(9):
        at = i * 256
        to = C_ADA + at if i == 0 else C_ADA + at - HALF
        put(int(i > 0), slice(0, EXP), slice(to, to + 256), dot(wide, dm[:, at : at + 256].astype(B)).astype(B))
    put(1, slice(0, EXP), slice(C_END - HALF, HALF), jnp.zeros((EXP, 2 * HALF - C_END), B))
    dwide = dot(dm.astype(B), g[:, C_ADA:C_FC2], NT)
    dact = lax.dot_general(
        dwide, sel[...].astype(F), (((1,), (0,)), ((), ())), precision=lax.Precision.HIGHEST, preferred_element_type=F
    )
    dc[...] = dact * (sig * (1.0 + c * (1.0 - sig)))


KEEP = (
    ("ain", (ROWS, D), B),
    ("qkv", (ROWS, 3 * D), B),
    ("lse", (6, 8, SEQ), F),
    ("att", (ROWS, D), B),
    ("o", (ROWS, D), F),
    ("x1", (ROWS, D), F),
    ("min", (ROWS, D), B),
    ("slope", (ROWS, FF), F),
    ("act", (ROWS, FF), B),
    ("f", (ROWS, D), F),
)
WEIGHTS = (("main", (D, C_ADA), B), ("bias", (8, C_ADA), F), ("bias2", (8, D), F), ("fc2", (FF, D), B))
TEMPS = (
    ("dmod", (8, 6 * D), F),
    ("db2", (8, D), F),
    ("df", (ROWS, D), B),
    ("dz", (ROWS, FF), B),
    ("wide", (EXP, ROWS), B),
    ("dx1", (ROWS, D), F),
    ("datt", (ROWS, D), B),
    ("dqkv", (ROWS, 3 * D), B),
)
SEL = (("sel", (EXP, D), B),)
MOD = (("mod", (8, 6 * D), F),)


def buffers(table):
    return [pltpu.VMEM(shape, dtype) for _, shape, dtype in table]


def shapes(table):
    return [jax.ShapeDtypeStruct(shape, dtype) for _, shape, dtype in table]


def named(table, refs):
    return {name: ref for (name, _, _), ref in zip(table, refs)}


def fetch(core, own, other, g, sems, ada_only=False):
    def go(low, high):
        if ada_only:
            copies = [
                pltpu.make_async_copy(low.at[:, C_ADA:HALF], g.at[:, C_ADA:HALF], sems.at[0]),
                pltpu.make_async_copy(high.at[:, : C_FC2 - HALF], g.at[:, HALF:C_FC2], sems.at[1]),
            ]
        else:
            copies = [
                pltpu.make_async_copy(low, g.at[:, :HALF], sems.at[0]),
                pltpu.make_async_copy(high.at[:, : C_END - HALF], g.at[:, HALF:], sems.at[1]),
            ]
        for copy in copies:
            copy.start()
        for copy in copies:
            copy.wait()

    @pl.when(core == 0)
    def _():
        go(own, other)

    @pl.when(core != 0)
    def _():
        go(other, own)


def pack_out(pack, keep, send, sems):
    copies = [pltpu.make_async_copy(pack.at[i], ref, sems.at[i]) for i, ref in enumerate((keep, send))]
    for copy in copies:
        copy.start()
    for copy in copies:
        copy.wait()


def putter(core, pack):
    def put(half, rows, cols, value):
        slot = core if half == 0 else 1 - core
        pack[slot, rows, cols] = value

    return put


def front_kernel(core, own, other, x, cond, *refs):
    n_keep, n_w = len(KEEP), len(WEIGHTS)
    y = refs[0]
    k = named(KEEP, refs[1 : 1 + n_keep])
    w = named(WEIGHTS, refs[1 + n_keep : 1 + n_keep + n_w])
    mod, g, sel, sems = refs[1 + n_keep + n_w :]
    fetch(core[0], own, other, g, sems)
    unpack(g, sel, w)
    modulate(cond, g, sel, mod)
    forward(x, w, mod, k, y)


def turn_kernel(core, own, other, x, cond, grad, y, dx, dc, keep, send, *refs):
    n_keep, n_w, n_t = len(KEEP), len(WEIGHTS), len(TEMPS)
    k = named(KEEP, refs[:n_keep])
    w = named(WEIGHTS, refs[n_keep : n_keep + n_w])
    t = named(TEMPS, refs[n_keep + n_w : n_keep + n_w + n_t])
    mod, g, sel, pack, sems = refs[n_keep + n_w + n_t :]
    fetch(core[0], own, other, g, sems)
    unpack(g, sel, w)
    modulate(cond, g, sel, mod)
    forward(x, w, mod, k, y)
    backward(grad, x, cond, g, sel, w, mod, k, t, dx, dc, putter(core[0], pack))
    pack_out(pack, keep, send, sems)


def back_kernel(core, own, other, x, cond, grad, *refs):
    n_keep, n_w, n_t = len(KEEP), len(WEIGHTS), len(TEMPS)
    k = named(KEEP, refs[:n_keep])
    w = named(WEIGHTS, refs[n_keep : n_keep + n_w])
    mod, dx, dc, keep, send = refs[n_keep + n_w : n_keep + n_w + 5]
    refs = refs[n_keep + n_w + 5 :]
    t = named(TEMPS, refs[:n_t])
    g, sel, pack, sems = refs[n_t:]
    sel[...] = selector()
    fetch(core[0], own, other, g, sems, ada_only=True)
    backward(grad, x, cond, g, sel, w, mod, k, t, dx, dc, putter(core[0], pack))
    pack_out(pack, keep, send, sems)


VM = pl.BlockSpec(memory_space=pltpu.VMEM)
ANY = pl.BlockSpec(memory_space=pl.ANY)
SM = pl.BlockSpec(memory_space=pltpu.SMEM)
PARAMS = pltpu.CompilerParams(vmem_limit_bytes=60 * 1024 * 1024)
G_BUF = pltpu.VMEM((EXP, C_END), B)
SEL_BUF = pltpu.VMEM((EXP, D), B)
SEMS = pltpu.SemaphoreType.DMA((2,))
ROWS_OUT = jax.ShapeDtypeStruct((ROWS, D), B)
COND_OUT = jax.ShapeDtypeStruct((8, D), F)
HALF_OUT = jax.ShapeDtypeStruct((EXP, HALF), B)
PACK_BUF = pltpu.VMEM((2, EXP, HALF), B)


def cost(units):
    return pl.CostEstimate(flops=units * 2_000_000_000, bytes_accessed=units * 10_000_000, transcendentals=units * 2_000_000)


def front(core, own, other, x, cond):
    outs = [ROWS_OUT] + shapes(KEEP) + shapes(WEIGHTS) + shapes(MOD)
    return pl.pallas_call(
        front_kernel,
        out_shape=outs,
        in_specs=[SM, ANY, ANY, VM, VM],
        out_specs=[VM] * len(outs),
        scratch_shapes=[G_BUF, SEL_BUF, SEMS],
        compiler_params=PARAMS,
        cost_estimate=cost(1),
        name="front",
    )(core, own, other, x, cond)


def turn(core, own, other, x, cond, grad):
    return pl.pallas_call(
        turn_kernel,
        out_shape=[ROWS_OUT, ROWS_OUT, COND_OUT, HALF_OUT, HALF_OUT],
        in_specs=[SM, ANY, ANY, VM, VM, VM],
        out_specs=[VM] * 3 + [ANY] * 2,
        scratch_shapes=buffers(KEEP) + buffers(WEIGHTS) + buffers(TEMPS) + buffers(MOD) + [G_BUF, SEL_BUF, PACK_BUF, SEMS],
        compiler_params=PARAMS,
        cost_estimate=cost(3),
        name="turn",
    )(core, own, other, x, cond, grad)


def back(core, own, other, x, cond, grad, kept):
    return pl.pallas_call(
        back_kernel,
        out_shape=[ROWS_OUT, COND_OUT, HALF_OUT, HALF_OUT],
        in_specs=[SM, ANY, ANY, VM, VM, VM] + [VM] * len(kept),
        out_specs=[VM] * 2 + [ANY] * 2,
        scratch_shapes=buffers(TEMPS) + [G_BUF, SEL_BUF, PACK_BUF, SEMS],
        compiler_params=PARAMS,
        cost_estimate=cost(2),
        name="back",
    )(core, own, other, x, cond, grad, *kept)


def line_up(j, w_qkv, b_qv, w_proj, b_proj, w_fc1, b_fc1, w_fc2, b_fc2, w_ada, b_ada):
    main = jnp.concatenate([w_qkv, w_proj, w_fc1, w_ada], axis=1)
    line = jnp.zeros((C_FC2,), B)
    at_qv = jnp.where(j < 32, 12 * j, 12 * j + D)
    line = lax.dynamic_update_slice(line, b_qv, (at_qv,))
    line = lax.dynamic_update_slice(line, b_proj, (C_PROJ + 6 * j,))
    line = lax.dynamic_update_slice(line, b_fc1, (C_FC1 + 24 * j,))
    line = lax.dynamic_update_slice(line, b_ada, (C_ADA + 36 * j,))
    spare = lax.dynamic_update_slice(jnp.zeros((C_FC2,), B), b_fc2, (C_PROJ + 6 * j,))
    top = jnp.concatenate([main, line[None], spare[None]], axis=0)
    return jnp.concatenate([top, w_fc2[:8], w_fc2[8:16], w_fc2[16:], jnp.zeros((8, 2 * HALF - C_END), B)], axis=1)


def swap(x):
    return lax.ppermute(x, "pipe", [(0, 1), (1, 0)])


def to_all(block):
    copies = jnp.broadcast_to(block[None], (CHIPS, *block.shape))
    return lax.all_to_all(copies, "shard", 0, 0, tiled=True).reshape(EXP, block.shape[1])


def scatter(block):
    return lax.all_to_all(block.reshape(CHIPS, 8, HALF), "shard", 0, 0, tiled=True)


def shards(latents, conditions, cotangent, w_qkv, b_qv, w_proj, b_proj, w_fc1, b_fc1, w_fc2, b_fc2, w_ada, b_ada):
    p = lax.axis_index("pipe")
    j = lax.axis_index("shard")
    first = p == 0
    core = p.reshape(1).astype(jnp.int32)
    block = line_up(j, w_qkv[0], b_qv[0], w_proj[0], b_proj[0], w_fc1[0], b_fc1[0], w_fc2[0], b_fc2[0], w_ada[0], b_ada[0])
    low, high = block[:, :HALF], block[:, HALF:]
    mine = jnp.where(first, low, high)
    came = swap(jnp.where(first, high, low))
    own0 = to_all(jnp.where(first, mine, came))
    own1 = lax.all_gather(jnp.where(first, came, mine), "shard", tiled=True)
    other0 = swap(own0)
    x = lax.dynamic_index_in_dim(latents, p, 0, keepdims=False).reshape(ROWS, D)
    cot = lax.dynamic_index_in_dim(cotangent, p, 0, keepdims=False).reshape(ROWS, D)
    cond = lax.dynamic_index_in_dim(conditions, p, 0, keepdims=False).astype(F)
    cond = jnp.concatenate([cond, jnp.zeros((6, D), F)], axis=0)

    h, *kept = front(core, own0, other0, x, cond)
    h, own1 = lax.optimization_barrier((h, own1))
    other1 = swap(own1)
    y, dx1, dc1, keep1, send1 = turn(core, own1, other1, h, cond, cot)
    parts1 = scatter(keep1 + swap(send1))
    dx0, dc0, keep0, send0 = back(core, own0, other0, x, cond, dx1, kept)
    parts1, send0 = lax.optimization_barrier((parts1, send0))
    parts0 = scatter(keep0 + swap(send0))

    def pair(for_first, for_second):
        keep = jnp.where(first, for_first, for_second)
        came = swap(jnp.where(first, for_second, for_first))
        both = jnp.where(first, jnp.stack([keep, came]), jnp.stack([came, keep]))
        return both.reshape(1, 2, 2, SEQ, D)

    section_outputs = pair(h, y)
    input_grads = pair(dx0, dx1)
    dc = (dc0 + dc1)[:2]
    dc_other = swap(dc)
    cond_grad = jnp.where(first, jnp.stack([dc, dc_other]), jnp.stack([dc_other, dc]))

    sum0 = jnp.sum(parts0.astype(F), axis=0)
    sum1 = jnp.sum(parts1.astype(F), axis=0)
    kept_half = jnp.where(first, sum0, sum1)
    came_half = swap(jnp.where(first, sum1, sum0))
    done = jnp.concatenate([jnp.where(first, kept_half, came_half), jnp.where(first, came_half, kept_half)], axis=1)[:, :C_END]

    rows = done[:6]
    at_qv = jnp.where(j < 32, 12 * j, 12 * j + D)
    line = done[6]
    outs = (
        rows[:, C_QKV:C_PROJ],
        lax.dynamic_slice(line, (at_qv,), (12,)),
        rows[:, C_PROJ:C_FC1],
        lax.dynamic_slice(line, (C_PROJ + 6 * j,), (6,)),
        rows[:, C_FC1:C_ADA],
        lax.dynamic_slice(line, (C_FC1 + 24 * j,), (24,)),
        done[:, C_FC2:].reshape(8, 3, D).transpose(1, 0, 2).reshape(24, D),
        lax.dynamic_slice(done[7], (C_PROJ + 6 * j,), (6,)),
        rows[:, C_ADA:C_FC2],
        lax.dynamic_slice(line, (C_ADA + 36 * j,), (36,)),
    )
    return (section_outputs, input_grads, cond_grad) + tuple(o[None] for o in outs)


def solution(mesh):
    rows = P(None, "shard", None, None)
    wide = P("pipe", "shard", None)
    thin = P("pipe", "shard")
    both = P("pipe", None, "shard", None, None)
    pairs = (wide, thin) * 5
    return jax.shard_map(
        shards,
        mesh=mesh,
        in_specs=(rows, P(None, "shard", None), rows) + pairs,
        out_specs=(both, both, P(None, "shard", None)) + pairs,
        check_vma=False,
    )
```

```python
import functools

import jax
import jax.numpy as jnp
from jax import lax
from jax.experimental import pallas as pl
from jax.experimental.pallas import tpu as pltpu
from jax.sharding import PartitionSpec as P

F = jnp.float32
B = jnp.bfloat16
D = 384
HEADS = 6
HEAD = 64
FF = 1536
SEQ = 256
EPS = 1e-06
CHIPS = 64
ROWS = 512
EXP = 512

C_QKV, C_PROJ, C_FC1, C_MAIN = 0, 1152, 1536, 3072
QUARTER = 768

G_FC2, G_ADA, G_BIAS, G_END = 2304, 3456, 5248, 5376
G_HALF = 2688
BIASES = ((0, 12), (12, 6), (18, 24), (42, 6), (48, 36))

P_HALF = 2560
P_DB0 = 2304
P_MOD, P_DB1, P_COND = 1152, 2304, 2432
SHIFTS = (0, 6, 4, 2)

K0 = 0.7978845608028654
K1 = 0.044715

NN = (1, 0)
NT = (1, 1)
TN = (0, 0)


def dot(a, b, dims=NN):
    return lax.dot_general(a, b, (((dims[0],), (dims[1],)), ((), ())), preferred_element_type=F)


def targets(shape, dim, shift):
    at = lax.broadcasted_iota(jnp.int32, shape, dim)
    r = ((at & 7) + (8 - shift)) & 7
    return jnp.where(r < 6, (at >> 3) * 6 + r, -1)


def build_selectors(sel, selt):
    col = lax.broadcasted_iota(jnp.int32, (1, D), 1)
    row = lax.broadcasted_iota(jnp.int32, (D, 1), 0)
    for i, shift in enumerate(SHIFTS):
        sel[i] = (targets((EXP, 1), 0, shift) == col).astype(F).astype(B)
        selt[i] = (row == targets((1, EXP), 1, shift)).astype(F).astype(B)


def group_of(n, width):
    return jnp.floor((n.astype(F) + 0.5) * (1.0 / width)).astype(jnp.int32)


def natural_bias(gb, lane, width):
    n = CHIPS * width
    at = lax.broadcasted_iota(jnp.int32, (1, n), 1)
    owner = group_of(at, width)
    spot = at - owner * width + lane
    pick = (lax.broadcasted_iota(jnp.int32, (128, 1), 0) == spot).astype(F).astype(B)
    wide = dot(gb, pick)
    return jnp.sum(jnp.where(lax.broadcasted_iota(jnp.int32, (CHIPS, 1), 0) == owner, wide, 0.0), axis=0, keepdims=True)


def tile_row(shape, dim):
    return lax.broadcasted_iota(jnp.int32, shape, dim) & 7


def stats(v):
    centre = v - jnp.mean(v, axis=-1, keepdims=True)
    inv = lax.rsqrt(jnp.mean(centre * centre, axis=-1, keepdims=True) + EPS)
    return centre * inv, inv


def norm_back(g, n, inv):
    mg = jnp.mean(g, axis=-1, keepdims=True)
    mgn = jnp.mean(g * n, axis=-1, keepdims=True)
    return inv * (g - mg - n * mgn)


def head_masks():
    lane = lax.broadcasted_iota(jnp.int32, (1, 128), 1)
    low = (lane < HEAD).astype(F)
    return low.astype(B), (1.0 - low).astype(B)


def unpack(g, selt, w):
    r8 = tile_row((EXP, 1), 0)

    def piece(a, c):
        return g[:, a * QUARTER + c : a * QUARTER + c + 384]

    def merge(edge, a, c):
        return jnp.where(r8 >= edge, piece(a, c).astype(F), piece(a + 1, c).astype(F)).astype(B)

    for c in (0, 384):
        w["main"][:, c : c + 384] = dot(selt[0], piece(0, c)).astype(B)
        w["main"][:, QUARTER + c : QUARTER + c + 384] = dot(selt[1], merge(6, 0, c)).astype(B)
        w["main"][:, 2 * QUARTER + c : 2 * QUARTER + c + 384] = dot(selt[2], merge(4, 1, c)).astype(B)
        w["main"][:, 3 * QUARTER + c : 3 * QUARTER + c + 384] = dot(selt[3], piece(2, c)).astype(B)

    lead = (lax.broadcasted_iota(jnp.int32, (CHIPS, EXP), 0) * 8 == lax.broadcasted_iota(jnp.int32, (CHIPS, EXP), 1)).astype(F).astype(B)
    gb = dot(lead, g[:, G_BIAS:G_END]).astype(B)
    qv, proj, fc1, fc2, ada = (natural_bias(gb, lane, width) for lane, width in BIASES)
    w["bias"][:, :D] = qv[:, :D]
    w["bias"][:, D : 2 * D] = jnp.zeros((1, D), F)
    w["bias"][:, 2 * D : C_PROJ] = qv[:, D:]
    w["bias"][:, C_PROJ:C_FC1] = proj
    w["bias"][:, C_FC1:C_MAIN] = fc1
    w["bias2"][...] = fc2

    def step2(i, _):
        at = pl.multiple_of(i * 128, 128)
        parts = [g[pl.ds(at, 128), G_FC2 + a * D : G_FC2 + (a + 1) * D].astype(F).reshape(16, 8, D) for a in range(3)]
        whole = jnp.concatenate(parts, axis=1).reshape(D, D).astype(B)
        w["fc2"][pl.ds(pl.multiple_of(i * D, D), D), :] = whole
        return 0

    lax.fori_loop(0, 4, step2, 0)
    return ada


def ada_groups():
    return [(i % 4, (6 * i) // 8, SHIFTS[i % 4] in (6, 4)) for i in range(9)]


def modulate(cond, g, selt, ada, mod):
    c = cond[...]
    act = (c * jax.nn.sigmoid(c)).astype(B)
    r8 = tile_row((1, EXP), 1)
    wides = [dot(act, selt[i]) for i in range(4)]
    for n, (i, a, more) in enumerate(ada_groups()):
        at = G_ADA + a * 256
        first = jnp.where(r8 >= SHIFTS[i], wides[i], 0.0).astype(B)
        part = dot(first, g[:, at : at + 256])
        if more:
            part = part + dot(jnp.where(r8 < SHIFTS[i], wides[i], 0.0).astype(B), g[:, at + 256 : at + 512])
        mod[:, n * 256 : (n + 1) * 256] = part + ada[:, n * 256 : (n + 1) * 256]


def cond_back(dm, g, g_at, selt):
    r8 = tile_row((1, EXP), 1)
    sums = [jnp.zeros((8, EXP), F)] * 4
    for n, (i, a, more) in enumerate(ada_groups()):
        at = g_at + a * 256
        piece = dm[:, n * 256 : (n + 1) * 256]
        sums[i] = sums[i] + jnp.where(r8 >= SHIFTS[i], dot(piece, g[:, at : at + 256], NT), 0.0)
        if more:
            sums[i] = sums[i] + jnp.where(r8 < SHIFTS[i], dot(piece, g[:, at + 256 : at + 512], NT), 0.0)
    total = jnp.zeros((8, D), F)
    for i in range(4):
        rest = sums[i]
        for _ in range(3):
            level = rest.astype(B)
            rest = rest - level.astype(F)
            total = total + dot(level, selt[i], NT)
    return total


def forward(x, w, mod, k, y):
    main, bias, fc2 = w["main"], w["bias"], w["fc2"]

    def ln_in(i, _):
        rows = pl.ds(pl.multiple_of(i * 128, 128), 128)
        lat = pl.ds(i // 2, 1)
        n, _ = stats(x[rows, :].astype(F))
        k["ain"][rows, :] = (n * (1.0 + mod[lat, D : 2 * D]) + mod[lat, :D]).astype(B)
        return 0

    lax.fori_loop(0, 4, ln_in, 0)

    for c in range(3):
        cs = slice(c * D, (c + 1) * D)
        k["qkv"][:, cs] = (dot(k["ain"][...], main[:, cs]) + bias[:, cs]).astype(B)

    low, high = head_masks()

    def attend(i, _):
        rows = pl.ds(pl.multiple_of((i // 3) * SEQ, SEQ), SEQ)
        at = (i % 3) * 128
        q = k["qkv"][rows, pl.ds(pl.multiple_of(at, 128), 128)]
        key = k["qkv"][rows, pl.ds(pl.multiple_of(D + at, 128), 128)]
        v = k["qkv"][rows, pl.ds(pl.multiple_of(2 * D + at, 128), 128)]
        total = None
        for h, m in enumerate((low, high)):
            s = dot(key, q * m, NT) * 0.125
            top = jnp.max(s, axis=0, keepdims=True)
            e = jnp.exp(s - top)
            t = jnp.sum(e, axis=0, keepdims=True)
            p = (e * (1.0 / t)).astype(B)
            k["lse"][i, h : h + 1, :] = top + jnp.log(t)
            part = dot(p, v * m, TN)
            total = part if total is None else total + part
        k["att"][rows, pl.ds(pl.multiple_of(at, 128), 128)] = total.astype(B)
        return 0

    lax.fori_loop(0, 6, attend, 0)

    def mid(i, _):
        rows = pl.ds(pl.multiple_of(i * 128, 128), 128)
        lat = pl.ds(i // 2, 1)
        o = dot(k["att"][rows, :], main[:, C_PROJ:C_FC1]) + bias[:, C_PROJ:C_FC1]
        x1 = x[rows, :].astype(F) + mod[lat, 2 * D : 3 * D] * o
        k["o"][rows, :] = o
        k["x1"][rows, :] = x1
        n, _ = stats(x1)
        k["min"][rows, :] = (n * (1.0 + mod[lat, 4 * D : 5 * D]) + mod[lat, 3 * D : 4 * D]).astype(B)
        return 0

    lax.fori_loop(0, 4, mid, 0)

    def mlp(i, _):
        at = pl.multiple_of(i * 256, 256)
        cs = pl.ds(at, 256)
        ws = pl.ds(pl.multiple_of(C_FC1 + at, 256), 256)
        z = dot(k["min"][...], main[:, ws]) + bias[:, ws]
        zz = z * z
        t = jnp.tanh(z * (K0 + K0 * K1 * zz))
        half = 0.5 + 0.5 * t
        k["act"][:, cs] = (z * half).astype(B)
        k["slope"][:, cs] = half + (0.5 * z) * (1.0 - t * t) * (K0 + 3.0 * K0 * K1 * zz)
        return 0

    lax.fori_loop(0, 6, mlp, 0)

    def out(i, _):
        rows = pl.ds(pl.multiple_of(i * 128, 128), 128)
        lat = pl.ds(i // 2, 1)
        f = dot(k["act"][rows, :], fc2[...]) + w["bias2"][...]
        k["f"][rows, :] = f
        y[rows, :] = (k["x1"][rows, :] + mod[lat, 5 * D : 6 * D] * f).astype(B)
        return 0

    lax.fori_loop(0, 4, out, 0)


def token_sum(v):
    return jnp.sum(v, axis=0, keepdims=True)


def spread(sel, i, v):
    return dot(sel[i], v, NT).astype(B)


def backward(core, grad, x, cond, g, g_at, sel, selt, w, mod, k, t, dx, dc, put):
    main, fc2 = w["main"], w["fc2"]
    dmod = t["dmod"]
    dmod[...] = jnp.zeros_like(dmod)

    def add_mod(lat, piece, v):
        cs = slice(piece * D, (piece + 1) * D)
        dmod[lat, cs] = dmod[lat, cs] + v

    t["db"][...] = jnp.zeros_like(t["db"])
    r8 = tile_row((EXP, 1), 0)

    def add_db(at, v):
        t["db"][:, at : at + v.shape[1]] = t["db"][:, at : at + v.shape[1]] + v


    def start(i, _):
        rows = pl.ds(pl.multiple_of(i * 128, 128), 128)
        lat = pl.ds(i // 2, 1)
        gr = grad[rows, :].astype(F)
        df = (gr * mod[lat, 5 * D : 6 * D]).astype(B)
        t["df"][rows, :] = df
        add_mod(lat, 5, token_sum(gr * k["f"][rows, :]))
        add_db(2688, token_sum(df.astype(F)))
        return 0

    lax.fori_loop(0, 4, start, 0)

    def dmlp(i, _):
        cs = pl.ds(pl.multiple_of(i * 256, 256), 256)
        da = dot(t["df"][...], fc2[cs, :], NT)
        dz = (da * k["slope"][:, cs]).astype(B)
        t["dz"][:, cs] = dz
        ds = pl.ds(pl.multiple_of(1152 + i * 256, 128), 256)
        t["db"][:, ds] = token_sum(dz.astype(F))
        return 0

    lax.fori_loop(0, 6, dmlp, 0)

    t["wide2"][...] = spread(sel, 2, k["min"][...])
    t["wide"][...] = spread(sel, 3, k["min"][...])
    for c in range(0, QUARTER, 256):
        d2 = dot(t["wide2"][...], t["dz"][:, c : c + 256])
        d3 = dot(t["wide"][...], t["dz"][:, QUARTER + c : QUARTER + c + 256])
        put(0, slice(0, EXP), slice(2 * QUARTER + c, 2 * QUARTER + c + 256), jnp.where(r8 < 2, d2, d3).astype(B))
        t["part"][:, c : c + 256] = d2

    for c in range(4):
        part = dot(k["act"][:, c * D : (c + 1) * D], t["df"][...], TN).reshape(16, 24, D)
        for a in range(3):
            put(
                1,
                slice(c * 128, (c + 1) * 128),
                slice(a * D, (a + 1) * D),
                part[:, 8 * a : 8 * a + 8, :].reshape(128, D).astype(B),
            )

    def dmid(i, _):
        rows = pl.ds(pl.multiple_of(i * 128, 128), 128)
        lat = pl.ds(i // 2, 1)
        dmin = dot(t["dz"][rows, :], main[:, C_FC1:C_MAIN], NT)
        n, inv = stats(k["x1"][rows, :])
        add_mod(lat, 4, token_sum(dmin * n))
        add_mod(lat, 3, token_sum(dmin))
        d1 = grad[rows, :].astype(F) + norm_back(dmin * (1.0 + mod[lat, 4 * D : 5 * D]), n, inv)
        t["dx1"][rows, :] = d1
        do = (d1 * mod[lat, 2 * D : 3 * D]).astype(B)
        add_mod(lat, 2, token_sum(d1 * k["o"][rows, :]))
        t["df"][rows, :] = do
        add_db(768, token_sum(do.astype(F)))
        t["datt"][rows, :] = dot(do, main[:, C_PROJ:C_FC1], NT).astype(B)
        return 0

    lax.fori_loop(0, 4, dmid, 0)

    t["wide2"][...] = spread(sel, 1, k["att"][...])
    d1 = dot(t["wide2"][...], t["df"][...])
    put(0, slice(0, EXP), slice(QUARTER + 384, 2 * QUARTER), jnp.where(r8 < 4, d1, t["part"][:, 384:]).astype(B))
    t["part2"][...] = d1

    low, high = head_masks()

    def dattend(i, _):
        rows = pl.ds(pl.multiple_of((i // 3) * SEQ, SEQ), SEQ)
        at = (i % 3) * 128
        qs = pl.ds(pl.multiple_of(at, 128), 128)
        ks = pl.ds(pl.multiple_of(D + at, 128), 128)
        vs = pl.ds(pl.multiple_of(2 * D + at, 128), 128)
        q = k["qkv"][rows, qs]
        key = k["qkv"][rows, ks]
        v = k["qkv"][rows, vs]
        da = t["datt"][rows, qs]
        dq = dk = dv = None
        for h, m in enumerate((low, high)):
            qm = q * m
            dam = da * m
            s = dot(key, qm, NT) * 0.125
            p = jnp.exp(s - k["lse"][i, h : h + 1, :])
            dp = dot(v, dam, NT)
            ds = (p * (dp - jnp.sum(p * dp, axis=0, keepdims=True))).astype(B)
            v1 = dot(p.astype(B), dam)
            k1 = dot(ds, qm)
            q1 = dot(ds, key * m, TN)
            dv = v1 if dv is None else dv + v1
            dk = k1 if dk is None else dk + k1
            dq = q1 if dq is None else dq + q1
        t["dqkv"][rows, qs] = (dq * 0.125).astype(B)
        t["dqkv"][rows, ks] = (dk * 0.125).astype(B)
        t["dqkv"][rows, vs] = dv.astype(B)
        return 0

    lax.fori_loop(0, 6, dattend, 0)

    t["wide"][...] = spread(sel, 0, k["ain"][...])
    t["wide2"][...] = spread(sel, 1, k["ain"][...])
    d1 = dot(t["wide2"][...], t["dqkv"][:, QUARTER:])
    d0 = dot(t["wide"][...], t["dqkv"][:, :384])
    put(0, slice(0, EXP), slice(0, 384), jnp.where(r8 < 6, d0, d1).astype(B))
    put(0, slice(0, EXP), slice(QUARTER, QUARTER + 384), jnp.where(r8 < 4, d1, t["part"][:, :384]).astype(B))
    d0 = dot(t["wide"][...], t["dqkv"][:, 384:QUARTER])
    put(0, slice(0, EXP), slice(384, QUARTER), jnp.where(r8 < 6, d0, t["part2"][...]).astype(B))

    def bias_sums(i, _):
        rows = pl.ds(pl.multiple_of(i * 128, 128), 128)
        add_db(0, token_sum(t["dqkv"][rows, :D].astype(F)))
        add_db(D, token_sum(t["dqkv"][rows, 2 * D :].astype(F)))
        return 0

    lax.fori_loop(0, 4, bias_sums, 0)

    def dlast(i, _):
        rows = pl.ds(pl.multiple_of(i * 128, 128), 128)
        lat = pl.ds(i // 2, 1)
        dain = dot(t["dqkv"][rows, :], main[:, C_QKV:C_PROJ], NT)
        n, inv = stats(x[rows, :].astype(F))
        add_mod(lat, 1, token_sum(dain * n))
        add_mod(lat, 0, token_sum(dain))
        back = norm_back(dain * (1.0 + mod[lat, D : 2 * D]), n, inv)
        dx[rows, :] = (t["dx1"][rows, :] + back).astype(B)
        return 0

    lax.fori_loop(0, 4, dlast, 0)

    c = cond[...]
    sig = jax.nn.sigmoid(c)
    act = c * sig
    dm = dmod[...].astype(B).astype(F)
    dc[...] = cond_back(dm.astype(B), g, g_at, selt) * (sig * (1.0 + c * (1.0 - sig)))

    mine = 2 * core
    block = pltpu.roll(dm[:, :1152], mine, 0) + pltpu.roll(dm[:, 1152:], mine + 4, 0)
    for q in range(4):
        rows = slice(q * 128, (q + 1) * 128)
        put(1, rows, slice(P_MOD, P_DB1), jnp.broadcast_to(block[None], (16, 8, 1152)).reshape(128, 1152).astype(B))

    db = t["db"]
    for half, at, first in ((0, P_DB0, 0), (0, P_DB0 + 128, 8), (1, P_DB1, 16)):
        rows = jnp.concatenate([db[:, (first + i) * 128 : (first + i + 1) * 128] for i in range(8)], axis=0)
        put(half, slice(0, EXP), slice(at, at + 128), jnp.broadcast_to(rows[None], (CHIPS, 8, 128)).reshape(EXP, 128).astype(B))

    act = act.astype(B).astype(F)
    both = pltpu.roll(act, mine, 0) + pltpu.roll(act, mine + 4, 0)
    both = jnp.broadcast_to(both[None], (CHIPS, 8, D)).reshape(EXP, D)
    feature = lax.broadcasted_iota(jnp.int32, (1, D), 1)
    device = lax.broadcasted_iota(jnp.int32, (EXP, 1), 0) >> 3
    both = jnp.where(group_of(feature, 6) == device, both, 0.0).astype(B)
    feature = lax.broadcasted_iota(jnp.int32, (D, 1), 0)
    lane = lax.broadcasted_iota(jnp.int32, (1, 128), 1)
    pick = ((feature - 6 * group_of(feature, 6)) == (lane & 7)) & (lane < 16)
    found = dot(both, pick.astype(F).astype(B))
    put(1, slice(0, EXP), slice(P_COND, P_HALF), jnp.where((r8 >> 2) == (lane >> 3), found, 0.0).astype(B))


KEEP = (
    ("ain", (ROWS, D), B),
    ("qkv", (ROWS, 3 * D), B),
    ("lse", (6, 8, SEQ), F),
    ("att", (ROWS, D), B),
    ("o", (ROWS, D), F),
    ("x1", (ROWS, D), F),
    ("min", (ROWS, D), B),
    ("slope", (ROWS, FF), F),
    ("act", (ROWS, FF), B),
    ("f", (ROWS, D), F),
)
WEIGHTS = (("main", (D, C_MAIN), B), ("bias", (1, C_MAIN), F), ("bias2", (1, D), F), ("fc2", (FF, D), B))
TEMPS = (
    ("dmod", (8, 6 * D), F),
    ("db", (1, 3072), F),
    ("part", (EXP, QUARTER), F),
    ("part2", (EXP, D), F),
    ("wide2", (EXP, ROWS), B),
    ("df", (ROWS, D), B),
    ("dz", (ROWS, FF), B),
    ("wide", (EXP, ROWS), B),
    ("dx1", (ROWS, D), F),
    ("datt", (ROWS, D), B),
    ("dqkv", (ROWS, 3 * D), B),
)
MOD = (("mod", (8, 6 * D), F),)


def buffers(table):
    return [pltpu.VMEM(shape, dtype) for _, shape, dtype in table]


def shapes(table):
    return [jax.ShapeDtypeStruct(shape, dtype) for _, shape, dtype in table]


def named(table, refs):
    return {name: ref for (name, _, _), ref in zip(table, refs)}


def fetch_halves(core, own, other, g, sems):
    def go(low, high):
        copies = [
            pltpu.make_async_copy(low, g.at[:, :G_HALF], sems.at[0]),
            pltpu.make_async_copy(high, g.at[:, G_HALF:], sems.at[1]),
        ]
        for copy in copies:
            copy.start()
        for copy in copies:
            copy.wait()

    @pl.when(core == 0)
    def _():
        go(own, other)

    @pl.when(core != 0)
    def _():
        go(other, own)


def fetch_ada(core, own, other, g, sems):
    def go(high):
        copy = pltpu.make_async_copy(high.at[:, G_ADA - G_HALF : G_BIAS - G_HALF], g, sems.at[0])
        copy.start()
        copy.wait()

    @pl.when(core == 0)
    def _():
        go(other)

    @pl.when(core != 0)
    def _():
        go(own)


def pack_out(pack, keep, send, sems):
    copies = [pltpu.make_async_copy(pack.at[i], ref, sems.at[i]) for i, ref in enumerate((keep, send))]
    for copy in copies:
        copy.start()
    for copy in copies:
        copy.wait()


def putter(core, pack):
    def put(half, rows, cols, value):
        slot = core if half == 0 else 1 - core
        pack[slot, rows, cols] = value

    return put


def front_kernel(core, own, other, x, cond, *refs):
    n_keep, n_w = len(KEEP), len(WEIGHTS)
    y = refs[0]
    k = named(KEEP, refs[1 : 1 + n_keep])
    w = named(WEIGHTS, refs[1 + n_keep : 1 + n_keep + n_w])
    mod, g, sel, selt, sems = refs[1 + n_keep + n_w :]
    build_selectors(sel, selt)
    fetch_halves(core[0], own, other, g, sems)
    ada = unpack(g, selt, w)
    modulate(cond, g, selt, ada, mod)
    forward(x, w, mod, k, y)


def turn_kernel(core, whole, x, cond, grad, y, dx, dc, keep, send, *refs):
    n_keep, n_w, n_t = len(KEEP), len(WEIGHTS), len(TEMPS)
    k = named(KEEP, refs[:n_keep])
    w = named(WEIGHTS, refs[n_keep : n_keep + n_w])
    t = named(TEMPS, refs[n_keep + n_w : n_keep + n_w + n_t])
    mod, g, sel, selt, pack, sems = refs[n_keep + n_w + n_t :]
    copy = pltpu.make_async_copy(whole, g, sems.at[0])
    copy.start()
    build_selectors(sel, selt)
    copy.wait()
    ada = unpack(g, selt, w)
    modulate(cond, g, selt, ada, mod)
    forward(x, w, mod, k, y)
    backward(core[0], grad, x, cond, g, G_ADA, sel, selt, w, mod, k, t, dx, dc, putter(core[0], pack))
    pack_out(pack, keep, send, sems)


def back_kernel(core, own, other, x, cond, grad, *refs):
    n_keep, n_w, n_t = len(KEEP), len(WEIGHTS), len(TEMPS)
    k = named(KEEP, refs[:n_keep])
    w = named(WEIGHTS, refs[n_keep : n_keep + n_w])
    mod, dx, dc, keep, send = refs[n_keep + n_w : n_keep + n_w + 5]
    refs = refs[n_keep + n_w + 5 :]
    t = named(TEMPS, refs[:n_t])
    g, sel, selt, pack, sems = refs[n_t:]
    build_selectors(sel, selt)
    fetch_ada(core[0], own, other, g, sems)
    backward(core[0], grad, x, cond, g, 0, sel, selt, w, mod, k, t, dx, dc, putter(core[0], pack))
    pack_out(pack, keep, send, sems)


VM = pl.BlockSpec(memory_space=pltpu.VMEM)
ANY = pl.BlockSpec(memory_space=pl.ANY)
SM = pl.BlockSpec(memory_space=pltpu.SMEM)
PARAMS = pltpu.CompilerParams(vmem_limit_bytes=60 * 1024 * 1024)
G_BUF = pltpu.VMEM((EXP, G_END), B)
ADA_BUF = pltpu.VMEM((EXP, G_BIAS - G_ADA), B)
SEL_BUFS = [pltpu.VMEM((4, EXP, D), B), pltpu.VMEM((4, D, EXP), B)]
SEMS = pltpu.SemaphoreType.DMA((2,))
ROWS_OUT = jax.ShapeDtypeStruct((ROWS, D), B)
COND_OUT = jax.ShapeDtypeStruct((8, D), F)
HALF_OUT = jax.ShapeDtypeStruct((EXP, P_HALF), B)
PACK_BUF = pltpu.VMEM((2, EXP, P_HALF), B)


def cost(units):
    return pl.CostEstimate(flops=units * 2_000_000_000, bytes_accessed=units * 10_000_000, transcendentals=units * 2_000_000)


def front(core, own, other, x, cond):
    outs = [ROWS_OUT] + shapes(KEEP) + shapes(WEIGHTS) + shapes(MOD)
    return pl.pallas_call(
        front_kernel,
        out_shape=outs,
        in_specs=[SM, ANY, ANY, VM, VM],
        out_specs=[VM] * len(outs),
        scratch_shapes=[G_BUF, *SEL_BUFS, SEMS],
        compiler_params=PARAMS,
        cost_estimate=cost(1),
        name="front",
    )(core, own, other, x, cond)


def turn(core, whole, x, cond, grad):
    return pl.pallas_call(
        turn_kernel,
        out_shape=[ROWS_OUT, ROWS_OUT, COND_OUT, HALF_OUT, HALF_OUT],
        in_specs=[SM, ANY, VM, VM, VM],
        out_specs=[VM] * 3 + [ANY] * 2,
        scratch_shapes=buffers(KEEP) + buffers(WEIGHTS) + buffers(TEMPS) + buffers(MOD) + [G_BUF, *SEL_BUFS, PACK_BUF, SEMS],
        compiler_params=PARAMS,
        cost_estimate=cost(3),
        name="turn",
    )(core, whole, x, cond, grad)


def back(core, own, other, x, cond, grad, kept):
    return pl.pallas_call(
        back_kernel,
        out_shape=[ROWS_OUT, COND_OUT, HALF_OUT, HALF_OUT],
        in_specs=[SM, ANY, ANY, VM, VM, VM] + [VM] * len(kept),
        out_specs=[VM] * 2 + [ANY] * 2,
        scratch_shapes=buffers(TEMPS) + [ADA_BUF, *SEL_BUFS, PACK_BUF, SEMS],
        compiler_params=PARAMS,
        cost_estimate=cost(2),
        name="back",
    )(core, own, other, x, cond, grad, *kept)


def line_up(w_qkv, b_qv, w_proj, b_proj, w_fc1, b_fc1, w_fc2, b_fc2, w_ada, b_ada):
    def pieces(rows):
        rows = jnp.concatenate(rows, axis=0)
        rows = jnp.pad(rows, ((0, -rows.shape[0] % 8), (0, 0)))
        return [rows[i : i + 8] for i in range(0, rows.shape[0], 8)]

    main = jnp.concatenate([w_qkv, w_proj, w_fc1], axis=1)
    bias = jnp.concatenate([b_qv, b_proj, b_fc1, b_fc2, b_ada])
    bias = jnp.pad(bias, (0, 1024 - bias.shape[0])).reshape(8, 128)
    return jnp.concatenate(
        pieces([main[:, i * QUARTER : (i + 1) * QUARTER] for i in range(4)])
        + pieces([w_fc2])
        + pieces([w_ada[:, i * 256 : (i + 1) * 256] for i in range(9)])
        + [bias],
        axis=1,
    )


def swap(x):
    return lax.ppermute(x, "pipe", [(0, 1), (1, 0)])


def to_all(block):
    copies = jnp.broadcast_to(block[None], (CHIPS, *block.shape))
    return lax.all_to_all(copies, "shard", 0, 0, tiled=True).reshape(EXP, block.shape[1])


def scatter(block):
    return lax.all_to_all(block.reshape(CHIPS, 8, P_HALF), "shard", 0, 0, tiled=True)


def shards(latents, conditions, cotangent, w_qkv, b_qv, w_proj, b_proj, w_fc1, b_fc1, w_fc2, b_fc2, w_ada, b_ada):
    p = lax.axis_index("pipe")
    j = lax.axis_index("shard")
    first = p == 0
    core = p.reshape(1).astype(jnp.int32)
    block = line_up(w_qkv[0], b_qv[0], w_proj[0], b_proj[0], w_fc1[0], b_fc1[0], w_fc2[0], b_fc2[0], w_ada[0], b_ada[0])
    block_other = swap(block)
    block1 = jnp.where(first, block_other, block)
    own1 = lax.all_gather(block1, "shard", tiled=True)
    half0 = jnp.where(first, block[:, :G_HALF], block_other[:, G_HALF:])
    own0 = to_all(half0)
    other0 = swap(own0)
    x = lax.dynamic_index_in_dim(latents, p, 0, keepdims=False).reshape(ROWS, D)
    cot = lax.dynamic_index_in_dim(cotangent, p, 0, keepdims=False).reshape(ROWS, D)
    cond = lax.dynamic_index_in_dim(conditions, p, 0, keepdims=False).astype(F)
    cond = jnp.concatenate([cond, jnp.zeros((6, D), F)], axis=0)

    h, *kept = front(core, own0, other0, x, cond)
    y, dx1, dc1, keep1, send1 = turn(core, own1, h, cond, cot)
    parts1 = scatter(keep1 + swap(send1))
    dx0, dc0, keep0, send0 = back(core, own0, other0, x, cond, dx1, kept)
    parts1, send0 = lax.optimization_barrier((parts1, send0))
    parts0 = scatter(keep0 + swap(send0))

    def pair(for_first, for_second):
        keep = jnp.where(first, for_first, for_second)
        came = swap(jnp.where(first, for_second, for_first))
        both = jnp.where(first, jnp.stack([keep, came]), jnp.stack([came, keep]))
        return both.reshape(1, 2, 2, SEQ, D)

    section_outputs = pair(h, y)
    input_grads = pair(dx0, dx1)
    dc = (dc0 + dc1)[:2]
    dc_other = swap(dc)
    cond_grad = jnp.where(first, jnp.stack([dc, dc_other]), jnp.stack([dc_other, dc]))

    def reduced(parts):
        lot = jnp.sum(parts.astype(F), axis=0)
        flat = parts.reshape(EXP, P_HALF)
        ada = lax.dot_general(
            flat[:, P_COND : P_COND + 16], flat[:, P_MOD:P_DB1], (((0,), (0,)), ((), ())), preferred_element_type=F
        )
        return jnp.concatenate([lot, ada[:8], ada[8:]], axis=1)

    lot0 = reduced(parts0)
    lot1 = reduced(parts1)
    kept_half = jnp.where(first, lot0, lot1)
    came_half = swap(jnp.where(first, lot1, lot0))
    low = jnp.where(first, kept_half, came_half)
    high = jnp.where(first, came_half, kept_half)

    rows = jnp.concatenate([low[:, a * QUARTER : (a + 1) * QUARTER] for a in range(3)], axis=0)
    quarters = [rows[6 * q : 6 * q + 6] for q in range(4)]
    db = jnp.concatenate([low[:, P_DB0 : P_DB0 + 128], low[:, P_DB0 + 128 : P_HALF], high[:, P_DB1:P_COND]], axis=0).reshape(-1)
    sums = high[:, P_MOD:P_DB1]
    db_ada = jnp.concatenate([sums[:4].sum(axis=0), sums[4:].sum(axis=0)])

    def slice_of(line, at, width):
        return lax.dynamic_slice(line, (at + width * j,), (width,))

    outs = (
        jnp.concatenate([quarters[0], quarters[1][:, :384]], axis=1),
        slice_of(db, 0, 12),
        quarters[1][:, 384:],
        slice_of(db, 768, 6),
        jnp.concatenate([quarters[2], quarters[3]], axis=1),
        slice_of(db, 1152, 24),
        jnp.concatenate([high[:, a * D : (a + 1) * D] for a in range(3)], axis=0),
        slice_of(db, 2688, 6),
        jnp.concatenate([high[:6, P_HALF : P_HALF + 1152], high[:6, P_HALF + 1152 :]], axis=1),
        slice_of(db_ada, 0, 36),
    )
    return (section_outputs, input_grads, cond_grad) + tuple(o[None] for o in outs)


def solution(mesh):
    rows = P(None, "shard", None, None)
    wide = P("pipe", "shard", None)
    thin = P("pipe", "shard")
    both = P("pipe", None, "shard", None, None)
    pairs = (wide, thin) * 5
    return jax.shard_map(
        shards,
        mesh=mesh,
        in_specs=(rows, P(None, "shard", None), rows) + pairs,
        out_specs=(both, both, P(None, "shard", None)) + pairs,
        check_vma=False,
    )
```

```python
import functools

import jax
import jax.numpy as jnp
from jax import lax
from jax.experimental import pallas as pl
from jax.experimental.pallas import tpu as pltpu
from jax.sharding import PartitionSpec as P

F = jnp.float32
B = jnp.bfloat16
D = 384
HEADS = 6
HEAD = 64
FF = 1536
SEQ = 256
EPS = 1e-06
CHIPS = 64
ROWS = 512
EXP = 512

C_QKV, C_PROJ, C_FC1, C_MAIN = 0, 1152, 1536, 3072
QUARTER = 768

G_FC2, G_ADA, G_BIAS, G_END = 2304, 3456, 5248, 5376
G_HALF = 2688
BIASES = ((0, 12), (12, 6), (18, 24), (42, 6), (48, 36))

P_HALF = 2560
P_DB0 = 2304
P_MOD, P_DB1, P_COND = 1152, 2304, 2432
SHIFTS = (0, 6, 4, 2)

K0 = 0.7978845608028654
K1 = 0.044715

UNROLL = 6
NN = (1, 0)
NT = (1, 1)
TN = (0, 0)


def dot(a, b, dims=NN):
    return lax.dot_general(a, b, (((dims[0],), (dims[1],)), ((), ())), preferred_element_type=F)


def targets(shape, dim, shift):
    at = lax.broadcasted_iota(jnp.int32, shape, dim)
    r = ((at & 7) + (8 - shift)) & 7
    return jnp.where(r < 6, (at >> 3) * 6 + r, -1)


def build_selectors(sel, selt):
    col = lax.broadcasted_iota(jnp.int32, (1, D), 1)
    row = lax.broadcasted_iota(jnp.int32, (D, 1), 0)
    for i, shift in enumerate(SHIFTS):
        sel[i] = (targets((EXP, 1), 0, shift) == col).astype(F).astype(B)
        selt[i] = (row == targets((1, EXP), 1, shift)).astype(F).astype(B)


def group_of(n, width):
    return jnp.floor((n.astype(F) + 0.5) * (1.0 / width)).astype(jnp.int32)


def natural_bias(gb, lane, width):
    n = CHIPS * width
    at = lax.broadcasted_iota(jnp.int32, (1, n), 1)
    owner = group_of(at, width)
    spot = at - owner * width + lane
    pick = (lax.broadcasted_iota(jnp.int32, (128, 1), 0) == spot).astype(F).astype(B)
    wide = dot(gb, pick)
    return jnp.sum(jnp.where(lax.broadcasted_iota(jnp.int32, (CHIPS, 1), 0) == owner, wide, 0.0), axis=0, keepdims=True)


def tile_row(shape, dim):
    return lax.broadcasted_iota(jnp.int32, shape, dim) & 7


def stats(v):
    centre = v - jnp.mean(v, axis=-1, keepdims=True)
    inv = lax.rsqrt(jnp.mean(centre * centre, axis=-1, keepdims=True) + EPS)
    return centre * inv, inv


def norm_back(g, n, inv):
    mg = jnp.mean(g, axis=-1, keepdims=True)
    mgn = jnp.mean(g * n, axis=-1, keepdims=True)
    return inv * (g - mg - n * mgn)


def head_masks():
    lane = lax.broadcasted_iota(jnp.int32, (1, 128), 1)
    low = (lane < HEAD).astype(F)
    return low.astype(B), (1.0 - low).astype(B)


def unpack(g, selt, w):
    r8 = tile_row((EXP, 1), 0)

    def piece(a, c):
        return g[:, a * QUARTER + c : a * QUARTER + c + 384]

    def merge(edge, a, c):
        return jnp.where(r8 >= edge, piece(a, c).astype(F), piece(a + 1, c).astype(F)).astype(B)

    for c in (0, 384):
        w["main"][:, c : c + 384] = dot(selt[0], piece(0, c)).astype(B)
        w["main"][:, QUARTER + c : QUARTER + c + 384] = dot(selt[1], merge(6, 0, c)).astype(B)
        w["main"][:, 2 * QUARTER + c : 2 * QUARTER + c + 384] = dot(selt[2], merge(4, 1, c)).astype(B)
        w["main"][:, 3 * QUARTER + c : 3 * QUARTER + c + 384] = dot(selt[3], piece(2, c)).astype(B)

    lead = (lax.broadcasted_iota(jnp.int32, (CHIPS, EXP), 0) * 8 == lax.broadcasted_iota(jnp.int32, (CHIPS, EXP), 1)).astype(F).astype(B)
    gb = dot(lead, g[:, G_BIAS:G_END]).astype(B)
    qv, proj, fc1, fc2, ada = (natural_bias(gb, lane, width) for lane, width in BIASES)
    w["bias"][:, :D] = qv[:, :D]
    w["bias"][:, D : 2 * D] = jnp.zeros((1, D), F)
    w["bias"][:, 2 * D : C_PROJ] = qv[:, D:]
    w["bias"][:, C_PROJ:C_FC1] = proj
    w["bias"][:, C_FC1:C_MAIN] = fc1
    w["bias2"][...] = fc2

    def step2(i, _):
        at = pl.multiple_of(i * 128, 128)
        parts = [g[pl.ds(at, 128), G_FC2 + a * D : G_FC2 + (a + 1) * D].astype(F).reshape(16, 8, D) for a in range(3)]
        whole = jnp.concatenate(parts, axis=1).reshape(D, D).astype(B)
        w["fc2"][pl.ds(pl.multiple_of(i * D, D), D), :] = whole
        return 0

    lax.fori_loop(0, 4, step2, 0)
    return ada


def ada_groups():
    return [(i % 4, (6 * i) // 8, SHIFTS[i % 4] in (6, 4)) for i in range(9)]


def modulate(cond, g, selt, ada, mod):
    c = cond[...]
    act = (c * jax.nn.sigmoid(c)).astype(B)
    r8 = tile_row((1, EXP), 1)
    wides = [dot(act, selt[i]) for i in range(4)]
    for n, (i, a, more) in enumerate(ada_groups()):
        at = G_ADA + a * 256
        first = jnp.where(r8 >= SHIFTS[i], wides[i], 0.0).astype(B)
        part = dot(first, g[:, at : at + 256])
        if more:
            part = part + dot(jnp.where(r8 < SHIFTS[i], wides[i], 0.0).astype(B), g[:, at + 256 : at + 512])
        mod[:, n * 256 : (n + 1) * 256] = part + ada[:, n * 256 : (n + 1) * 256]


def cond_back(dm, g, g_at, selt):
    r8 = tile_row((EXP, 1), 0)
    sums = [jnp.zeros((EXP, 8), F)] * 4
    for n, (i, a, more) in enumerate(ada_groups()):
        at = g_at + a * 256
        piece = dm[:, n * 256 : (n + 1) * 256]
        sums[i] = sums[i] + jnp.where(r8 >= SHIFTS[i], dot(g[:, at : at + 256], piece, NT), 0.0)
        if more:
            sums[i] = sums[i] + jnp.where(r8 < SHIFTS[i], dot(g[:, at + 256 : at + 512], piece, NT), 0.0)
    total = jnp.zeros((8, D), F)
    for i in range(4):
        rest = sums[i].T
        for _ in range(3):
            level = rest.astype(B)
            rest = rest - level.astype(F)
            total = total + dot(level, selt[i], NT)
    return total


def forward(x, w, mod, k, y, save=lambda *names: None):
    main, bias, fc2 = w["main"], w["bias"], w["fc2"]

    def ln_in(i, _):
        rows = pl.ds(pl.multiple_of(i * 128, 128), 128)
        lat = pl.ds(i // 2, 1)
        n, _ = stats(x[rows, :].astype(F))
        k["ain"][rows, :] = (n * (1.0 + mod[lat, D : 2 * D]) + mod[lat, :D]).astype(B)
        return 0

    lax.fori_loop(0, 4, ln_in, 0, unroll=True)

    for c in range(3):
        cs = slice(c * D, (c + 1) * D)
        k["qkv"][:, cs] = (dot(k["ain"][...], main[:, cs]) + bias[:, cs]).astype(B)

    low, high = head_masks()

    def attend(i, _):
        rows = pl.ds(pl.multiple_of((i // 3) * SEQ, SEQ), SEQ)
        at = (i % 3) * 128
        q = k["qkv"][rows, pl.ds(pl.multiple_of(at, 128), 128)]
        key = k["qkv"][rows, pl.ds(pl.multiple_of(D + at, 128), 128)]
        vt = k["qkv"][rows, pl.ds(pl.multiple_of(2 * D + at, 128), 128)].T
        heads = []
        for h, m in enumerate((low, high)):
            s = dot(key, q * (m * 0.125), NT)
            top = jnp.max(s, axis=0, keepdims=True)
            e = jnp.exp(s - top)
            t = jnp.sum(e, axis=0, keepdims=True)
            p = (e * (1.0 / t)).astype(B)
            k["lse"][i, h : h + 1, :] = top + jnp.log(t)
            heads.append(dot(vt[h * HEAD : (h + 1) * HEAD], p))
        k["att"][rows, pl.ds(pl.multiple_of(at, 128), 128)] = jnp.concatenate(heads, axis=0).T.astype(B)
        return 0

    lax.fori_loop(0, 6, attend, 0, unroll=UNROLL)
    save("ain", "qkv", "lse", "att")
    k["o"][...] = dot(k["att"][...], main[:, C_PROJ:C_FC1]) + bias[:, C_PROJ:C_FC1]

    def mid(i, _):
        rows = pl.ds(pl.multiple_of(i * 128, 128), 128)
        lat = pl.ds(i // 2, 1)
        x1 = x[rows, :].astype(F) + mod[lat, 2 * D : 3 * D] * k["o"][rows, :]
        k["x1"][rows, :] = x1
        n, _ = stats(x1)
        k["min"][rows, :] = (n * (1.0 + mod[lat, 4 * D : 5 * D]) + mod[lat, 3 * D : 4 * D]).astype(B)
        return 0

    lax.fori_loop(0, 4, mid, 0, unroll=True)

    def mlp(i, _):
        at = pl.multiple_of(i * 256, 256)
        cs = pl.ds(at, 256)
        ws = pl.ds(pl.multiple_of(C_FC1 + at, 256), 256)
        z = dot(k["min"][...], main[:, ws]) + bias[:, ws]
        zz = z * z
        t = jnp.tanh(z * (K0 + K0 * K1 * zz))
        half = 0.5 + 0.5 * t
        k["act"][:, cs] = (z * half).astype(B)
        k["slope"][:, cs] = half + (0.5 * z) * (1.0 - t * t) * (K0 + 3.0 * K0 * K1 * zz)
        return 0

    lax.fori_loop(0, 6, mlp, 0, unroll=True)

    save("o", "x1", "min", "slope", "act")
    k["f"][...] = dot(k["act"][...], fc2[...]) + w["bias2"][...]

    def out(i, _):
        rows = pl.ds(pl.multiple_of(i * 128, 128), 128)
        lat = pl.ds(i // 2, 1)
        y[rows, :] = (k["x1"][rows, :] + mod[lat, 5 * D : 6 * D] * k["f"][rows, :]).astype(B)
        return 0

    save("f")
    lax.fori_loop(0, 4, out, 0, unroll=True)


def token_sum(v):
    return jnp.sum(v, axis=0, keepdims=True)


def spread(sel, i, v):
    return dot(sel[i], v, NT).astype(B)


def backward(core, grad, x, cond, g, g_at, sel, selt, w, mod, k, t, dx, dc, put, ship, finish):
    main, fc2 = w["main"], w["fc2"]
    dmod = t["dmod"]
    dmod[...] = jnp.zeros_like(dmod)

    def add_mod(lat, piece, v):
        cs = slice(piece * D, (piece + 1) * D)
        dmod[lat, cs] = dmod[lat, cs] + v

    t["db"][...] = jnp.zeros_like(t["db"])
    r8 = tile_row((EXP, 1), 0)

    def add_db(at, v):
        t["db"][:, at : at + v.shape[1]] = t["db"][:, at : at + v.shape[1]] + v


    def start(i, _):
        rows = pl.ds(pl.multiple_of(i * 128, 128), 128)
        lat = pl.ds(i // 2, 1)
        gr = grad[rows, :].astype(F)
        df = (gr * mod[lat, 5 * D : 6 * D]).astype(B)
        t["df"][rows, :] = df
        add_mod(lat, 5, token_sum(gr * k["f"][rows, :]))
        add_db(2688, token_sum(df.astype(F)))
        return 0

    lax.fori_loop(0, 4, start, 0, unroll=True)

    def dmlp(i, _):
        cs = pl.ds(pl.multiple_of(i * 256, 256), 256)
        da = dot(t["df"][...], fc2[cs, :], NT)
        dz = (da * k["slope"][:, cs]).astype(B)
        t["dz"][:, cs] = dz
        ds = pl.ds(pl.multiple_of(1152 + i * 256, 128), 256)
        t["db"][:, ds] = token_sum(dz.astype(F))
        return 0

    lax.fori_loop(0, 6, dmlp, 0, unroll=True)

    t["wide2"][...] = spread(sel, 2, k["min"][...])
    t["wide"][...] = spread(sel, 3, k["min"][...])
    for c in range(0, QUARTER, 256):
        d2 = dot(t["wide2"][...], t["dz"][:, c : c + 256])
        d3 = dot(t["wide"][...], t["dz"][:, QUARTER + c : QUARTER + c + 256])
        put(0, slice(0, EXP), slice(2 * QUARTER + c, 2 * QUARTER + c + 256), jnp.where(r8 < 2, d2, d3).astype(B))
        t["part"][:, c : c + 256] = d2

    for c in range(4):
        part = dot(k["act"][:, c * D : (c + 1) * D], t["df"][...], TN).reshape(16, 24, D)
        for a in range(3):
            put(
                1,
                slice(c * 128, (c + 1) * 128),
                slice(a * D, (a + 1) * D),
                part[:, 8 * a : 8 * a + 8, :].reshape(128, D).astype(B),
            )

    t["dn"][...] = dot(t["dz"][...], main[:, C_FC1:C_MAIN], NT)

    def dmid(i, _):
        rows = pl.ds(pl.multiple_of(i * 128, 128), 128)
        lat = pl.ds(i // 2, 1)
        dmin = t["dn"][rows, :]
        n, inv = stats(k["x1"][rows, :])
        add_mod(lat, 4, token_sum(dmin * n))
        add_mod(lat, 3, token_sum(dmin))
        d1 = grad[rows, :].astype(F) + norm_back(dmin * (1.0 + mod[lat, 4 * D : 5 * D]), n, inv)
        t["dx1"][rows, :] = d1
        do = (d1 * mod[lat, 2 * D : 3 * D]).astype(B)
        add_mod(lat, 2, token_sum(d1 * k["o"][rows, :]))
        t["df"][rows, :] = do
        add_db(768, token_sum(do.astype(F)))
        return 0

    lax.fori_loop(0, 4, dmid, 0, unroll=True)
    t["datt"][...] = dot(t["df"][...], main[:, C_PROJ:C_FC1], NT).astype(B)

    t["wide2"][...] = spread(sel, 1, k["att"][...])
    d1 = dot(t["wide2"][...], t["df"][...])
    put(0, slice(0, EXP), slice(QUARTER + 384, 2 * QUARTER), jnp.where(r8 < 4, d1, t["part"][:, 384:]).astype(B))
    t["part2"][...] = d1

    low, high = head_masks()

    def dattend(i, _):
        rows = pl.ds(pl.multiple_of((i // 3) * SEQ, SEQ), SEQ)
        at = (i % 3) * 128
        qs = pl.ds(pl.multiple_of(at, 128), 128)
        ks = pl.ds(pl.multiple_of(D + at, 128), 128)
        vs = pl.ds(pl.multiple_of(2 * D + at, 128), 128)
        q = k["qkv"][rows, qs]
        key = k["qkv"][rows, ks]
        v = k["qkv"][rows, vs]
        da = t["datt"][rows, qs]
        kt = key.T
        dk = dv = None
        dqs = []
        for h, m in enumerate((low, high)):
            qm = q * (m * 0.125)
            dam = da * m
            s = dot(key, qm, NT)
            p = jnp.exp(s - k["lse"][i, h : h + 1, :])
            dp = dot(v, dam, NT)
            ds = (p * (dp - jnp.sum(p * dp, axis=0, keepdims=True))).astype(B)
            v1 = dot(p.astype(B), dam)
            k1 = dot(ds, qm)
            dqs.append(dot(kt[h * HEAD : (h + 1) * HEAD], ds))
            dv = v1 if dv is None else dv + v1
            dk = k1 if dk is None else dk + k1
        t["dqkv"][rows, qs] = (jnp.concatenate(dqs, axis=0).T * 0.125).astype(B)
        t["dqkv"][rows, ks] = dk.astype(B)
        t["dqkv"][rows, vs] = dv.astype(B)
        return 0

    lax.fori_loop(0, 6, dattend, 0, unroll=UNROLL)

    t["wide"][...] = spread(sel, 0, k["ain"][...])
    t["wide2"][...] = spread(sel, 1, k["ain"][...])
    d1 = dot(t["wide2"][...], t["dqkv"][:, QUARTER:])
    d0 = dot(t["wide"][...], t["dqkv"][:, :384])
    put(0, slice(0, EXP), slice(0, 384), jnp.where(r8 < 6, d0, d1).astype(B))
    put(0, slice(0, EXP), slice(QUARTER, QUARTER + 384), jnp.where(r8 < 4, d1, t["part"][:, :384]).astype(B))
    d0 = dot(t["wide"][...], t["dqkv"][:, 384:QUARTER])
    put(0, slice(0, EXP), slice(384, QUARTER), jnp.where(r8 < 6, d0, t["part2"][...]).astype(B))
    ship(0, 0, P_DB0)
    ship(1, 0, P_MOD)

    def bias_sums(i, _):
        rows = pl.ds(pl.multiple_of(i * 128, 128), 128)
        add_db(0, token_sum(t["dqkv"][rows, :D].astype(F)))
        add_db(D, token_sum(t["dqkv"][rows, 2 * D :].astype(F)))
        return 0

    lax.fori_loop(0, 4, bias_sums, 0, unroll=True)

    t["dn"][...] = dot(t["dqkv"][...], main[:, C_QKV:C_PROJ], NT)

    def dlast(i, _):
        rows = pl.ds(pl.multiple_of(i * 128, 128), 128)
        lat = pl.ds(i // 2, 1)
        dain = t["dn"][rows, :]
        n, inv = stats(x[rows, :].astype(F))
        add_mod(lat, 1, token_sum(dain * n))
        add_mod(lat, 0, token_sum(dain))
        back = norm_back(dain * (1.0 + mod[lat, D : 2 * D]), n, inv)
        dx[rows, :] = (t["dx1"][rows, :] + back).astype(B)
        return 0

    lax.fori_loop(0, 4, dlast, 0, unroll=True)

    c = cond[...]
    sig = jax.nn.sigmoid(c)
    act = c * sig
    dm = dmod[...].astype(B).astype(F)
    dc[...] = cond_back(dm.astype(B), g, g_at, selt) * (sig * (1.0 + c * (1.0 - sig)))

    mine = 2 * core
    block = pltpu.roll(dm[:, :1152], mine, 0) + pltpu.roll(dm[:, 1152:], mine + 4, 0)
    for q in range(4):
        rows = slice(q * 128, (q + 1) * 128)
        put(1, rows, slice(P_MOD, P_DB1), jnp.broadcast_to(block[None], (16, 8, 1152)).reshape(128, 1152).astype(B))

    db = t["db"]
    for half, at, first in ((0, P_DB0, 0), (0, P_DB0 + 128, 8), (1, P_DB1, 16)):
        rows = jnp.concatenate([db[:, (first + i) * 128 : (first + i + 1) * 128] for i in range(8)], axis=0)
        put(half, slice(0, EXP), slice(at, at + 128), jnp.broadcast_to(rows[None], (CHIPS, 8, 128)).reshape(EXP, 128).astype(B))

    act = act.astype(B).astype(F)
    both = pltpu.roll(act, mine, 0) + pltpu.roll(act, mine + 4, 0)
    both = jnp.broadcast_to(both[None], (CHIPS, 8, D)).reshape(EXP, D)
    feature = lax.broadcasted_iota(jnp.int32, (1, D), 1)
    device = lax.broadcasted_iota(jnp.int32, (EXP, 1), 0) >> 3
    both = jnp.where(group_of(feature, 6) == device, both, 0.0).astype(B)
    feature = lax.broadcasted_iota(jnp.int32, (D, 1), 0)
    lane = lax.broadcasted_iota(jnp.int32, (1, 128), 1)
    pick = ((feature - 6 * group_of(feature, 6)) == (lane & 7)) & (lane < 16)
    found = dot(both, pick.astype(F).astype(B))
    put(1, slice(0, EXP), slice(P_COND, P_HALF), jnp.where((r8 >> 2) == (lane >> 3), found, 0.0).astype(B))
    ship(0, P_DB0, P_HALF)
    ship(1, P_MOD, P_HALF)
    finish()


KEEP = (
    ("ain", (ROWS, D), B),
    ("qkv", (ROWS, 3 * D), B),
    ("lse", (6, 8, SEQ), F),
    ("att", (ROWS, D), B),
    ("o", (ROWS, D), F),
    ("x1", (ROWS, D), F),
    ("min", (ROWS, D), B),
    ("slope", (ROWS, FF), F),
    ("act", (ROWS, FF), B),
    ("f", (ROWS, D), F),
)
WEIGHTS = (("main", (D, C_MAIN), B), ("bias", (1, C_MAIN), F), ("bias2", (1, D), F), ("fc2", (FF, D), B))
TEMPS = (
    ("dmod", (8, 6 * D), F),
    ("db", (1, 3072), F),
    ("part", (EXP, QUARTER), F),
    ("part2", (EXP, D), F),
    ("wide2", (EXP, ROWS), B),
    ("df", (ROWS, D), B),
    ("dz", (ROWS, FF), B),
    ("wide", (EXP, ROWS), B),
    ("dx1", (ROWS, D), F),
    ("dn", (ROWS, D), F),
    ("datt", (ROWS, D), B),
    ("dqkv", (ROWS, 3 * D), B),
)
MOD = (("mod", (8, 6 * D), F),)


def buffers(table):
    return [pltpu.VMEM(shape, dtype) for _, shape, dtype in table]


def shapes(table):
    return [jax.ShapeDtypeStruct(shape, dtype) for _, shape, dtype in table]


def named(table, refs):
    return {name: ref for (name, _, _), ref in zip(table, refs)}


def fetch_halves(core, own, other, g, sems):
    def go(low, high):
        copies = [
            pltpu.make_async_copy(low, g.at[:, :G_HALF], sems.at[0]),
            pltpu.make_async_copy(high, g.at[:, G_HALF:], sems.at[1]),
        ]
        for copy in copies:
            copy.start()
        for copy in copies:
            copy.wait()

    @pl.when(core == 0)
    def _():
        go(own, other)

    @pl.when(core != 0)
    def _():
        go(other, own)


def fetch_ada(core, own, other, g, sems):
    def go(high):
        copy = pltpu.make_async_copy(high.at[:, G_ADA - G_HALF : G_BIAS - G_HALF], g, sems.at[0])
        copy.start()
        copy.wait()

    @pl.when(core == 0)
    def _():
        go(other)

    @pl.when(core != 0)
    def _():
        go(own)


def sender(core, pack, keep, send, sems):
    started = []

    def start(half, first, last):
        n = len(started)
        cols = slice(first, last)

        def copy(slot, ref):
            return pltpu.make_async_copy(pack.at[slot, :, cols], ref.at[:, cols], sems.at[n])

        mine = copy(0, keep)
        theirs = copy(1, send)
        started.append((half, mine, theirs))

        @pl.when(core == half)
        def _():
            mine.start()

        @pl.when(core != half)
        def _():
            theirs.start()

    def finish():
        for half, mine, theirs in started:

            @pl.when(core == half)
            def _(mine=mine):
                mine.wait()

            @pl.when(core != half)
            def _(theirs=theirs):
                theirs.wait()

    return start, finish


def putter(core, pack):
    def put(half, rows, cols, value):
        slot = core if half == 0 else 1 - core
        pack[slot, rows, cols] = value

    return put


def front_kernel(core, own, other, x, cond, y, *refs):
    saved = KEEP + WEIGHTS + MOD
    n = len(saved)
    out = named(saved, refs[:n])
    buf = named(saved, refs[n : 2 * n])
    g, sel, selt, sems, save_sems = refs[2 * n :]
    copies = []

    def save(*names):
        for name in names:
            copy = pltpu.make_async_copy(buf[name], out[name], save_sems.at[len(copies)])
            copy.start()
            copies.append(copy)

    build_selectors(sel, selt)
    fetch_halves(core[0], own, other, g, sems)
    ada = unpack(g, selt, buf)
    save("main", "bias", "bias2", "fc2")
    modulate(cond, g, selt, ada, buf["mod"])
    save("mod")
    forward(x, buf, buf["mod"], buf, y, save)
    for copy in copies:
        copy.wait()


def turn_kernel(core, own, other, x, cond, grad, y, dx, dc, keep, send, *refs):
    n_keep, n_w, n_t = len(KEEP), len(WEIGHTS), len(TEMPS)
    k = named(KEEP, refs[:n_keep])
    w = named(WEIGHTS, refs[n_keep : n_keep + n_w])
    t = named(TEMPS, refs[n_keep + n_w : n_keep + n_w + n_t])
    mod, g, sel, selt, pack, sems = refs[n_keep + n_w + n_t :]
    build_selectors(sel, selt)
    fetch_halves(core[0], own, other, g, sems)
    ada = unpack(g, selt, w)
    modulate(cond, g, selt, ada, mod)
    forward(x, w, mod, k, y)
    backward(core[0], grad, x, cond, g, G_ADA, sel, selt, w, mod, k, t, dx, dc, putter(core[0], pack), *sender(core[0], pack, keep, send, sems))


def back_kernel(core, own, other, x, cond, grad, *refs):
    n_keep, n_w, n_t = len(KEEP), len(WEIGHTS), len(TEMPS)
    k = named(KEEP, refs[:n_keep])
    w = named(WEIGHTS, refs[n_keep : n_keep + n_w])
    mod, dx, dc, keep, send = refs[n_keep + n_w : n_keep + n_w + 5]
    refs = refs[n_keep + n_w + 5 :]
    t = named(TEMPS, refs[:n_t])
    g, sel, selt, pack, sems = refs[n_t:]
    build_selectors(sel, selt)
    fetch_ada(core[0], own, other, g, sems)
    backward(core[0], grad, x, cond, g, 0, sel, selt, w, mod, k, t, dx, dc, putter(core[0], pack), *sender(core[0], pack, keep, send, sems))


VM = pl.BlockSpec(memory_space=pltpu.VMEM)
ANY = pl.BlockSpec(memory_space=pl.ANY)
SM = pl.BlockSpec(memory_space=pltpu.SMEM)
PARAMS = pltpu.CompilerParams(vmem_limit_bytes=60 * 1024 * 1024)
G_BUF = pltpu.VMEM((EXP, G_END), B)
ADA_BUF = pltpu.VMEM((EXP, G_BIAS - G_ADA), B)
SEL_BUFS = [pltpu.VMEM((4, EXP, D), B), pltpu.VMEM((4, D, EXP), B)]
SEMS = pltpu.SemaphoreType.DMA((5,))
ROWS_OUT = jax.ShapeDtypeStruct((ROWS, D), B)
COND_OUT = jax.ShapeDtypeStruct((8, D), F)
HALF_OUT = jax.ShapeDtypeStruct((EXP, P_HALF), B)
PACK_BUF = pltpu.VMEM((2, EXP, P_HALF), B)


def cost(units):
    return pl.CostEstimate(flops=units * 2_000_000_000, bytes_accessed=units * 10_000_000, transcendentals=units * 2_000_000)


def front(core, own, other, x, cond):
    outs = [ROWS_OUT] + shapes(KEEP) + shapes(WEIGHTS) + shapes(MOD)
    return pl.pallas_call(
        front_kernel,
        out_shape=outs,
        in_specs=[SM, ANY, ANY, VM, VM],
        out_specs=[VM] + [ANY] * (len(outs) - 1),
        scratch_shapes=buffers(KEEP + WEIGHTS + MOD)
        + [G_BUF, *SEL_BUFS, SEMS, pltpu.SemaphoreType.DMA((len(outs) - 1,))],
        compiler_params=PARAMS,
        cost_estimate=cost(1),
        name="front",
    )(core, own, other, x, cond)


def turn(core, own, other, x, cond, grad):
    return pl.pallas_call(
        turn_kernel,
        out_shape=[ROWS_OUT, ROWS_OUT, COND_OUT, HALF_OUT, HALF_OUT],
        in_specs=[SM, ANY, ANY, VM, VM, VM],
        out_specs=[VM] * 3 + [ANY] * 2,
        scratch_shapes=buffers(KEEP) + buffers(WEIGHTS) + buffers(TEMPS) + buffers(MOD) + [G_BUF, *SEL_BUFS, PACK_BUF, SEMS],
        compiler_params=PARAMS,
        cost_estimate=cost(3),
        name="turn",
    )(core, own, other, x, cond, grad)


def back(core, own, other, x, cond, grad, kept):
    return pl.pallas_call(
        back_kernel,
        out_shape=[ROWS_OUT, COND_OUT, HALF_OUT, HALF_OUT],
        in_specs=[SM, ANY, ANY, VM, VM, VM] + [VM] * len(kept),
        out_specs=[VM] * 2 + [ANY] * 2,
        scratch_shapes=buffers(TEMPS) + [ADA_BUF, *SEL_BUFS, PACK_BUF, SEMS],
        compiler_params=PARAMS,
        cost_estimate=cost(2),
        name="back",
    )(core, own, other, x, cond, grad, *kept)


def line_up_kernel(w_qkv, w_proj, w_fc1, w_fc2, w_ada, bias, out, main, ada):
    def rows(ref, first, last):
        return ref[:, first:last].astype(F)

    main[0:6, :] = rows(w_qkv, 0, QUARTER)
    main[6:12, :384] = rows(w_qkv, QUARTER, C_PROJ)
    main[6:12, 384:] = rows(w_proj, 0, D)
    main[12:18, :] = rows(w_fc1, 0, QUARTER)
    main[18:24, :] = rows(w_fc1, QUARTER, FF)
    ada[48:56, :] = jnp.zeros((8, 256), F)
    for i in range(9):
        ada[6 * i : 6 * i + 6, :] = rows(w_ada, 256 * i, 256 * i + 256)
    for a in range(3):
        out[:, a * QUARTER : (a + 1) * QUARTER] = main[8 * a : 8 * a + 8, :].astype(B)
        out[:, G_FC2 + a * D : G_FC2 + (a + 1) * D] = w_fc2[8 * a : 8 * a + 8, :]
    for a in range(7):
        out[:, G_ADA + a * 256 : G_ADA + (a + 1) * 256] = ada[8 * a : 8 * a + 8, :].astype(B)
    first = lax.broadcasted_iota(jnp.int32, (8, 1), 0) == 0
    out[:, G_BIAS:G_END] = jnp.where(first, bias[...].astype(F), 0.0).astype(B)


def line_up(w_qkv, b_qv, w_proj, b_proj, w_fc1, b_fc1, w_fc2, b_fc2, w_ada, b_ada):
    bias = jnp.concatenate([b_qv, b_proj, b_fc1, b_fc2, b_ada, jnp.zeros((44,), B)]).reshape(1, 128)
    return pl.pallas_call(
        line_up_kernel,
        out_shape=jax.ShapeDtypeStruct((8, G_END), B),
        in_specs=[VM] * 6,
        out_specs=VM,
        scratch_shapes=[pltpu.VMEM((24, QUARTER), F), pltpu.VMEM((56, 256), F)],
        name="line_up",
    )(w_qkv, w_proj, w_fc1, w_fc2, w_ada, bias)


def swap(x):
    return lax.ppermute(x, "pipe", [(0, 1), (1, 0)])


def to_all(blocks):
    copies = jnp.broadcast_to(blocks[None], (CHIPS, *blocks.shape))
    came = lax.all_to_all(copies, "shard", 0, 0, tiled=True)
    return [came[:, i].reshape(EXP, blocks.shape[2]) for i in range(2)]


def scatter(block):
    return lax.all_to_all(block.reshape(CHIPS, 8, P_HALF), "shard", 0, 0, tiled=True)


def shards(latents, conditions, cotangent, w_qkv, b_qv, w_proj, b_proj, w_fc1, b_fc1, w_fc2, b_fc2, w_ada, b_ada):
    p = lax.axis_index("pipe")
    j = lax.axis_index("shard")
    first = p == 0
    core = p.reshape(1).astype(jnp.int32)
    block = line_up(w_qkv[0], b_qv[0], w_proj[0], b_proj[0], w_fc1[0], b_fc1[0], w_fc2[0], b_fc2[0], w_ada[0], b_ada[0])
    block_other = swap(block)
    low = jnp.where(first, block[:, :G_HALF], block_other[:, G_HALF:])
    high = jnp.where(first, block_other[:, :G_HALF], block[:, G_HALF:])
    own0, own1 = to_all(jnp.stack([low, high]))
    other0 = swap(own0)
    other1 = swap(own1)
    x = lax.dynamic_index_in_dim(latents, p, 0, keepdims=False).reshape(ROWS, D)
    cot = lax.dynamic_index_in_dim(cotangent, p, 0, keepdims=False).reshape(ROWS, D)
    cond = lax.dynamic_index_in_dim(conditions, p, 0, keepdims=False).astype(F)
    cond = jnp.concatenate([cond, jnp.zeros((6, D), F)], axis=0)

    h, *kept = front(core, own0, other0, x, cond)
    y, dx1, dc1, keep1, send1 = turn(core, own1, other1, h, cond, cot)
    parts1 = scatter(keep1 + swap(send1))
    dx0, dc0, keep0, send0 = back(core, own0, other0, x, cond, dx1, kept)
    parts1, send0 = lax.optimization_barrier((parts1, send0))
    parts0 = scatter(keep0 + swap(send0))

    def pair(for_first, for_second):
        keep = jnp.where(first, for_first, for_second)
        came = swap(jnp.where(first, for_second, for_first))
        both = jnp.where(first, jnp.stack([keep, came]), jnp.stack([came, keep]))
        return both.reshape(1, 2, 2, SEQ, D)

    section_outputs = pair(h, y)
    input_grads = pair(dx0, dx1)
    dc = (dc0 + dc1)[:2]
    dc_other = swap(dc)
    cond_grad = jnp.where(first, jnp.stack([dc, dc_other]), jnp.stack([dc_other, dc]))

    def reduced(parts):
        lot = jnp.sum(parts.astype(F), axis=0)
        flat = parts.reshape(EXP, P_HALF)
        ada = lax.dot_general(
            flat[:, P_COND : P_COND + 16], flat[:, P_MOD:P_DB1], (((0,), (0,)), ((), ())), preferred_element_type=F
        )
        return jnp.concatenate([lot, ada[:8], ada[8:]], axis=1)

    lot0 = reduced(parts0)
    lot1 = reduced(parts1)
    kept_half = jnp.where(first, lot0, lot1)
    came_half = swap(jnp.where(first, lot1, lot0))
    low = jnp.where(first, kept_half, came_half)
    high = jnp.where(first, came_half, kept_half)

    rows = jnp.concatenate([low[:, a * QUARTER : (a + 1) * QUARTER] for a in range(3)], axis=0)
    quarters = [rows[6 * q : 6 * q + 6] for q in range(4)]
    db = jnp.concatenate([low[:, P_DB0 : P_DB0 + 128], low[:, P_DB0 + 128 : P_HALF], high[:, P_DB1:P_COND]], axis=0).reshape(-1)
    sums = high[:, P_MOD:P_DB1]
    db_ada = jnp.concatenate([sums[:4].sum(axis=0), sums[4:].sum(axis=0)])

    def slice_of(line, at, width):
        return lax.dynamic_slice(line, (at + width * j,), (width,))

    outs = (
        jnp.concatenate([quarters[0], quarters[1][:, :384]], axis=1),
        slice_of(db, 0, 12),
        quarters[1][:, 384:],
        slice_of(db, 768, 6),
        jnp.concatenate([quarters[2], quarters[3]], axis=1),
        slice_of(db, 1152, 24),
        jnp.concatenate([high[:, a * D : (a + 1) * D] for a in range(3)], axis=0),
        slice_of(db, 2688, 6),
        jnp.concatenate([high[:6, P_HALF : P_HALF + 1152], high[:6, P_HALF + 1152 :]], axis=1),
        slice_of(db_ada, 0, 36),
    )
    return (section_outputs, input_grads, cond_grad) + tuple(o[None] for o in outs)


def solution(mesh):
    rows = P(None, "shard", None, None)
    wide = P("pipe", "shard", None)
    thin = P("pipe", "shard")
    both = P("pipe", None, "shard", None, None)
    pairs = (wide, thin) * 5
    return jax.shard_map(
        shards,
        mesh=mesh,
        in_specs=(rows, P(None, "shard", None), rows) + pairs,
        out_specs=(both, both, P(None, "shard", None)) + pairs,
        check_vma=False,
    )
```

```python
import functools

import jax
import jax.numpy as jnp
from jax import lax
from jax.experimental import pallas as pl
from jax.experimental.pallas import tpu as pltpu
from jax.sharding import PartitionSpec as P

F = jnp.float32
B = jnp.bfloat16
D = 384
HEADS = 6
HEAD = 64
FF = 1536
SEQ = 256
EPS = 1e-06
CHIPS = 64
ROWS = 512
EXP = 512

C_QKV, C_PROJ, C_FC1, C_MAIN = 0, 1152, 1536, 3072
QUARTER = 768

G_FC2, G_ADA, G_BIAS, G_END = 2304, 3456, 5248, 5376
G_HALF = 2688
BIASES = ((0, 12), (12, 6), (18, 24), (42, 6), (48, 36))

P_HALF = 2560
P_DB0 = 2304
P_MOD, P_DB1, P_COND = 1152, 2304, 2432
SHIFTS = (0, 6, 4, 2)

K0 = 0.7978845608028654
K1 = 0.044715

UNROLL = 6
NN = (1, 0)
NT = (1, 1)
TN = (0, 0)


def dot(a, b, dims=NN):
    return lax.dot_general(a, b, (((dims[0],), (dims[1],)), ((), ())), preferred_element_type=F)


def targets(shape, dim, shift):
    at = lax.broadcasted_iota(jnp.int32, shape, dim)
    r = ((at & 7) + (8 - shift)) & 7
    return jnp.where(r < 6, (at >> 3) * 6 + r, -1)


def build_selectors(sel, selt):
    col = lax.broadcasted_iota(jnp.int32, (1, D), 1)
    row = lax.broadcasted_iota(jnp.int32, (D, 1), 0)
    for i, shift in enumerate(SHIFTS):
        sel[i] = (targets((EXP, 1), 0, shift) == col).astype(F).astype(B)
        selt[i] = (row == targets((1, EXP), 1, shift)).astype(F).astype(B)


def group_of(n, width):
    return jnp.floor((n.astype(F) + 0.5) * (1.0 / width)).astype(jnp.int32)


def natural_bias(gb, lane, width):
    n = CHIPS * width
    at = lax.broadcasted_iota(jnp.int32, (1, n), 1)
    owner = group_of(at, width)
    spot = at - owner * width + lane
    pick = (lax.broadcasted_iota(jnp.int32, (128, 1), 0) == spot).astype(F).astype(B)
    wide = dot(gb, pick)
    return jnp.sum(jnp.where(lax.broadcasted_iota(jnp.int32, (CHIPS, 1), 0) == owner, wide, 0.0), axis=0, keepdims=True)


def tile_row(shape, dim):
    return lax.broadcasted_iota(jnp.int32, shape, dim) & 7


def stats(v):
    centre = v - jnp.mean(v, axis=-1, keepdims=True)
    inv = lax.rsqrt(jnp.mean(centre * centre, axis=-1, keepdims=True) + EPS)
    return centre * inv, inv


def norm_back(g, n, inv):
    mg = jnp.mean(g, axis=-1, keepdims=True)
    mgn = jnp.mean(g * n, axis=-1, keepdims=True)
    return inv * (g - mg - n * mgn)


def head_masks():
    lane = lax.broadcasted_iota(jnp.int32, (1, 128), 1)
    low = (lane < HEAD).astype(F)
    return low.astype(B), (1.0 - low).astype(B)


def unpack(g, selt, w):
    r8 = tile_row((EXP, 1), 0)

    def piece(a, c):
        return g[:, a * QUARTER + c : a * QUARTER + c + 384]

    def merge(edge, a, c):
        return jnp.where(r8 >= edge, piece(a, c).astype(F), piece(a + 1, c).astype(F)).astype(B)

    for c in (0, 384):
        w["main"][:, c : c + 384] = dot(selt[0], piece(0, c)).astype(B)
        w["main"][:, QUARTER + c : QUARTER + c + 384] = dot(selt[1], merge(6, 0, c)).astype(B)
        w["main"][:, 2 * QUARTER + c : 2 * QUARTER + c + 384] = dot(selt[2], merge(4, 1, c)).astype(B)
        w["main"][:, 3 * QUARTER + c : 3 * QUARTER + c + 384] = dot(selt[3], piece(2, c)).astype(B)

    lead = (lax.broadcasted_iota(jnp.int32, (CHIPS, EXP), 0) * 8 == lax.broadcasted_iota(jnp.int32, (CHIPS, EXP), 1)).astype(F).astype(B)
    gb = dot(lead, g[:, G_BIAS:G_END]).astype(B)
    qv, proj, fc1, fc2, ada = (natural_bias(gb, lane, width) for lane, width in BIASES)
    w["bias"][:, :D] = qv[:, :D]
    w["bias"][:, D : 2 * D] = jnp.zeros((1, D), F)
    w["bias"][:, 2 * D : C_PROJ] = qv[:, D:]
    w["bias"][:, C_PROJ:C_FC1] = proj
    w["bias"][:, C_FC1:C_MAIN] = fc1
    w["bias2"][...] = fc2

    def step2(i, _):
        at = pl.multiple_of(i * 128, 128)
        parts = [g[pl.ds(at, 128), G_FC2 + a * D : G_FC2 + (a + 1) * D].astype(F).reshape(16, 8, D) for a in range(3)]
        whole = jnp.concatenate(parts, axis=1).reshape(D, D).astype(B)
        w["fc2"][pl.ds(pl.multiple_of(i * D, D), D), :] = whole
        return 0

    lax.fori_loop(0, 4, step2, 0)
    return ada


def ada_groups():
    return [(i % 4, (6 * i) // 8, SHIFTS[i % 4] in (6, 4)) for i in range(9)]


def modulate(cond, g, selt, ada, mod):
    c = cond[...]
    act = (c * jax.nn.sigmoid(c)).astype(B)
    r8 = tile_row((1, EXP), 1)
    wides = [dot(act, selt[i]) for i in range(4)]
    for n, (i, a, more) in enumerate(ada_groups()):
        at = G_ADA + a * 256
        first = jnp.where(r8 >= SHIFTS[i], wides[i], 0.0).astype(B)
        part = dot(first, g[:, at : at + 256])
        if more:
            part = part + dot(jnp.where(r8 < SHIFTS[i], wides[i], 0.0).astype(B), g[:, at + 256 : at + 512])
        mod[:, n * 256 : (n + 1) * 256] = part + ada[:, n * 256 : (n + 1) * 256]


def cond_back(dm, g, g_at, selt):
    r8 = tile_row((EXP, 1), 0)
    sums = [jnp.zeros((EXP, 8), F)] * 4
    for n, (i, a, more) in enumerate(ada_groups()):
        at = g_at + a * 256
        piece = dm[:, n * 256 : (n + 1) * 256]
        sums[i] = sums[i] + jnp.where(r8 >= SHIFTS[i], dot(g[:, at : at + 256], piece, NT), 0.0)
        if more:
            sums[i] = sums[i] + jnp.where(r8 < SHIFTS[i], dot(g[:, at + 256 : at + 512], piece, NT), 0.0)
    total = jnp.zeros((8, D), F)
    for i in range(4):
        rest = sums[i].T
        for _ in range(3):
            level = rest.astype(B)
            rest = rest - level.astype(F)
            total = total + dot(level, selt[i], NT)
    return total


def forward(x, w, mod, k, y, save=lambda *names: None):
    main, bias, fc2 = w["main"], w["bias"], w["fc2"]

    def ln_in(i, _):
        rows = pl.ds(pl.multiple_of(i * 128, 128), 128)
        lat = pl.ds(i // 2, 1)
        n, _ = stats(x[rows, :].astype(F))
        k["ain"][rows, :] = (n * (1.0 + mod[lat, D : 2 * D]) + mod[lat, :D]).astype(B)
        return 0

    lax.fori_loop(0, 4, ln_in, 0, unroll=True)

    for c in range(3):
        cs = slice(c * D, (c + 1) * D)
        k["qkv"][:, cs] = (dot(k["ain"][...], main[:, cs]) + bias[:, cs]).astype(B)

    low, high = head_masks()

    def attend(i, _):
        rows = pl.ds(pl.multiple_of((i // 3) * SEQ, SEQ), SEQ)
        at = (i % 3) * 128
        q = k["qkv"][rows, pl.ds(pl.multiple_of(at, 128), 128)]
        key = k["qkv"][rows, pl.ds(pl.multiple_of(D + at, 128), 128)]
        vt = k["qkv"][rows, pl.ds(pl.multiple_of(2 * D + at, 128), 128)].T
        heads = []
        for h, m in enumerate((low, high)):
            s = dot(key, q * (m * 0.125), NT)
            top = jnp.max(s, axis=0, keepdims=True)
            e = jnp.exp(s - top)
            t = jnp.sum(e, axis=0, keepdims=True)
            p = (e * (1.0 / t)).astype(B)
            k["lse"][i, h : h + 1, :] = top + jnp.log(t)
            heads.append(dot(vt[h * HEAD : (h + 1) * HEAD], p))
        k["att"][rows, pl.ds(pl.multiple_of(at, 128), 128)] = jnp.concatenate(heads, axis=0).T.astype(B)
        return 0

    lax.fori_loop(0, 6, attend, 0, unroll=UNROLL)
    save("ain", "qkv", "lse", "att")
    k["o"][...] = dot(k["att"][...], main[:, C_PROJ:C_FC1]) + bias[:, C_PROJ:C_FC1]

    def mid(i, _):
        rows = pl.ds(pl.multiple_of(i * 128, 128), 128)
        lat = pl.ds(i // 2, 1)
        x1 = x[rows, :].astype(F) + mod[lat, 2 * D : 3 * D] * k["o"][rows, :]
        k["x1"][rows, :] = x1
        n, _ = stats(x1)
        k["min"][rows, :] = (n * (1.0 + mod[lat, 4 * D : 5 * D]) + mod[lat, 3 * D : 4 * D]).astype(B)
        return 0

    lax.fori_loop(0, 4, mid, 0, unroll=True)

    def mlp(i, _):
        at = pl.multiple_of(i * 256, 256)
        cs = pl.ds(at, 256)
        ws = pl.ds(pl.multiple_of(C_FC1 + at, 256), 256)
        z = dot(k["min"][...], main[:, ws]) + bias[:, ws]
        zz = z * z
        t = jnp.tanh(z * (K0 + K0 * K1 * zz))
        half = 0.5 + 0.5 * t
        k["act"][:, cs] = (z * half).astype(B)
        k["slope"][:, cs] = half + (0.5 * z) * (1.0 - t * t) * (K0 + 3.0 * K0 * K1 * zz)
        return 0

    lax.fori_loop(0, 6, mlp, 0, unroll=True)

    save("o", "x1", "min", "slope", "act")
    k["f"][...] = dot(k["act"][...], fc2[...]) + w["bias2"][...]

    def out(i, _):
        rows = pl.ds(pl.multiple_of(i * 128, 128), 128)
        lat = pl.ds(i // 2, 1)
        y[rows, :] = (k["x1"][rows, :] + mod[lat, 5 * D : 6 * D] * k["f"][rows, :]).astype(B)
        return 0

    save("f")
    lax.fori_loop(0, 4, out, 0, unroll=True)


def token_sum(v):
    return jnp.sum(v, axis=0, keepdims=True)


def spread(sel, i, v):
    return dot(sel[i], v, NT).astype(B)


def backward(core, grad, x, cond, g, g_at, sel, selt, w, mod, k, t, dx, dc, put, ship, finish):
    main, fc2 = w["main"], w["fc2"]
    dmod = t["dmod"]
    dmod[...] = jnp.zeros_like(dmod)

    def add_mod(lat, piece, v):
        cs = slice(piece * D, (piece + 1) * D)
        dmod[lat, cs] = dmod[lat, cs] + v

    t["db"][...] = jnp.zeros_like(t["db"])
    r8 = tile_row((EXP, 1), 0)

    def add_db(at, v):
        t["db"][:, at : at + v.shape[1]] = t["db"][:, at : at + v.shape[1]] + v


    def start(i, _):
        rows = pl.ds(pl.multiple_of(i * 128, 128), 128)
        lat = pl.ds(i // 2, 1)
        gr = grad[rows, :].astype(F)
        df = (gr * mod[lat, 5 * D : 6 * D]).astype(B)
        t["df"][rows, :] = df
        add_mod(lat, 5, token_sum(gr * k["f"][rows, :]))
        add_db(2688, token_sum(df.astype(F)))
        return 0

    lax.fori_loop(0, 4, start, 0, unroll=True)

    def dmlp(i, _):
        cs = pl.ds(pl.multiple_of(i * 256, 256), 256)
        da = dot(t["df"][...], fc2[cs, :], NT)
        dz = (da * k["slope"][:, cs]).astype(B)
        t["dz"][:, cs] = dz
        ds = pl.ds(pl.multiple_of(1152 + i * 256, 128), 256)
        t["db"][:, ds] = token_sum(dz.astype(F))
        return 0

    lax.fori_loop(0, 6, dmlp, 0, unroll=True)

    t["wide2"][...] = spread(sel, 2, k["min"][...])
    t["wide"][...] = spread(sel, 3, k["min"][...])
    for c in range(0, QUARTER, 256):
        d2 = dot(t["wide2"][...], t["dz"][:, c : c + 256])
        d3 = dot(t["wide"][...], t["dz"][:, QUARTER + c : QUARTER + c + 256])
        put(0, slice(0, EXP), slice(2 * QUARTER + c, 2 * QUARTER + c + 256), jnp.where(r8 < 2, d2, d3).astype(B))
        t["part"][:, c : c + 256] = d2

    for c in range(4):
        part = dot(k["act"][:, c * D : (c + 1) * D], t["df"][...], TN).reshape(16, 24, D)
        for a in range(3):
            put(
                1,
                slice(c * 128, (c + 1) * 128),
                slice(a * D, (a + 1) * D),
                part[:, 8 * a : 8 * a + 8, :].reshape(128, D).astype(B),
            )

    t["dn"][...] = dot(t["dz"][...], main[:, C_FC1:C_MAIN], NT)

    def dmid(i, _):
        rows = pl.ds(pl.multiple_of(i * 128, 128), 128)
        lat = pl.ds(i // 2, 1)
        dmin = t["dn"][rows, :]
        n, inv = stats(k["x1"][rows, :])
        add_mod(lat, 4, token_sum(dmin * n))
        add_mod(lat, 3, token_sum(dmin))
        d1 = grad[rows, :].astype(F) + norm_back(dmin * (1.0 + mod[lat, 4 * D : 5 * D]), n, inv)
        t["dx1"][rows, :] = d1
        do = (d1 * mod[lat, 2 * D : 3 * D]).astype(B)
        add_mod(lat, 2, token_sum(d1 * k["o"][rows, :]))
        t["df"][rows, :] = do
        add_db(768, token_sum(do.astype(F)))
        return 0

    lax.fori_loop(0, 4, dmid, 0, unroll=True)
    t["datt"][...] = dot(t["df"][...], main[:, C_PROJ:C_FC1], NT).astype(B)

    t["wide2"][...] = spread(sel, 1, k["att"][...])
    d1 = dot(t["wide2"][...], t["df"][...])
    put(0, slice(0, EXP), slice(QUARTER + 384, 2 * QUARTER), jnp.where(r8 < 4, d1, t["part"][:, 384:]).astype(B))
    t["part2"][...] = d1

    low, high = head_masks()

    def dattend(i, _):
        rows = pl.ds(pl.multiple_of((i // 3) * SEQ, SEQ), SEQ)
        at = (i % 3) * 128
        qs = pl.ds(pl.multiple_of(at, 128), 128)
        ks = pl.ds(pl.multiple_of(D + at, 128), 128)
        vs = pl.ds(pl.multiple_of(2 * D + at, 128), 128)
        q = k["qkv"][rows, qs]
        key = k["qkv"][rows, ks]
        v = k["qkv"][rows, vs]
        da = t["datt"][rows, qs]
        kt = key.T
        dk = dv = None
        dqs = []
        for h, m in enumerate((low, high)):
            qm = q * (m * 0.125)
            dam = da * m
            s = dot(key, qm, NT)
            p = jnp.exp(s - k["lse"][i, h : h + 1, :])
            dp = dot(v, dam, NT)
            ds = (p * (dp - jnp.sum(p * dp, axis=0, keepdims=True))).astype(B)
            v1 = dot(p.astype(B), dam)
            k1 = dot(ds, qm)
            dqs.append(dot(kt[h * HEAD : (h + 1) * HEAD], ds))
            dv = v1 if dv is None else dv + v1
            dk = k1 if dk is None else dk + k1
        t["dqkv"][rows, qs] = (jnp.concatenate(dqs, axis=0).T * 0.125).astype(B)
        t["dqkv"][rows, ks] = dk.astype(B)
        t["dqkv"][rows, vs] = dv.astype(B)
        return 0

    lax.fori_loop(0, 6, dattend, 0, unroll=UNROLL)

    t["wide"][...] = spread(sel, 0, k["ain"][...])
    t["wide2"][...] = spread(sel, 1, k["ain"][...])
    d1 = dot(t["wide2"][...], t["dqkv"][:, QUARTER:])
    d0 = dot(t["wide"][...], t["dqkv"][:, :384])
    put(0, slice(0, EXP), slice(0, 384), jnp.where(r8 < 6, d0, d1).astype(B))
    put(0, slice(0, EXP), slice(QUARTER, QUARTER + 384), jnp.where(r8 < 4, d1, t["part"][:, :384]).astype(B))
    d0 = dot(t["wide"][...], t["dqkv"][:, 384:QUARTER])
    put(0, slice(0, EXP), slice(384, QUARTER), jnp.where(r8 < 6, d0, t["part2"][...]).astype(B))
    ship(0, 0, P_DB0)
    ship(1, 0, P_MOD)

    def bias_sums(i, _):
        rows = pl.ds(pl.multiple_of(i * 128, 128), 128)
        add_db(0, token_sum(t["dqkv"][rows, :D].astype(F)))
        add_db(D, token_sum(t["dqkv"][rows, 2 * D :].astype(F)))
        return 0

    lax.fori_loop(0, 4, bias_sums, 0, unroll=True)

    t["dn"][...] = dot(t["dqkv"][...], main[:, C_QKV:C_PROJ], NT)

    def dlast(i, _):
        rows = pl.ds(pl.multiple_of(i * 128, 128), 128)
        lat = pl.ds(i // 2, 1)
        dain = t["dn"][rows, :]
        n, inv = stats(x[rows, :].astype(F))
        add_mod(lat, 1, token_sum(dain * n))
        add_mod(lat, 0, token_sum(dain))
        back = norm_back(dain * (1.0 + mod[lat, D : 2 * D]), n, inv)
        dx[rows, :] = (t["dx1"][rows, :] + back).astype(B)
        return 0

    lax.fori_loop(0, 4, dlast, 0, unroll=True)

    c = cond[...]
    sig = jax.nn.sigmoid(c)
    act = c * sig
    dm = dmod[...].astype(B).astype(F)
    dc[...] = cond_back(dm.astype(B), g, g_at, selt) * (sig * (1.0 + c * (1.0 - sig)))

    mine = 2 * core
    block = pltpu.roll(dm[:, :1152], mine, 0) + pltpu.roll(dm[:, 1152:], mine + 4, 0)
    for q in range(4):
        rows = slice(q * 128, (q + 1) * 128)
        put(1, rows, slice(P_MOD, P_DB1), jnp.broadcast_to(block[None], (16, 8, 1152)).reshape(128, 1152).astype(B))

    db = t["db"]
    for half, at, first in ((0, P_DB0, 0), (0, P_DB0 + 128, 8), (1, P_DB1, 16)):
        rows = jnp.concatenate([db[:, (first + i) * 128 : (first + i + 1) * 128] for i in range(8)], axis=0)
        put(half, slice(0, EXP), slice(at, at + 128), jnp.broadcast_to(rows[None], (CHIPS, 8, 128)).reshape(EXP, 128).astype(B))

    act = act.astype(B).astype(F)
    both = pltpu.roll(act, mine, 0) + pltpu.roll(act, mine + 4, 0)
    both = jnp.broadcast_to(both[None], (CHIPS, 8, D)).reshape(EXP, D)
    feature = lax.broadcasted_iota(jnp.int32, (1, D), 1)
    device = lax.broadcasted_iota(jnp.int32, (EXP, 1), 0) >> 3
    both = jnp.where(group_of(feature, 6) == device, both, 0.0).astype(B)
    feature = lax.broadcasted_iota(jnp.int32, (D, 1), 0)
    lane = lax.broadcasted_iota(jnp.int32, (1, 128), 1)
    pick = ((feature - 6 * group_of(feature, 6)) == (lane & 7)) & (lane < 16)
    found = dot(both, pick.astype(F).astype(B))
    put(1, slice(0, EXP), slice(P_COND, P_HALF), jnp.where((r8 >> 2) == (lane >> 3), found, 0.0).astype(B))
    ship(0, P_DB0, P_HALF)
    ship(1, P_MOD, P_HALF)
    finish()


KEEP = (
    ("ain", (ROWS, D), B),
    ("qkv", (ROWS, 3 * D), B),
    ("lse", (6, 8, SEQ), F),
    ("att", (ROWS, D), B),
    ("o", (ROWS, D), F),
    ("x1", (ROWS, D), F),
    ("min", (ROWS, D), B),
    ("slope", (ROWS, FF), F),
    ("act", (ROWS, FF), B),
    ("f", (ROWS, D), F),
)
WEIGHTS = (("main", (D, C_MAIN), B), ("bias", (1, C_MAIN), F), ("bias2", (1, D), F), ("fc2", (FF, D), B))
TEMPS = (
    ("dmod", (8, 6 * D), F),
    ("db", (1, 3072), F),
    ("part", (EXP, QUARTER), F),
    ("part2", (EXP, D), F),
    ("wide2", (EXP, ROWS), B),
    ("df", (ROWS, D), B),
    ("dz", (ROWS, FF), B),
    ("wide", (EXP, ROWS), B),
    ("dx1", (ROWS, D), F),
    ("dn", (ROWS, D), F),
    ("datt", (ROWS, D), B),
    ("dqkv", (ROWS, 3 * D), B),
)
MOD = (("mod", (8, 6 * D), F),)


def buffers(table):
    return [pltpu.VMEM(shape, dtype) for _, shape, dtype in table]


def shapes(table):
    return [jax.ShapeDtypeStruct(shape, dtype) for _, shape, dtype in table]


def named(table, refs):
    return {name: ref for (name, _, _), ref in zip(table, refs)}


def fetch_halves(core, own, other, g, sems):
    def go(low, high):
        copies = [
            pltpu.make_async_copy(low, g.at[:, :G_HALF], sems.at[0]),
            pltpu.make_async_copy(high, g.at[:, G_HALF:], sems.at[1]),
        ]
        for copy in copies:
            copy.start()
        for copy in copies:
            copy.wait()

    @pl.when(core == 0)
    def _():
        go(own, other)

    @pl.when(core != 0)
    def _():
        go(other, own)


def fetch_ada(core, own, other, g, sems):
    def go(high):
        copy = pltpu.make_async_copy(high.at[:, G_ADA - G_HALF : G_BIAS - G_HALF], g, sems.at[0])
        copy.start()
        copy.wait()

    @pl.when(core == 0)
    def _():
        go(other)

    @pl.when(core != 0)
    def _():
        go(own)


def sender(core, pack, keep, send, sems):
    started = []

    def start(half, first, last):
        n = len(started)
        cols = slice(first, last)

        def copy(slot, ref):
            return pltpu.make_async_copy(pack.at[slot, :, cols], ref.at[:, cols], sems.at[n])

        mine = copy(0, keep)
        theirs = copy(1, send)
        started.append((half, mine, theirs))

        @pl.when(core == half)
        def _():
            mine.start()

        @pl.when(core != half)
        def _():
            theirs.start()

    def finish():
        for half, mine, theirs in started:

            @pl.when(core == half)
            def _(mine=mine):
                mine.wait()

            @pl.when(core != half)
            def _(theirs=theirs):
                theirs.wait()

    return start, finish


def putter(core, pack):
    def put(half, rows, cols, value):
        slot = core if half == 0 else 1 - core
        pack[slot, rows, cols] = value

    return put


def front_kernel(core, own, other, x, cond, y, *refs):
    saved = KEEP + WEIGHTS + MOD
    n = len(saved)
    out = named(saved, refs[:n])
    buf = named(saved, refs[n : 2 * n])
    g, sel, selt, sems, save_sems = refs[2 * n :]
    copies = []

    def save(*names):
        for name in names:
            copy = pltpu.make_async_copy(buf[name], out[name], save_sems.at[len(copies)])
            copy.start()
            copies.append(copy)

    build_selectors(sel, selt)
    fetch_halves(core[0], own, other, g, sems)
    ada = unpack(g, selt, buf)
    save("main", "bias", "bias2", "fc2")
    modulate(cond, g, selt, ada, buf["mod"])
    save("mod")
    forward(x, buf, buf["mod"], buf, y, save)
    for copy in copies:
        copy.wait()


def turn_kernel(core, own, other, x, cond, grad, y, dx, dc, keep, send, *refs):
    n_keep, n_w, n_t = len(KEEP), len(WEIGHTS), len(TEMPS)
    k = named(KEEP, refs[:n_keep])
    w = named(WEIGHTS, refs[n_keep : n_keep + n_w])
    t = named(TEMPS, refs[n_keep + n_w : n_keep + n_w + n_t])
    mod, g, sel, selt, pack, sems = refs[n_keep + n_w + n_t :]
    build_selectors(sel, selt)
    fetch_halves(core[0], own, other, g, sems)
    ada = unpack(g, selt, w)
    modulate(cond, g, selt, ada, mod)
    forward(x, w, mod, k, y)
    backward(core[0], grad, x, cond, g, G_ADA, sel, selt, w, mod, k, t, dx, dc, putter(core[0], pack), *sender(core[0], pack, keep, send, sems))


def back_kernel(core, own, other, x, cond, grad, *refs):
    n_keep, n_w, n_t = len(KEEP), len(WEIGHTS), len(TEMPS)
    k = named(KEEP, refs[:n_keep])
    w = named(WEIGHTS, refs[n_keep : n_keep + n_w])
    mod, dx, dc, keep, send = refs[n_keep + n_w : n_keep + n_w + 5]
    refs = refs[n_keep + n_w + 5 :]
    t = named(TEMPS, refs[:n_t])
    g, sel, selt, pack, sems = refs[n_t:]
    build_selectors(sel, selt)
    fetch_ada(core[0], own, other, g, sems)
    backward(core[0], grad, x, cond, g, 0, sel, selt, w, mod, k, t, dx, dc, putter(core[0], pack), *sender(core[0], pack, keep, send, sems))


VM = pl.BlockSpec(memory_space=pltpu.VMEM)
ANY = pl.BlockSpec(memory_space=pl.ANY)
SM = pl.BlockSpec(memory_space=pltpu.SMEM)
PARAMS = pltpu.CompilerParams(vmem_limit_bytes=60 * 1024 * 1024)
G_BUF = pltpu.VMEM((EXP, G_END), B)
ADA_BUF = pltpu.VMEM((EXP, G_BIAS - G_ADA), B)
SEL_BUFS = [pltpu.VMEM((4, EXP, D), B), pltpu.VMEM((4, D, EXP), B)]
SEMS = pltpu.SemaphoreType.DMA((5,))
ROWS_OUT = jax.ShapeDtypeStruct((ROWS, D), B)
COND_OUT = jax.ShapeDtypeStruct((8, D), F)
HALF_OUT = jax.ShapeDtypeStruct((EXP, P_HALF), B)
PACK_BUF = pltpu.VMEM((2, EXP, P_HALF), B)


def cost(units):
    return pl.CostEstimate(flops=units * 2_000_000_000, bytes_accessed=units * 10_000_000, transcendentals=units * 2_000_000)


def front(core, own, other, x, cond):
    outs = [ROWS_OUT] + shapes(KEEP) + shapes(WEIGHTS) + shapes(MOD)
    return pl.pallas_call(
        front_kernel,
        out_shape=outs,
        in_specs=[SM, ANY, ANY, VM, VM],
        out_specs=[VM] + [ANY] * (len(outs) - 1),
        scratch_shapes=buffers(KEEP + WEIGHTS + MOD)
        + [G_BUF, *SEL_BUFS, SEMS, pltpu.SemaphoreType.DMA((len(outs) - 1,))],
        compiler_params=PARAMS,
        cost_estimate=cost(1),
        name="front",
    )(core, own, other, x, cond)


def turn(core, own, other, x, cond, grad):
    return pl.pallas_call(
        turn_kernel,
        out_shape=[ROWS_OUT, ROWS_OUT, COND_OUT, HALF_OUT, HALF_OUT],
        in_specs=[SM, ANY, ANY, VM, VM, VM],
        out_specs=[VM] * 3 + [ANY] * 2,
        scratch_shapes=buffers(KEEP) + buffers(WEIGHTS) + buffers(TEMPS) + buffers(MOD) + [G_BUF, *SEL_BUFS, PACK_BUF, SEMS],
        compiler_params=PARAMS,
        cost_estimate=cost(3),
        name="turn",
    )(core, own, other, x, cond, grad)


def back(core, own, other, x, cond, grad, kept):
    return pl.pallas_call(
        back_kernel,
        out_shape=[ROWS_OUT, COND_OUT, HALF_OUT, HALF_OUT],
        in_specs=[SM, ANY, ANY, VM, VM, VM] + [VM] * len(kept),
        out_specs=[VM] * 2 + [ANY] * 2,
        scratch_shapes=buffers(TEMPS) + [ADA_BUF, *SEL_BUFS, PACK_BUF, SEMS],
        compiler_params=PARAMS,
        cost_estimate=cost(2),
        name="back",
    )(core, own, other, x, cond, grad, *kept)


def line_up_kernel(w_qkv, w_proj, w_fc1, w_fc2, w_ada, b_qv, b_proj, b_fc1, b_fc2, b_ada, out, main, ada, bias):
    def rows(ref, first, last):
        return ref[:, first:last].astype(F)

    main[0:6, :] = rows(w_qkv, 0, QUARTER)
    main[6:12, :384] = rows(w_qkv, QUARTER, C_PROJ)
    main[6:12, 384:] = rows(w_proj, 0, D)
    main[12:18, :] = rows(w_fc1, 0, QUARTER)
    main[18:24, :] = rows(w_fc1, QUARTER, FF)
    ada[48:56, :] = jnp.zeros((8, 256), F)
    for i in range(9):
        ada[6 * i : 6 * i + 6, :] = rows(w_ada, 256 * i, 256 * i + 256)
    for a in range(3):
        out[:, a * QUARTER : (a + 1) * QUARTER] = main[8 * a : 8 * a + 8, :].astype(B)
        out[:, G_FC2 + a * D : G_FC2 + (a + 1) * D] = w_fc2[8 * a : 8 * a + 8, :]
    for a in range(7):
        out[:, G_ADA + a * 256 : G_ADA + (a + 1) * 256] = ada[8 * a : 8 * a + 8, :].astype(B)
    bias[...] = jnp.zeros((8, 128), F)
    for ref, (lane, width) in zip((b_qv, b_proj, b_fc1, b_fc2, b_ada), BIASES):
        bias[0:1, lane : lane + width] = ref[...].astype(F)
    out[:, G_BIAS:G_END] = bias[...].astype(B)


def line_up(w_qkv, b_qv, w_proj, b_proj, w_fc1, b_fc1, w_fc2, b_fc2, w_ada, b_ada):
    biases = [b.reshape(1, -1) for b in (b_qv, b_proj, b_fc1, b_fc2, b_ada)]
    return pl.pallas_call(
        line_up_kernel,
        out_shape=jax.ShapeDtypeStruct((8, G_END), B),
        in_specs=[VM] * 10,
        out_specs=VM,
        scratch_shapes=[pltpu.VMEM((24, QUARTER), F), pltpu.VMEM((56, 256), F), pltpu.VMEM((8, 128), F)],
        name="line_up",
    )(w_qkv, w_proj, w_fc1, w_fc2, w_ada, *biases)


def swap(x):
    return lax.ppermute(x, "pipe", [(0, 1), (1, 0)])


def to_all(block):
    copies = jnp.broadcast_to(block[None], (CHIPS, *block.shape))
    return lax.all_to_all(copies, "shard", 0, 0, tiled=True).reshape(EXP, block.shape[1])


def scatter(block):
    return lax.all_to_all(block.reshape(CHIPS, 8, P_HALF), "shard", 0, 0, tiled=True)


def shards(latents, conditions, cotangent, w_qkv, b_qv, w_proj, b_proj, w_fc1, b_fc1, w_fc2, b_fc2, w_ada, b_ada):
    p = lax.axis_index("pipe")
    j = lax.axis_index("shard")
    first = p == 0
    core = p.reshape(1).astype(jnp.int32)
    block = line_up(w_qkv[0], b_qv[0], w_proj[0], b_proj[0], w_fc1[0], b_fc1[0], w_fc2[0], b_fc2[0], w_ada[0], b_ada[0])
    block_other = swap(block)
    low = jnp.where(first, block[:, :G_HALF], block_other[:, G_HALF:])
    high = jnp.where(first, block_other[:, :G_HALF], block[:, G_HALF:])
    own0 = to_all(low)
    other0 = swap(own0)
    high, own0 = lax.optimization_barrier((high, own0))
    own1 = to_all(high)
    x = lax.dynamic_index_in_dim(latents, p, 0, keepdims=False).reshape(ROWS, D)
    cot = lax.dynamic_index_in_dim(cotangent, p, 0, keepdims=False).reshape(ROWS, D)
    cond = lax.dynamic_index_in_dim(conditions, p, 0, keepdims=False).astype(F)
    cond = jnp.concatenate([cond, jnp.zeros((6, D), F)], axis=0)

    h, *kept = front(core, own0, other0, x, cond)
    h, own1 = lax.optimization_barrier((h, own1))
    other1 = swap(own1)
    y, dx1, dc1, keep1, send1 = turn(core, own1, other1, h, cond, cot)
    parts1 = scatter(keep1 + swap(send1))
    dx0, dc0, keep0, send0 = back(core, own0, other0, x, cond, dx1, kept)
    parts1, send0 = lax.optimization_barrier((parts1, send0))
    parts0 = scatter(keep0 + swap(send0))

    def pair(for_first, for_second):
        keep = jnp.where(first, for_first, for_second)
        came = swap(jnp.where(first, for_second, for_first))
        both = jnp.where(first, jnp.stack([keep, came]), jnp.stack([came, keep]))
        return both.reshape(1, 2, 2, SEQ, D)

    section_outputs = pair(h, y)
    input_grads = pair(dx0, dx1)
    dc = (dc0 + dc1)[:2]
    dc_other = swap(dc)
    cond_grad = jnp.where(first, jnp.stack([dc, dc_other]), jnp.stack([dc_other, dc]))

    parts0, section_outputs, input_grads, cond_grad = lax.optimization_barrier(
        (parts0, section_outputs, input_grads, cond_grad)
    )

    def reduced(parts):
        lot = jnp.sum(parts.astype(F), axis=0)
        flat = parts.reshape(EXP, P_HALF)
        ada = lax.dot_general(
            flat[:, P_COND : P_COND + 16], flat[:, P_MOD:P_DB1], (((0,), (0,)), ((), ())), preferred_element_type=F
        )
        return jnp.concatenate([lot, ada[:8], ada[8:]], axis=1)

    lot0 = reduced(parts0)
    lot1 = reduced(parts1)
    kept_half = jnp.where(first, lot0, lot1)
    came_half = swap(jnp.where(first, lot1, lot0))
    low = jnp.where(first, kept_half, came_half)
    high = jnp.where(first, came_half, kept_half)

    rows = jnp.concatenate([low[:, a * QUARTER : (a + 1) * QUARTER] for a in range(3)], axis=0)
    quarters = [rows[6 * q : 6 * q + 6] for q in range(4)]
    db = jnp.concatenate([low[:, P_DB0 : P_DB0 + 128], low[:, P_DB0 + 128 : P_HALF], high[:, P_DB1:P_COND]], axis=0).reshape(-1)
    sums = high[:, P_MOD:P_DB1]
    db_ada = jnp.concatenate([sums[:4].sum(axis=0), sums[4:].sum(axis=0)])

    def slice_of(line, at, width):
        return lax.dynamic_slice(line, (at + width * j,), (width,))

    outs = (
        jnp.concatenate([quarters[0], quarters[1][:, :384]], axis=1),
        slice_of(db, 0, 12),
        quarters[1][:, 384:],
        slice_of(db, 768, 6),
        jnp.concatenate([quarters[2], quarters[3]], axis=1),
        slice_of(db, 1152, 24),
        jnp.concatenate([high[:, a * D : (a + 1) * D] for a in range(3)], axis=0),
        slice_of(db, 2688, 6),
        jnp.concatenate([high[:6, P_HALF : P_HALF + 1152], high[:6, P_HALF + 1152 :]], axis=1),
        slice_of(db_ada, 0, 36),
    )
    return (section_outputs, input_grads, cond_grad) + tuple(o[None] for o in outs)


def solution(mesh):
    rows = P(None, "shard", None, None)
    wide = P("pipe", "shard", None)
    thin = P("pipe", "shard")
    both = P("pipe", None, "shard", None, None)
    pairs = (wide, thin) * 5
    return jax.shard_map(
        shards,
        mesh=mesh,
        in_specs=(rows, P(None, "shard", None), rows) + pairs,
        out_specs=(both, both, P(None, "shard", None)) + pairs,
        check_vma=False,
    )
```

```python
import functools

import jax
import jax.numpy as jnp
from jax import lax
from jax.experimental import pallas as pl
from jax.experimental.pallas import tpu as pltpu
from jax.sharding import PartitionSpec as P

F = jnp.float32
B = jnp.bfloat16
D = 384
HEADS = 6
HEAD = 64
FF = 1536
SEQ = 256
EPS = 1e-06
CHIPS = 64
ROWS = 512
EXP = 512

C_QKV, C_PROJ, C_FC1, C_MAIN = 0, 1152, 1536, 3072
QUARTER = 768

G_FC2, G_ADA, G_BIAS, G_END = 2304, 3456, 5248, 5376
G_HALF = 2688
BIASES = ((0, 12), (12, 6), (18, 24), (42, 6), (48, 36))

P_HALF = 2560
P_DB0 = 2304
P_MOD, P_DB1, P_COND = 1152, 2304, 2432
SHIFTS = (0, 6, 4, 2)

K0 = 0.7978845608028654
K1 = 0.044715

UNROLL = 6
NN = (1, 0)
NT = (1, 1)
TN = (0, 0)


def dot(a, b, dims=NN):
    return lax.dot_general(a, b, (((dims[0],), (dims[1],)), ((), ())), preferred_element_type=F)


STRIDES = {"y": 16, "x": 4, "z": 1}
STAGES = (("x", "y", "z"), ("y", "z", "x"))


def owner(block, place, core):
    total = 0
    for stage, axis in enumerate(STAGES[core]):
        here = place[1 + "yxz".index(axis)]
        behind = (block >> (2 * stage)) & 3
        total = total + STRIDES[axis] * ((here - behind) & 3)
    return total


def targets(shape, dim, shift, owner_of):
    at = lax.broadcasted_iota(jnp.int32, shape, dim)
    r = ((at & 7) + (8 - shift)) & 7
    return jnp.where(r < 6, owner_of(at >> 3) * 6 + r, -1)


def send_selectors(sel):
    col = lax.broadcasted_iota(jnp.int32, (1, D), 1)
    for i, shift in enumerate(SHIFTS):
        sel[i] = (targets((EXP, 1), 0, shift, lambda block: block) == col).astype(F).astype(B)


def gather_selectors(selt, place, core):
    row = lax.broadcasted_iota(jnp.int32, (D, 1), 0)
    for i, shift in enumerate(SHIFTS):
        found = targets((1, EXP), 1, shift, lambda block: owner(block, place, core))
        selt[i] = (row == found).astype(F).astype(B)


def row_order(place, core):
    at = lax.broadcasted_iota(jnp.int32, (1, EXP), 1)
    found = owner(at >> 3, place, core) * 8 + (at & 7)
    return (lax.broadcasted_iota(jnp.int32, (EXP, 1), 0) == found).astype(F).astype(B)


def group_of(n, width):
    return jnp.floor((n.astype(F) + 0.5) * (1.0 / width)).astype(jnp.int32)


def natural_bias(gb, lane, width):
    n = CHIPS * width
    at = lax.broadcasted_iota(jnp.int32, (1, n), 1)
    owner = group_of(at, width)
    spot = at - owner * width + lane
    pick = (lax.broadcasted_iota(jnp.int32, (128, 1), 0) == spot).astype(F).astype(B)
    wide = dot(gb, pick)
    return jnp.sum(jnp.where(lax.broadcasted_iota(jnp.int32, (CHIPS, 1), 0) == owner, wide, 0.0), axis=0, keepdims=True)


def tile_row(shape, dim):
    return lax.broadcasted_iota(jnp.int32, shape, dim) & 7


def stats(v):
    centre = v - jnp.mean(v, axis=-1, keepdims=True)
    inv = lax.rsqrt(jnp.mean(centre * centre, axis=-1, keepdims=True) + EPS)
    return centre * inv, inv


def norm_back(g, n, inv):
    mg = jnp.mean(g, axis=-1, keepdims=True)
    mgn = jnp.mean(g * n, axis=-1, keepdims=True)
    return inv * (g - mg - n * mgn)


def head_masks():
    lane = lax.broadcasted_iota(jnp.int32, (1, 128), 1)
    low = (lane < HEAD).astype(F)
    return low.astype(B), (1.0 - low).astype(B)


def unpack(g, selt, place, order, w):
    r8 = tile_row((EXP, 1), 0)

    def piece(a, c):
        return g[:, a * QUARTER + c : a * QUARTER + c + 384]

    def merge(edge, a, c):
        return jnp.where(r8 >= edge, piece(a, c).astype(F), piece(a + 1, c).astype(F)).astype(B)

    for c in (0, 384):
        w["main"][:, c : c + 384] = dot(selt[0], piece(0, c)).astype(B)
        w["main"][:, QUARTER + c : QUARTER + c + 384] = dot(selt[1], merge(6, 0, c)).astype(B)
        w["main"][:, 2 * QUARTER + c : 2 * QUARTER + c + 384] = dot(selt[2], merge(4, 1, c)).astype(B)
        w["main"][:, 3 * QUARTER + c : 3 * QUARTER + c + 384] = dot(selt[3], piece(2, c)).astype(B)

    lane = lax.broadcasted_iota(jnp.int32, (1, EXP), 1)
    from_device = jnp.where((lane & 7) == 0, owner(lane >> 3, place, 1), -1)
    lead = (lax.broadcasted_iota(jnp.int32, (CHIPS, 1), 0) == from_device).astype(F).astype(B)
    gb = dot(lead, g[:, G_BIAS:G_END]).astype(B)
    qv, proj, fc1, fc2, ada = (natural_bias(gb, lane, width) for lane, width in BIASES)
    w["bias"][:, :D] = qv[:, :D]
    w["bias"][:, D : 2 * D] = jnp.zeros((1, D), F)
    w["bias"][:, 2 * D : C_PROJ] = qv[:, D:]
    w["bias"][:, C_PROJ:C_FC1] = proj
    w["bias"][:, C_FC1:C_MAIN] = fc1
    w["bias2"][...] = fc2

    for core in range(2):
        order[core] = row_order(place, core)
    for i in range(4):
        rows = slice(i * 128, (i + 1) * 128)
        parts = [
            dot(order[min(a, 1), rows], g[:, G_FC2 + a * D : G_FC2 + (a + 1) * D]).reshape(16, 8, D) for a in range(3)
        ]
        w["fc2"][i * D : (i + 1) * D, :] = jnp.concatenate(parts, axis=1).reshape(D, D).astype(B)
    return ada


def ada_groups():
    return [(i % 4, (6 * i) // 8, SHIFTS[i % 4] in (6, 4)) for i in range(9)]


def modulate(cond, g, selt, ada, mod):
    c = cond[...]
    act = (c * jax.nn.sigmoid(c)).astype(B)
    r8 = tile_row((1, EXP), 1)
    wides = [dot(act, selt[i]) for i in range(4)]
    for n, (i, a, more) in enumerate(ada_groups()):
        at = G_ADA + a * 256
        first = jnp.where(r8 >= SHIFTS[i], wides[i], 0.0).astype(B)
        part = dot(first, g[:, at : at + 256])
        if more:
            part = part + dot(jnp.where(r8 < SHIFTS[i], wides[i], 0.0).astype(B), g[:, at + 256 : at + 512])
        mod[:, n * 256 : (n + 1) * 256] = part + ada[:, n * 256 : (n + 1) * 256]


def cond_back(dm, g, g_at, selt):
    r8 = tile_row((EXP, 1), 0)
    sums = [jnp.zeros((EXP, 8), F)] * 4
    for n, (i, a, more) in enumerate(ada_groups()):
        at = g_at + a * 256
        piece = dm[:, n * 256 : (n + 1) * 256]
        sums[i] = sums[i] + jnp.where(r8 >= SHIFTS[i], dot(g[:, at : at + 256], piece, NT), 0.0)
        if more:
            sums[i] = sums[i] + jnp.where(r8 < SHIFTS[i], dot(g[:, at + 256 : at + 512], piece, NT), 0.0)
    total = jnp.zeros((8, D), F)
    for i in range(4):
        rest = sums[i].T
        for _ in range(3):
            level = rest.astype(B)
            rest = rest - level.astype(F)
            total = total + dot(level, selt[i], NT)
    return total


def forward(x, w, mod, k, y, save=lambda *names: None):
    main, bias, fc2 = w["main"], w["bias"], w["fc2"]

    def ln_in(i, _):
        rows = pl.ds(pl.multiple_of(i * 128, 128), 128)
        lat = pl.ds(i // 2, 1)
        n, _ = stats(x[rows, :].astype(F))
        k["ain"][rows, :] = (n * (1.0 + mod[lat, D : 2 * D]) + mod[lat, :D]).astype(B)
        return 0

    lax.fori_loop(0, 4, ln_in, 0, unroll=True)

    for c in range(3):
        cs = slice(c * D, (c + 1) * D)
        k["qkv"][:, cs] = (dot(k["ain"][...], main[:, cs]) + bias[:, cs]).astype(B)

    low, high = head_masks()

    def attend(i, _):
        rows = pl.ds(pl.multiple_of((i // 3) * SEQ, SEQ), SEQ)
        at = (i % 3) * 128
        q = k["qkv"][rows, pl.ds(pl.multiple_of(at, 128), 128)]
        key = k["qkv"][rows, pl.ds(pl.multiple_of(D + at, 128), 128)]
        vt = k["qkv"][rows, pl.ds(pl.multiple_of(2 * D + at, 128), 128)].T
        heads = []
        for h, m in enumerate((low, high)):
            s = dot(key, q * (m * 0.125), NT)
            top = jnp.max(s, axis=0, keepdims=True)
            e = jnp.exp(s - top)
            t = jnp.sum(e, axis=0, keepdims=True)
            p = (e * (1.0 / t)).astype(B)
            k["lse"][i, h : h + 1, :] = top + jnp.log(t)
            heads.append(dot(vt[h * HEAD : (h + 1) * HEAD], p))
        k["att"][rows, pl.ds(pl.multiple_of(at, 128), 128)] = jnp.concatenate(heads, axis=0).T.astype(B)
        return 0

    lax.fori_loop(0, 6, attend, 0, unroll=UNROLL)
    save("ain", "qkv", "lse", "att")
    k["o"][...] = dot(k["att"][...], main[:, C_PROJ:C_FC1]) + bias[:, C_PROJ:C_FC1]

    def mid(i, _):
        rows = pl.ds(pl.multiple_of(i * 128, 128), 128)
        lat = pl.ds(i // 2, 1)
        x1 = x[rows, :].astype(F) + mod[lat, 2 * D : 3 * D] * k["o"][rows, :]
        k["x1"][rows, :] = x1
        n, _ = stats(x1)
        k["min"][rows, :] = (n * (1.0 + mod[lat, 4 * D : 5 * D]) + mod[lat, 3 * D : 4 * D]).astype(B)
        return 0

    lax.fori_loop(0, 4, mid, 0, unroll=True)

    def mlp(i, _):
        at = pl.multiple_of(i * 256, 256)
        cs = pl.ds(at, 256)
        ws = pl.ds(pl.multiple_of(C_FC1 + at, 256), 256)
        z = dot(k["min"][...], main[:, ws]) + bias[:, ws]
        zz = z * z
        t = jnp.tanh(z * (K0 + K0 * K1 * zz))
        half = 0.5 + 0.5 * t
        k["act"][:, cs] = (z * half).astype(B)
        k["slope"][:, cs] = half + (0.5 * z) * (1.0 - t * t) * (K0 + 3.0 * K0 * K1 * zz)
        return 0

    lax.fori_loop(0, 6, mlp, 0, unroll=True)

    save("o", "x1", "min", "slope", "act")
    k["f"][...] = dot(k["act"][...], fc2[...]) + w["bias2"][...]

    def out(i, _):
        rows = pl.ds(pl.multiple_of(i * 128, 128), 128)
        lat = pl.ds(i // 2, 1)
        y[rows, :] = (k["x1"][rows, :] + mod[lat, 5 * D : 6 * D] * k["f"][rows, :]).astype(B)
        return 0

    save("f")
    lax.fori_loop(0, 4, out, 0, unroll=True)


def token_sum(v):
    return jnp.sum(v, axis=0, keepdims=True)


def spread(sel, i, v):
    return dot(sel[i], v, NT).astype(B)


def backward(core, grad, x, cond, g, g_at, sel, selt, w, mod, k, t, dx, dc, put, ship, finish):
    main, fc2 = w["main"], w["fc2"]
    dmod = t["dmod"]
    dmod[...] = jnp.zeros_like(dmod)

    def add_mod(lat, piece, v):
        cs = slice(piece * D, (piece + 1) * D)
        dmod[lat, cs] = dmod[lat, cs] + v

    t["db"][...] = jnp.zeros_like(t["db"])
    r8 = tile_row((EXP, 1), 0)

    def add_db(at, v):
        t["db"][:, at : at + v.shape[1]] = t["db"][:, at : at + v.shape[1]] + v


    def start(i, _):
        rows = pl.ds(pl.multiple_of(i * 128, 128), 128)
        lat = pl.ds(i // 2, 1)
        gr = grad[rows, :].astype(F)
        df = (gr * mod[lat, 5 * D : 6 * D]).astype(B)
        t["df"][rows, :] = df
        add_mod(lat, 5, token_sum(gr * k["f"][rows, :]))
        add_db(2688, token_sum(df.astype(F)))
        return 0

    lax.fori_loop(0, 4, start, 0, unroll=True)

    def dmlp(i, _):
        cs = pl.ds(pl.multiple_of(i * 256, 256), 256)
        da = dot(t["df"][...], fc2[cs, :], NT)
        dz = (da * k["slope"][:, cs]).astype(B)
        t["dz"][:, cs] = dz
        ds = pl.ds(pl.multiple_of(1152 + i * 256, 128), 256)
        t["db"][:, ds] = token_sum(dz.astype(F))
        return 0

    lax.fori_loop(0, 6, dmlp, 0, unroll=True)

    t["wide2"][...] = spread(sel, 2, k["min"][...])
    t["wide"][...] = spread(sel, 3, k["min"][...])
    for c in range(0, QUARTER, 256):
        d2 = dot(t["wide2"][...], t["dz"][:, c : c + 256])
        d3 = dot(t["wide"][...], t["dz"][:, QUARTER + c : QUARTER + c + 256])
        put(0, slice(0, EXP), slice(2 * QUARTER + c, 2 * QUARTER + c + 256), jnp.where(r8 < 2, d2, d3).astype(B))
        t["part"][:, c : c + 256] = d2

    for c in range(4):
        part = dot(k["act"][:, c * D : (c + 1) * D], t["df"][...], TN).reshape(16, 24, D)
        for a in range(3):
            put(
                1,
                slice(c * 128, (c + 1) * 128),
                slice(a * D, (a + 1) * D),
                part[:, 8 * a : 8 * a + 8, :].reshape(128, D).astype(B),
            )

    t["dn"][...] = dot(t["dz"][...], main[:, C_FC1:C_MAIN], NT)

    def dmid(i, _):
        rows = pl.ds(pl.multiple_of(i * 128, 128), 128)
        lat = pl.ds(i // 2, 1)
        dmin = t["dn"][rows, :]
        n, inv = stats(k["x1"][rows, :])
        add_mod(lat, 4, token_sum(dmin * n))
        add_mod(lat, 3, token_sum(dmin))
        d1 = grad[rows, :].astype(F) + norm_back(dmin * (1.0 + mod[lat, 4 * D : 5 * D]), n, inv)
        t["dx1"][rows, :] = d1
        do = (d1 * mod[lat, 2 * D : 3 * D]).astype(B)
        add_mod(lat, 2, token_sum(d1 * k["o"][rows, :]))
        t["df"][rows, :] = do
        add_db(768, token_sum(do.astype(F)))
        return 0

    lax.fori_loop(0, 4, dmid, 0, unroll=True)
    t["datt"][...] = dot(t["df"][...], main[:, C_PROJ:C_FC1], NT).astype(B)

    t["wide2"][...] = spread(sel, 1, k["att"][...])
    d1 = dot(t["wide2"][...], t["df"][...])
    put(0, slice(0, EXP), slice(QUARTER + 384, 2 * QUARTER), jnp.where(r8 < 4, d1, t["part"][:, 384:]).astype(B))
    t["part2"][...] = d1

    low, high = head_masks()

    def dattend(i, _):
        rows = pl.ds(pl.multiple_of((i // 3) * SEQ, SEQ), SEQ)
        at = (i % 3) * 128
        qs = pl.ds(pl.multiple_of(at, 128), 128)
        ks = pl.ds(pl.multiple_of(D + at, 128), 128)
        vs = pl.ds(pl.multiple_of(2 * D + at, 128), 128)
        q = k["qkv"][rows, qs]
        key = k["qkv"][rows, ks]
        v = k["qkv"][rows, vs]
        da = t["datt"][rows, qs]
        kt = key.T
        dk = dv = None
        dqs = []
        for h, m in enumerate((low, high)):
            qm = q * (m * 0.125)
            dam = da * m
            s = dot(key, qm, NT)
            p = jnp.exp(s - k["lse"][i, h : h + 1, :])
            dp = dot(v, dam, NT)
            ds = (p * (dp - jnp.sum(p * dp, axis=0, keepdims=True))).astype(B)
            v1 = dot(p.astype(B), dam)
            k1 = dot(ds, qm)
            dqs.append(dot(kt[h * HEAD : (h + 1) * HEAD], ds))
            dv = v1 if dv is None else dv + v1
            dk = k1 if dk is None else dk + k1
        t["dqkv"][rows, qs] = (jnp.concatenate(dqs, axis=0).T * 0.125).astype(B)
        t["dqkv"][rows, ks] = dk.astype(B)
        t["dqkv"][rows, vs] = dv.astype(B)
        return 0

    lax.fori_loop(0, 6, dattend, 0, unroll=UNROLL)

    t["wide"][...] = spread(sel, 0, k["ain"][...])
    t["wide2"][...] = spread(sel, 1, k["ain"][...])
    d1 = dot(t["wide2"][...], t["dqkv"][:, QUARTER:])
    d0 = dot(t["wide"][...], t["dqkv"][:, :384])
    put(0, slice(0, EXP), slice(0, 384), jnp.where(r8 < 6, d0, d1).astype(B))
    put(0, slice(0, EXP), slice(QUARTER, QUARTER + 384), jnp.where(r8 < 4, d1, t["part"][:, :384]).astype(B))
    d0 = dot(t["wide"][...], t["dqkv"][:, 384:QUARTER])
    put(0, slice(0, EXP), slice(384, QUARTER), jnp.where(r8 < 6, d0, t["part2"][...]).astype(B))
    ship(0, 0, P_DB0)
    ship(1, 0, P_MOD)

    def bias_sums(i, _):
        rows = pl.ds(pl.multiple_of(i * 128, 128), 128)
        add_db(0, token_sum(t["dqkv"][rows, :D].astype(F)))
        add_db(D, token_sum(t["dqkv"][rows, 2 * D :].astype(F)))
        return 0

    lax.fori_loop(0, 4, bias_sums, 0, unroll=True)

    t["dn"][...] = dot(t["dqkv"][...], main[:, C_QKV:C_PROJ], NT)

    def dlast(i, _):
        rows = pl.ds(pl.multiple_of(i * 128, 128), 128)
        lat = pl.ds(i // 2, 1)
        dain = t["dn"][rows, :]
        n, inv = stats(x[rows, :].astype(F))
        add_mod(lat, 1, token_sum(dain * n))
        add_mod(lat, 0, token_sum(dain))
        back = norm_back(dain * (1.0 + mod[lat, D : 2 * D]), n, inv)
        dx[rows, :] = (t["dx1"][rows, :] + back).astype(B)
        return 0

    lax.fori_loop(0, 4, dlast, 0, unroll=True)

    c = cond[...]
    sig = jax.nn.sigmoid(c)
    act = c * sig
    dm = dmod[...].astype(B).astype(F)
    dc[...] = cond_back(dm.astype(B), g, g_at, selt) * (sig * (1.0 + c * (1.0 - sig)))

    mine = 2 * core
    block = pltpu.roll(dm[:, :1152], mine, 0) + pltpu.roll(dm[:, 1152:], mine + 4, 0)
    for q in range(4):
        rows = slice(q * 128, (q + 1) * 128)
        put(1, rows, slice(P_MOD, P_DB1), jnp.broadcast_to(block[None], (16, 8, 1152)).reshape(128, 1152).astype(B))

    db = t["db"]
    for half, at, first in ((0, P_DB0, 0), (0, P_DB0 + 128, 8), (1, P_DB1, 16)):
        rows = jnp.concatenate([db[:, (first + i) * 128 : (first + i + 1) * 128] for i in range(8)], axis=0)
        put(half, slice(0, EXP), slice(at, at + 128), jnp.broadcast_to(rows[None], (CHIPS, 8, 128)).reshape(EXP, 128).astype(B))

    act = act.astype(B).astype(F)
    both = pltpu.roll(act, mine, 0) + pltpu.roll(act, mine + 4, 0)
    both = jnp.broadcast_to(both[None], (CHIPS, 8, D)).reshape(EXP, D)
    feature = lax.broadcasted_iota(jnp.int32, (1, D), 1)
    device = lax.broadcasted_iota(jnp.int32, (EXP, 1), 0) >> 3
    both = jnp.where(group_of(feature, 6) == device, both, 0.0).astype(B)
    feature = lax.broadcasted_iota(jnp.int32, (D, 1), 0)
    lane = lax.broadcasted_iota(jnp.int32, (1, 128), 1)
    pick = ((feature - 6 * group_of(feature, 6)) == (lane & 7)) & (lane < 16)
    found = dot(both, pick.astype(F).astype(B))
    put(1, slice(0, EXP), slice(P_COND, P_HALF), jnp.where((r8 >> 2) == (lane >> 3), found, 0.0).astype(B))
    ship(0, P_DB0, P_HALF)
    ship(1, P_MOD, P_HALF)
    finish()


KEEP = (
    ("ain", (ROWS, D), B),
    ("qkv", (ROWS, 3 * D), B),
    ("lse", (6, 8, SEQ), F),
    ("att", (ROWS, D), B),
    ("o", (ROWS, D), F),
    ("x1", (ROWS, D), F),
    ("min", (ROWS, D), B),
    ("slope", (ROWS, FF), F),
    ("act", (ROWS, FF), B),
    ("f", (ROWS, D), F),
)
WEIGHTS = (("main", (D, C_MAIN), B), ("bias", (1, C_MAIN), F), ("bias2", (1, D), F), ("fc2", (FF, D), B))
TEMPS = (
    ("dmod", (8, 6 * D), F),
    ("db", (1, 3072), F),
    ("part", (EXP, QUARTER), F),
    ("part2", (EXP, D), F),
    ("wide2", (EXP, ROWS), B),
    ("df", (ROWS, D), B),
    ("dz", (ROWS, FF), B),
    ("wide", (EXP, ROWS), B),
    ("dx1", (ROWS, D), F),
    ("dn", (ROWS, D), F),
    ("datt", (ROWS, D), B),
    ("dqkv", (ROWS, 3 * D), B),
)
MOD = (("mod", (8, 6 * D), F),)


def buffers(table):
    return [pltpu.VMEM(shape, dtype) for _, shape, dtype in table]


def shapes(table):
    return [jax.ShapeDtypeStruct(shape, dtype) for _, shape, dtype in table]


def named(table, refs):
    return {name: ref for (name, _, _), ref in zip(table, refs)}


def fetch_halves(core, own, other, g, sems):
    def go(low, high):
        copies = [
            pltpu.make_async_copy(low, g.at[:, :G_HALF], sems.at[0]),
            pltpu.make_async_copy(high, g.at[:, G_HALF:], sems.at[1]),
        ]
        for copy in copies:
            copy.start()
        for copy in copies:
            copy.wait()

    @pl.when(core == 0)
    def _():
        go(own, other)

    @pl.when(core != 0)
    def _():
        go(other, own)


def fetch_ada(core, own, other, g, sems):
    def go(high):
        copy = pltpu.make_async_copy(high.at[:, G_ADA - G_HALF : G_BIAS - G_HALF], g, sems.at[0])
        copy.start()
        copy.wait()

    @pl.when(core == 0)
    def _():
        go(other)

    @pl.when(core != 0)
    def _():
        go(own)


def sender(core, pack, keep, send, sems):
    started = []

    def start(half, first, last):
        n = len(started)
        cols = slice(first, last)

        def copy(slot, ref):
            return pltpu.make_async_copy(pack.at[slot, :, cols], ref.at[:, cols], sems.at[n])

        mine = copy(0, keep)
        theirs = copy(1, send)
        started.append((half, mine, theirs))

        @pl.when(core == half)
        def _():
            mine.start()

        @pl.when(core != half)
        def _():
            theirs.start()

    def finish():
        for half, mine, theirs in started:

            @pl.when(core == half)
            def _(mine=mine):
                mine.wait()

            @pl.when(core != half)
            def _(theirs=theirs):
                theirs.wait()

    return start, finish


def putter(core, pack):
    def put(half, rows, cols, value):
        slot = core if half == 0 else 1 - core
        pack[slot, rows, cols] = value

    return put


def front_kernel(place, own, other, x, cond, y, *refs):
    saved = KEEP + WEIGHTS + MOD
    n = len(saved)
    out = named(saved, refs[:n])
    buf = named(saved, refs[n : 2 * n])
    g, low, high, order, sems, save_sems = refs[2 * n :]
    copies = []

    def save(*names):
        for name in names:
            copy = pltpu.make_async_copy(buf[name], out[name], save_sems.at[len(copies)])
            copy.start()
            copies.append(copy)

    gather_selectors(low, place, 0)
    gather_selectors(high, place, 1)
    fetch_halves(place[0], own, other, g, sems)
    ada = unpack(g, low, place, order, buf)
    save("main", "bias", "bias2", "fc2")
    modulate(cond, g, high, ada, buf["mod"])
    save("mod")
    forward(x, buf, buf["mod"], buf, y, save)
    for copy in copies:
        copy.wait()


def turn_kernel(place, own, other, x, cond, grad, y, dx, dc, keep, send, *refs):
    n_keep, n_w, n_t = len(KEEP), len(WEIGHTS), len(TEMPS)
    k = named(KEEP, refs[:n_keep])
    w = named(WEIGHTS, refs[n_keep : n_keep + n_w])
    t = named(TEMPS, refs[n_keep + n_w : n_keep + n_w + n_t])
    mod, g, sel, low, high, order, pack, sems = refs[n_keep + n_w + n_t :]
    send_selectors(sel)
    gather_selectors(low, place, 0)
    gather_selectors(high, place, 1)
    core = place[0]
    fetch_halves(core, own, other, g, sems)
    ada = unpack(g, low, place, order, w)
    modulate(cond, g, high, ada, mod)
    forward(x, w, mod, k, y)
    backward(core, grad, x, cond, g, G_ADA, sel, high, w, mod, k, t, dx, dc, putter(core, pack), *sender(core, pack, keep, send, sems))


def back_kernel(place, own, other, x, cond, grad, *refs):
    n_keep, n_w, n_t = len(KEEP), len(WEIGHTS), len(TEMPS)
    k = named(KEEP, refs[:n_keep])
    w = named(WEIGHTS, refs[n_keep : n_keep + n_w])
    mod, dx, dc, keep, send = refs[n_keep + n_w : n_keep + n_w + 5]
    refs = refs[n_keep + n_w + 5 :]
    t = named(TEMPS, refs[:n_t])
    g, sel, high, pack, sems = refs[n_t:]
    send_selectors(sel)
    gather_selectors(high, place, 1)
    core = place[0]
    fetch_ada(core, own, other, g, sems)
    backward(core, grad, x, cond, g, 0, sel, high, w, mod, k, t, dx, dc, putter(core, pack), *sender(core, pack, keep, send, sems))


VM = pl.BlockSpec(memory_space=pltpu.VMEM)
ANY = pl.BlockSpec(memory_space=pl.ANY)
SM = pl.BlockSpec(memory_space=pltpu.SMEM)
PARAMS = pltpu.CompilerParams(vmem_limit_bytes=60 * 1024 * 1024)
G_BUF = pltpu.VMEM((EXP, G_END), B)
ADA_BUF = pltpu.VMEM((EXP, G_BIAS - G_ADA), B)
SEL_BUF = pltpu.VMEM((4, EXP, D), B)
SELT_BUF = pltpu.VMEM((4, D, EXP), B)
ORDER_BUF = pltpu.VMEM((2, EXP, EXP), B)
SEMS = pltpu.SemaphoreType.DMA((5,))
ROWS_OUT = jax.ShapeDtypeStruct((ROWS, D), B)
COND_OUT = jax.ShapeDtypeStruct((8, D), F)
HALF_OUT = jax.ShapeDtypeStruct((EXP, P_HALF), B)
PACK_BUF = pltpu.VMEM((2, EXP, P_HALF), B)


def cost(units):
    return pl.CostEstimate(flops=units * 2_000_000_000, bytes_accessed=units * 10_000_000, transcendentals=units * 2_000_000)


def front(place, own, other, x, cond):
    outs = [ROWS_OUT] + shapes(KEEP) + shapes(WEIGHTS) + shapes(MOD)
    return pl.pallas_call(
        front_kernel,
        out_shape=outs,
        in_specs=[SM, ANY, ANY, VM, VM],
        out_specs=[VM] + [ANY] * (len(outs) - 1),
        scratch_shapes=buffers(KEEP + WEIGHTS + MOD)
        + [G_BUF, SELT_BUF, SELT_BUF, ORDER_BUF, SEMS, pltpu.SemaphoreType.DMA((len(outs) - 1,))],
        compiler_params=PARAMS,
        cost_estimate=cost(1),
        name="front",
    )(place, own, other, x, cond)


def turn(place, own, other, x, cond, grad):
    return pl.pallas_call(
        turn_kernel,
        out_shape=[ROWS_OUT, ROWS_OUT, COND_OUT, HALF_OUT, HALF_OUT],
        in_specs=[SM, ANY, ANY, VM, VM, VM],
        out_specs=[VM] * 3 + [ANY] * 2,
        scratch_shapes=buffers(KEEP) + buffers(WEIGHTS) + buffers(TEMPS) + buffers(MOD) + [G_BUF, SEL_BUF, SELT_BUF, SELT_BUF, ORDER_BUF, PACK_BUF, SEMS],
        compiler_params=PARAMS,
        cost_estimate=cost(3),
        name="turn",
    )(place, own, other, x, cond, grad)


def back(place, own, other, x, cond, grad, kept):
    return pl.pallas_call(
        back_kernel,
        out_shape=[ROWS_OUT, COND_OUT, HALF_OUT, HALF_OUT],
        in_specs=[SM, ANY, ANY, VM, VM, VM] + [VM] * len(kept),
        out_specs=[VM] * 2 + [ANY] * 2,
        scratch_shapes=buffers(TEMPS) + [ADA_BUF, SEL_BUF, SELT_BUF, PACK_BUF, SEMS],
        compiler_params=PARAMS,
        cost_estimate=cost(2),
        name="back",
    )(place, own, other, x, cond, grad, *kept)


def line_up_kernel(w_qkv, w_proj, w_fc1, w_fc2, w_ada, b_qv, b_proj, b_fc1, b_fc2, b_ada, out, main, ada, bias):
    def rows(ref, first, last):
        return ref[:, first:last].astype(F)

    main[0:6, :] = rows(w_qkv, 0, QUARTER)
    main[6:12, :384] = rows(w_qkv, QUARTER, C_PROJ)
    main[6:12, 384:] = rows(w_proj, 0, D)
    main[12:18, :] = rows(w_fc1, 0, QUARTER)
    main[18:24, :] = rows(w_fc1, QUARTER, FF)
    ada[48:56, :] = jnp.zeros((8, 256), F)
    for i in range(9):
        ada[6 * i : 6 * i + 6, :] = rows(w_ada, 256 * i, 256 * i + 256)
    for a in range(3):
        out[:, a * QUARTER : (a + 1) * QUARTER] = main[8 * a : 8 * a + 8, :].astype(B)
        out[:, G_FC2 + a * D : G_FC2 + (a + 1) * D] = w_fc2[8 * a : 8 * a + 8, :]
    for a in range(7):
        out[:, G_ADA + a * 256 : G_ADA + (a + 1) * 256] = ada[8 * a : 8 * a + 8, :].astype(B)
    bias[...] = jnp.zeros((8, 128), F)
    for ref, (lane, width) in zip((b_qv, b_proj, b_fc1, b_fc2, b_ada), BIASES):
        bias[0:1, lane : lane + width] = ref[...].astype(F)
    out[:, G_BIAS:G_END] = bias[...].astype(B)


def line_up(w_qkv, b_qv, w_proj, b_proj, w_fc1, b_fc1, w_fc2, b_fc2, w_ada, b_ada):
    biases = [b.reshape(1, -1) for b in (b_qv, b_proj, b_fc1, b_fc2, b_ada)]
    return pl.pallas_call(
        line_up_kernel,
        out_shape=jax.ShapeDtypeStruct((8, G_END), B),
        in_specs=[VM] * 10,
        out_specs=VM,
        scratch_shapes=[pltpu.VMEM((24, QUARTER), F), pltpu.VMEM((56, 256), F), pltpu.VMEM((8, 128), F)],
        name="line_up",
    )(w_qkv, w_proj, w_fc1, w_fc2, w_ada, *biases)


def swap(x):
    return lax.ppermute(x, "pipe", [(0, 1), (1, 0)])


def gather_stage(block, stage):
    def behind(by):
        pairs = []
        for core in range(2):
            stride = STRIDES[STAGES[core][stage]]
            for i in range(CHIPS):
                at = (i // stride) % 4
                pairs.append((core * CHIPS + i, core * CHIPS + i + ((at + by) % 4 - at) * stride))
        return lax.ppermute(block, ("pipe", "shard"), pairs)

    return [block] + [behind(by) for by in (1, 2, 3)]


def scatter(block):
    return lax.all_to_all(block.reshape(CHIPS, 8, P_HALF), "shard", 0, 0, tiled=True)


def shards(latents, conditions, cotangent, w_qkv, b_qv, w_proj, b_proj, w_fc1, b_fc1, w_fc2, b_fc2, w_ada, b_ada):
    p = lax.axis_index("pipe")
    j = lax.axis_index("shard")
    first = p == 0
    place = jnp.stack([p, j >> 4, (j >> 2) & 3, j & 3]).astype(jnp.int32)
    block = line_up(w_qkv[0], b_qv[0], w_proj[0], b_proj[0], w_fc1[0], b_fc1[0], w_fc2[0], b_fc2[0], w_ada[0], b_ada[0])
    block_other = swap(block)
    low = jnp.where(first, block[:, :G_HALF], block_other[:, G_HALF:])
    high = jnp.where(first, block_other[:, :G_HALF], block[:, G_HALF:])
    both = jnp.concatenate([low, high], axis=1)
    for stage in range(2):
        both = jnp.concatenate(gather_stage(both, stage), axis=0)
    own0 = jnp.concatenate(gather_stage(both[:, :G_HALF], 2), axis=0)
    other0 = swap(own0)
    high, own0 = lax.optimization_barrier((both[:, G_HALF:], own0))
    pieces1 = gather_stage(high, 2)
    x = lax.dynamic_index_in_dim(latents, p, 0, keepdims=False).reshape(ROWS, D)
    cot = lax.dynamic_index_in_dim(cotangent, p, 0, keepdims=False).reshape(ROWS, D)
    cond = lax.dynamic_index_in_dim(conditions, p, 0, keepdims=False).astype(F)
    cond = jnp.concatenate([cond, jnp.zeros((6, D), F)], axis=0)

    h, *kept = front(place, own0, other0, x, cond)
    h, *pieces1 = lax.optimization_barrier((h, *pieces1))
    own1 = jnp.concatenate(pieces1, axis=0)
    other1 = swap(own1)
    y, dx1, dc1, keep1, send1 = turn(place, own1, other1, h, cond, cot)
    parts1 = scatter(keep1 + swap(send1))
    dx0, dc0, keep0, send0 = back(place, own0, other0, x, cond, dx1, kept)
    parts1, send0 = lax.optimization_barrier((parts1, send0))
    parts0 = scatter(keep0 + swap(send0))

    def pair(for_first, for_second):
        keep = jnp.where(first, for_first, for_second)
        came = swap(jnp.where(first, for_second, for_first))
        both = jnp.where(first, jnp.stack([keep, came]), jnp.stack([came, keep]))
        return both.reshape(1, 2, 2, SEQ, D)

    section_outputs = pair(h, y)
    input_grads = pair(dx0, dx1)
    dc = (dc0 + dc1)[:2]
    dc_other = swap(dc)
    cond_grad = jnp.where(first, jnp.stack([dc, dc_other]), jnp.stack([dc_other, dc]))

    parts0, section_outputs, input_grads, cond_grad = lax.optimization_barrier(
        (parts0, section_outputs, input_grads, cond_grad)
    )

    def reduced(parts):
        lot = jnp.sum(parts.astype(F), axis=0)
        flat = parts.reshape(EXP, P_HALF)
        ada = lax.dot_general(
            flat[:, P_COND : P_COND + 16], flat[:, P_MOD:P_DB1], (((0,), (0,)), ((), ())), preferred_element_type=F
        )
        return jnp.concatenate([lot, ada[:8], ada[8:]], axis=1)

    lot0 = reduced(parts0)
    lot1 = reduced(parts1)
    kept_half = jnp.where(first, lot0, lot1)
    came_half = swap(jnp.where(first, lot1, lot0))
    low = jnp.where(first, kept_half, came_half)
    high = jnp.where(first, came_half, kept_half)

    rows = jnp.concatenate([low[:, a * QUARTER : (a + 1) * QUARTER] for a in range(3)], axis=0)
    quarters = [rows[6 * q : 6 * q + 6] for q in range(4)]
    db = jnp.concatenate([low[:, P_DB0 : P_DB0 + 128], low[:, P_DB0 + 128 : P_HALF], high[:, P_DB1:P_COND]], axis=0).reshape(-1)
    sums = high[:, P_MOD:P_DB1]
    db_ada = jnp.concatenate([sums[:4].sum(axis=0), sums[4:].sum(axis=0)])

    def slice_of(line, at, width):
        return lax.dynamic_slice(line, (at + width * j,), (width,))

    outs = (
        jnp.concatenate([quarters[0], quarters[1][:, :384]], axis=1),
        slice_of(db, 0, 12),
        quarters[1][:, 384:],
        slice_of(db, 768, 6),
        jnp.concatenate([quarters[2], quarters[3]], axis=1),
        slice_of(db, 1152, 24),
        jnp.concatenate([high[:, a * D : (a + 1) * D] for a in range(3)], axis=0),
        slice_of(db, 2688, 6),
        jnp.concatenate([high[:6, P_HALF : P_HALF + 1152], high[:6, P_HALF + 1152 :]], axis=1),
        slice_of(db_ada, 0, 36),
    )
    return (section_outputs, input_grads, cond_grad) + tuple(o[None] for o in outs)


def solution(mesh):
    rows = P(None, "shard", None, None)
    wide = P("pipe", "shard", None)
    thin = P("pipe", "shard")
    both = P("pipe", None, "shard", None, None)
    pairs = (wide, thin) * 5
    return jax.shard_map(
        shards,
        mesh=mesh,
        in_specs=(rows, P(None, "shard", None), rows) + pairs,
        out_specs=(both, both, P(None, "shard", None)) + pairs,
        check_vma=False,
    )
```

```python
import functools

import jax
import jax.numpy as jnp
from jax import lax
from jax.experimental import pallas as pl
from jax.experimental.pallas import tpu as pltpu
from jax.sharding import PartitionSpec as P

F = jnp.float32
B = jnp.bfloat16
D = 384
HEADS = 6
HEAD = 64
FF = 1536
SEQ = 256
EPS = 1e-06
CHIPS = 64
ROWS = 512
EXP = 512

C_QKV, C_PROJ, C_FC1, C_MAIN = 0, 1152, 1536, 3072
QUARTER = 768

G_FC2, G_ADA, G_BIAS, G_END = 2304, 3456, 5248, 5376
G_HALF = 2688
BIASES = ((0, 12), (12, 6), (18, 24), (42, 6), (48, 36))

P_HALF = 2560
P_DB0 = 2304
P_MOD, P_DB1, P_COND = 1152, 2304, 2432
SHIFTS = (0, 6, 4, 2)

K0 = 0.7978845608028654
K1 = 0.044715

UNROLL = 6
NN = (1, 0)
NT = (1, 1)
TN = (0, 0)


def dot(a, b, dims=NN):
    return lax.dot_general(a, b, (((dims[0],), (dims[1],)), ((), ())), preferred_element_type=F)


STRIDES = {"y": 16, "x": 4, "z": 1}
STAGES = (("x", "y", "z"), ("y", "z", "x"))


def owner(block, place, core):
    total = 0
    for stage, axis in enumerate(STAGES[core]):
        here = place[1 + "yxz".index(axis)]
        behind = (block >> (2 * stage)) & 3
        total = total + STRIDES[axis] * ((here - behind) & 3)
    return total


def targets(shape, dim, shift, owner_of):
    at = lax.broadcasted_iota(jnp.int32, shape, dim)
    r = ((at & 7) + (8 - shift)) & 7
    return jnp.where(r < 6, owner_of(at >> 3) * 6 + r, -1)


def send_selectors(sel):
    col = lax.broadcasted_iota(jnp.int32, (1, D), 1)
    for i, shift in enumerate(SHIFTS):
        sel[i] = (targets((EXP, 1), 0, shift, lambda block: block) == col).astype(F).astype(B)


def gather_selectors(selt, place, core):
    row = lax.broadcasted_iota(jnp.int32, (D, 1), 0)
    for i, shift in enumerate(SHIFTS):
        found = targets((1, EXP), 1, shift, lambda block: owner(block, place, core))
        selt[i] = (row == found).astype(F).astype(B)


def row_order(place, core):
    at = lax.broadcasted_iota(jnp.int32, (1, EXP), 1)
    found = owner(at >> 3, place, core) * 8 + (at & 7)
    return (lax.broadcasted_iota(jnp.int32, (EXP, 1), 0) == found).astype(F).astype(B)


def group_of(n, width):
    return jnp.floor((n.astype(F) + 0.5) * (1.0 / width)).astype(jnp.int32)


def natural_bias(gb, lane, width):
    n = CHIPS * width
    at = lax.broadcasted_iota(jnp.int32, (1, n), 1)
    owner = group_of(at, width)
    spot = at - owner * width + lane
    pick = (lax.broadcasted_iota(jnp.int32, (128, 1), 0) == spot).astype(F).astype(B)
    wide = dot(gb, pick)
    return jnp.sum(jnp.where(lax.broadcasted_iota(jnp.int32, (CHIPS, 1), 0) == owner, wide, 0.0), axis=0, keepdims=True)


def order_rows(order, place):
    for core in range(2):
        order[core] = row_order(place, core)


def tile_row(shape, dim):
    return lax.broadcasted_iota(jnp.int32, shape, dim) & 7


def stats(v):
    centre = v - jnp.mean(v, axis=-1, keepdims=True)
    inv = lax.rsqrt(jnp.mean(centre * centre, axis=-1, keepdims=True) + EPS)
    return centre * inv, inv


def norm_back(g, n, inv):
    mg = jnp.mean(g, axis=-1, keepdims=True)
    mgn = jnp.mean(g * n, axis=-1, keepdims=True)
    return inv * (g - mg - n * mgn)


def head_masks():
    lane = lax.broadcasted_iota(jnp.int32, (1, 128), 1)
    low = (lane < HEAD).astype(F)
    return low.astype(B), (1.0 - low).astype(B)


def unpack(g, selt, place, order, w):
    r8 = tile_row((EXP, 1), 0)

    def piece(a, c):
        return g[:, a * QUARTER + c : a * QUARTER + c + 384]

    def merge(edge, a, c):
        return jnp.where(r8 >= edge, piece(a, c).astype(F), piece(a + 1, c).astype(F)).astype(B)

    for c in (0, 384):
        w["main"][:, c : c + 384] = dot(selt[0], piece(0, c)).astype(B)
        w["main"][:, QUARTER + c : QUARTER + c + 384] = dot(selt[1], merge(6, 0, c)).astype(B)
        w["main"][:, 2 * QUARTER + c : 2 * QUARTER + c + 384] = dot(selt[2], merge(4, 1, c)).astype(B)
        w["main"][:, 3 * QUARTER + c : 3 * QUARTER + c + 384] = dot(selt[3], piece(2, c)).astype(B)

    lane = lax.broadcasted_iota(jnp.int32, (1, EXP), 1)
    from_device = jnp.where((lane & 7) == 0, owner(lane >> 3, place, 1), -1)
    lead = (lax.broadcasted_iota(jnp.int32, (CHIPS, 1), 0) == from_device).astype(F).astype(B)
    gb = dot(lead, g[:, G_BIAS:G_END]).astype(B)
    qv, proj, fc1, fc2, ada = (natural_bias(gb, lane, width) for lane, width in BIASES)
    w["bias"][:, :D] = qv[:, :D]
    w["bias"][:, D : 2 * D] = jnp.zeros((1, D), F)
    w["bias"][:, 2 * D : C_PROJ] = qv[:, D:]
    w["bias"][:, C_PROJ:C_FC1] = proj
    w["bias"][:, C_FC1:C_MAIN] = fc1
    w["bias2"][...] = fc2

    for i in range(4):
        rows = slice(i * 128, (i + 1) * 128)
        parts = [
            dot(order[min(a, 1), rows], g[:, G_FC2 + a * D : G_FC2 + (a + 1) * D]).reshape(16, 8, D) for a in range(3)
        ]
        w["fc2"][i * D : (i + 1) * D, :] = jnp.concatenate(parts, axis=1).reshape(D, D).astype(B)
    return ada


def ada_groups():
    return [(i % 4, (6 * i) // 8, SHIFTS[i % 4] in (6, 4)) for i in range(9)]


def modulate(cond, g, selt, ada, mod):
    c = cond[...]
    act = (c * jax.nn.sigmoid(c)).astype(B)
    r8 = tile_row((1, EXP), 1)
    wides = [dot(act, selt[i]) for i in range(4)]
    for n, (i, a, more) in enumerate(ada_groups()):
        at = G_ADA + a * 256
        first = jnp.where(r8 >= SHIFTS[i], wides[i], 0.0).astype(B)
        part = dot(first, g[:, at : at + 256])
        if more:
            part = part + dot(jnp.where(r8 < SHIFTS[i], wides[i], 0.0).astype(B), g[:, at + 256 : at + 512])
        mod[:, n * 256 : (n + 1) * 256] = part + ada[:, n * 256 : (n + 1) * 256]


def cond_back(dm, g, g_at, selt):
    r8 = tile_row((EXP, 1), 0)
    sums = [jnp.zeros((EXP, 8), F)] * 4
    for n, (i, a, more) in enumerate(ada_groups()):
        at = g_at + a * 256
        piece = dm[:, n * 256 : (n + 1) * 256]
        sums[i] = sums[i] + jnp.where(r8 >= SHIFTS[i], dot(g[:, at : at + 256], piece, NT), 0.0)
        if more:
            sums[i] = sums[i] + jnp.where(r8 < SHIFTS[i], dot(g[:, at + 256 : at + 512], piece, NT), 0.0)
    total = jnp.zeros((8, D), F)
    for i in range(4):
        rest = sums[i].T
        for _ in range(3):
            level = rest.astype(B)
            rest = rest - level.astype(F)
            total = total + dot(level, selt[i], NT)
    return total


def forward(x, w, mod, k, y, save=lambda *names: None):
    main, bias, fc2 = w["main"], w["bias"], w["fc2"]

    def ln_in(i, _):
        rows = pl.ds(pl.multiple_of(i * 128, 128), 128)
        lat = pl.ds(i // 2, 1)
        n, _ = stats(x[rows, :].astype(F))
        k["ain"][rows, :] = (n * (1.0 + mod[lat, D : 2 * D]) + mod[lat, :D]).astype(B)
        return 0

    lax.fori_loop(0, 4, ln_in, 0, unroll=True)

    for c in range(3):
        cs = slice(c * D, (c + 1) * D)
        k["qkv"][:, cs] = (dot(k["ain"][...], main[:, cs]) + bias[:, cs]).astype(B)

    low, high = head_masks()

    def attend(i, _):
        rows = pl.ds(pl.multiple_of((i // 3) * SEQ, SEQ), SEQ)
        at = (i % 3) * 128
        q = k["qkv"][rows, pl.ds(pl.multiple_of(at, 128), 128)]
        key = k["qkv"][rows, pl.ds(pl.multiple_of(D + at, 128), 128)]
        vt = k["qkv"][rows, pl.ds(pl.multiple_of(2 * D + at, 128), 128)].T
        heads = []
        for h, m in enumerate((low, high)):
            s = dot(key, q * (m * 0.125), NT)
            top = jnp.max(s, axis=0, keepdims=True)
            e = jnp.exp(s - top)
            t = jnp.sum(e, axis=0, keepdims=True)
            p = (e * (1.0 / t)).astype(B)
            k["lse"][i, h : h + 1, :] = top + jnp.log(t)
            heads.append(dot(vt[h * HEAD : (h + 1) * HEAD], p))
        k["att"][rows, pl.ds(pl.multiple_of(at, 128), 128)] = jnp.concatenate(heads, axis=0).T.astype(B)
        return 0

    lax.fori_loop(0, 6, attend, 0, unroll=UNROLL)
    save("ain", "qkv", "lse", "att")
    k["o"][...] = dot(k["att"][...], main[:, C_PROJ:C_FC1]) + bias[:, C_PROJ:C_FC1]

    def mid(i, _):
        rows = pl.ds(pl.multiple_of(i * 128, 128), 128)
        lat = pl.ds(i // 2, 1)
        x1 = x[rows, :].astype(F) + mod[lat, 2 * D : 3 * D] * k["o"][rows, :]
        k["x1"][rows, :] = x1
        n, _ = stats(x1)
        k["min"][rows, :] = (n * (1.0 + mod[lat, 4 * D : 5 * D]) + mod[lat, 3 * D : 4 * D]).astype(B)
        return 0

    lax.fori_loop(0, 4, mid, 0, unroll=True)

    def mlp(i, _):
        at = pl.multiple_of(i * 256, 256)
        cs = pl.ds(at, 256)
        ws = pl.ds(pl.multiple_of(C_FC1 + at, 256), 256)
        z = dot(k["min"][...], main[:, ws]) + bias[:, ws]
        zz = z * z
        t = jnp.tanh(z * (K0 + K0 * K1 * zz))
        half = 0.5 + 0.5 * t
        k["act"][:, cs] = (z * half).astype(B)
        k["slope"][:, cs] = half + (0.5 * z) * (1.0 - t * t) * (K0 + 3.0 * K0 * K1 * zz)
        return 0

    lax.fori_loop(0, 6, mlp, 0, unroll=True)

    save("o", "x1", "min", "slope", "act")
    k["f"][...] = dot(k["act"][...], fc2[...]) + w["bias2"][...]

    def out(i, _):
        rows = pl.ds(pl.multiple_of(i * 128, 128), 128)
        lat = pl.ds(i // 2, 1)
        y[rows, :] = (k["x1"][rows, :] + mod[lat, 5 * D : 6 * D] * k["f"][rows, :]).astype(B)
        return 0

    save("f")
    lax.fori_loop(0, 4, out, 0, unroll=True)


def token_sum(v):
    return jnp.sum(v, axis=0, keepdims=True)


def spread(sel, i, v):
    return dot(sel[i], v, NT).astype(B)


def backward(core, grad, x, cond, g, g_at, sel, selt, w, mod, k, t, dx, dc, put, ship, finish):
    main, fc2 = w["main"], w["fc2"]
    dmod = t["dmod"]
    dmod[...] = jnp.zeros_like(dmod)

    def add_mod(lat, piece, v):
        cs = slice(piece * D, (piece + 1) * D)
        dmod[lat, cs] = dmod[lat, cs] + v

    t["db"][...] = jnp.zeros_like(t["db"])
    r8 = tile_row((EXP, 1), 0)

    def add_db(at, v):
        t["db"][:, at : at + v.shape[1]] = t["db"][:, at : at + v.shape[1]] + v


    def start(i, _):
        rows = pl.ds(pl.multiple_of(i * 128, 128), 128)
        lat = pl.ds(i // 2, 1)
        gr = grad[rows, :].astype(F)
        df = (gr * mod[lat, 5 * D : 6 * D]).astype(B)
        t["df"][rows, :] = df
        add_mod(lat, 5, token_sum(gr * k["f"][rows, :]))
        add_db(2688, token_sum(df.astype(F)))
        return 0

    lax.fori_loop(0, 4, start, 0, unroll=True)

    def dmlp(i, _):
        cs = pl.ds(pl.multiple_of(i * 256, 256), 256)
        da = dot(t["df"][...], fc2[cs, :], NT)
        dz = (da * k["slope"][:, cs]).astype(B)
        t["dz"][:, cs] = dz
        ds = pl.ds(pl.multiple_of(1152 + i * 256, 128), 256)
        t["db"][:, ds] = token_sum(dz.astype(F))
        return 0

    lax.fori_loop(0, 6, dmlp, 0, unroll=True)

    t["wide2"][...] = spread(sel, 2, k["min"][...])
    t["wide"][...] = spread(sel, 3, k["min"][...])
    for c in range(0, QUARTER, 256):
        d2 = dot(t["wide2"][...], t["dz"][:, c : c + 256])
        d3 = dot(t["wide"][...], t["dz"][:, QUARTER + c : QUARTER + c + 256])
        put(0, slice(0, EXP), slice(2 * QUARTER + c, 2 * QUARTER + c + 256), jnp.where(r8 < 2, d2, d3).astype(B))
        t["part"][:, c : c + 256] = d2

    for c in range(4):
        part = dot(k["act"][:, c * D : (c + 1) * D], t["df"][...], TN).reshape(16, 24, D)
        for a in range(3):
            put(
                1,
                slice(c * 128, (c + 1) * 128),
                slice(a * D, (a + 1) * D),
                part[:, 8 * a : 8 * a + 8, :].reshape(128, D).astype(B),
            )

    t["dn"][...] = dot(t["dz"][...], main[:, C_FC1:C_MAIN], NT)

    def dmid(i, _):
        rows = pl.ds(pl.multiple_of(i * 128, 128), 128)
        lat = pl.ds(i // 2, 1)
        dmin = t["dn"][rows, :]
        n, inv = stats(k["x1"][rows, :])
        add_mod(lat, 4, token_sum(dmin * n))
        add_mod(lat, 3, token_sum(dmin))
        d1 = grad[rows, :].astype(F) + norm_back(dmin * (1.0 + mod[lat, 4 * D : 5 * D]), n, inv)
        t["dx1"][rows, :] = d1
        do = (d1 * mod[lat, 2 * D : 3 * D]).astype(B)
        add_mod(lat, 2, token_sum(d1 * k["o"][rows, :]))
        t["df"][rows, :] = do
        add_db(768, token_sum(do.astype(F)))
        return 0

    lax.fori_loop(0, 4, dmid, 0, unroll=True)
    t["datt"][...] = dot(t["df"][...], main[:, C_PROJ:C_FC1], NT).astype(B)

    t["wide2"][...] = spread(sel, 1, k["att"][...])
    d1 = dot(t["wide2"][...], t["df"][...])
    put(0, slice(0, EXP), slice(QUARTER + 384, 2 * QUARTER), jnp.where(r8 < 4, d1, t["part"][:, 384:]).astype(B))
    t["part2"][...] = d1

    low, high = head_masks()

    def dattend(i, _):
        rows = pl.ds(pl.multiple_of((i // 3) * SEQ, SEQ), SEQ)
        at = (i % 3) * 128
        qs = pl.ds(pl.multiple_of(at, 128), 128)
        ks = pl.ds(pl.multiple_of(D + at, 128), 128)
        vs = pl.ds(pl.multiple_of(2 * D + at, 128), 128)
        q = k["qkv"][rows, qs]
        key = k["qkv"][rows, ks]
        v = k["qkv"][rows, vs]
        da = t["datt"][rows, qs]
        kt = key.T
        dk = dv = None
        dqs = []
        for h, m in enumerate((low, high)):
            qm = q * (m * 0.125)
            dam = da * m
            s = dot(key, qm, NT)
            p = jnp.exp(s - k["lse"][i, h : h + 1, :])
            dp = dot(v, dam, NT)
            ds = (p * (dp - jnp.sum(p * dp, axis=0, keepdims=True))).astype(B)
            v1 = dot(p.astype(B), dam)
            k1 = dot(ds, qm)
            dqs.append(dot(kt[h * HEAD : (h + 1) * HEAD], ds))
            dv = v1 if dv is None else dv + v1
            dk = k1 if dk is None else dk + k1
        t["dqkv"][rows, qs] = (jnp.concatenate(dqs, axis=0).T * 0.125).astype(B)
        t["dqkv"][rows, ks] = dk.astype(B)
        t["dqkv"][rows, vs] = dv.astype(B)
        return 0

    lax.fori_loop(0, 6, dattend, 0, unroll=UNROLL)

    t["wide"][...] = spread(sel, 0, k["ain"][...])
    t["wide2"][...] = spread(sel, 1, k["ain"][...])
    d1 = dot(t["wide2"][...], t["dqkv"][:, QUARTER:])
    d0 = dot(t["wide"][...], t["dqkv"][:, :384])
    put(0, slice(0, EXP), slice(0, 384), jnp.where(r8 < 6, d0, d1).astype(B))
    put(0, slice(0, EXP), slice(QUARTER, QUARTER + 384), jnp.where(r8 < 4, d1, t["part"][:, :384]).astype(B))
    d0 = dot(t["wide"][...], t["dqkv"][:, 384:QUARTER])
    put(0, slice(0, EXP), slice(384, QUARTER), jnp.where(r8 < 6, d0, t["part2"][...]).astype(B))
    ship(0, 0, P_DB0)
    ship(1, 0, P_MOD)

    def bias_sums(i, _):
        rows = pl.ds(pl.multiple_of(i * 128, 128), 128)
        add_db(0, token_sum(t["dqkv"][rows, :D].astype(F)))
        add_db(D, token_sum(t["dqkv"][rows, 2 * D :].astype(F)))
        return 0

    lax.fori_loop(0, 4, bias_sums, 0, unroll=True)

    t["dn"][...] = dot(t["dqkv"][...], main[:, C_QKV:C_PROJ], NT)

    def dlast(i, _):
        rows = pl.ds(pl.multiple_of(i * 128, 128), 128)
        lat = pl.ds(i // 2, 1)
        dain = t["dn"][rows, :]
        n, inv = stats(x[rows, :].astype(F))
        add_mod(lat, 1, token_sum(dain * n))
        add_mod(lat, 0, token_sum(dain))
        back = norm_back(dain * (1.0 + mod[lat, D : 2 * D]), n, inv)
        dx[rows, :] = (t["dx1"][rows, :] + back).astype(B)
        return 0

    lax.fori_loop(0, 4, dlast, 0, unroll=True)

    c = cond[...]
    sig = jax.nn.sigmoid(c)
    act = c * sig
    dm = dmod[...].astype(B).astype(F)
    dc[...] = cond_back(dm.astype(B), g, g_at, selt) * (sig * (1.0 + c * (1.0 - sig)))

    mine = 2 * core
    block = pltpu.roll(dm[:, :1152], mine, 0) + pltpu.roll(dm[:, 1152:], mine + 4, 0)
    for q in range(4):
        rows = slice(q * 128, (q + 1) * 128)
        put(1, rows, slice(P_MOD, P_DB1), jnp.broadcast_to(block[None], (16, 8, 1152)).reshape(128, 1152).astype(B))

    db = t["db"]
    for half, at, first in ((0, P_DB0, 0), (0, P_DB0 + 128, 8), (1, P_DB1, 16)):
        rows = jnp.concatenate([db[:, (first + i) * 128 : (first + i + 1) * 128] for i in range(8)], axis=0)
        put(half, slice(0, EXP), slice(at, at + 128), jnp.broadcast_to(rows[None], (CHIPS, 8, 128)).reshape(EXP, 128).astype(B))

    act = act.astype(B).astype(F)
    both = pltpu.roll(act, mine, 0) + pltpu.roll(act, mine + 4, 0)
    both = jnp.broadcast_to(both[None], (CHIPS, 8, D)).reshape(EXP, D)
    feature = lax.broadcasted_iota(jnp.int32, (1, D), 1)
    device = lax.broadcasted_iota(jnp.int32, (EXP, 1), 0) >> 3
    both = jnp.where(group_of(feature, 6) == device, both, 0.0).astype(B)
    feature = lax.broadcasted_iota(jnp.int32, (D, 1), 0)
    lane = lax.broadcasted_iota(jnp.int32, (1, 128), 1)
    pick = ((feature - 6 * group_of(feature, 6)) == (lane & 7)) & (lane < 16)
    found = dot(both, pick.astype(F).astype(B))
    put(1, slice(0, EXP), slice(P_COND, P_HALF), jnp.where((r8 >> 2) == (lane >> 3), found, 0.0).astype(B))
    ship(0, P_DB0, P_HALF)
    ship(1, P_MOD, P_HALF)
    finish()


KEEP = (
    ("ain", (ROWS, D), B),
    ("qkv", (ROWS, 3 * D), B),
    ("lse", (6, 8, SEQ), F),
    ("att", (ROWS, D), B),
    ("o", (ROWS, D), F),
    ("x1", (ROWS, D), F),
    ("min", (ROWS, D), B),
    ("slope", (ROWS, FF), F),
    ("act", (ROWS, FF), B),
    ("f", (ROWS, D), F),
)
WEIGHTS = (("main", (D, C_MAIN), B), ("bias", (1, C_MAIN), F), ("bias2", (1, D), F), ("fc2", (FF, D), B))
TEMPS = (
    ("dmod", (8, 6 * D), F),
    ("db", (1, 3072), F),
    ("part", (EXP, QUARTER), F),
    ("part2", (EXP, D), F),
    ("wide2", (EXP, ROWS), B),
    ("df", (ROWS, D), B),
    ("dz", (ROWS, FF), B),
    ("wide", (EXP, ROWS), B),
    ("dx1", (ROWS, D), F),
    ("dn", (ROWS, D), F),
    ("datt", (ROWS, D), B),
    ("dqkv", (ROWS, 3 * D), B),
)
MOD = (("mod", (8, 6 * D), F),)


def buffers(table):
    return [pltpu.VMEM(shape, dtype) for _, shape, dtype in table]


def shapes(table):
    return [jax.ShapeDtypeStruct(shape, dtype) for _, shape, dtype in table]


def named(table, refs):
    return {name: ref for (name, _, _), ref in zip(table, refs)}


def fetch(core, blocks, sems, parts):
    own, other = blocks[:4], blocks[4:]

    def each(low, high, act):
        for i in range(4):
            for n, (half, cols, into) in enumerate(parts):
                source = (low, high)[half][i].at[:, cols]
                copy = pltpu.make_async_copy(source, into.at[i * 128 : (i + 1) * 128], sems.at[n * 4 + i])
                act(copy)

    def both(act):
        @pl.when(core == 0)
        def _():
            each(own, other, act)

        @pl.when(core != 0)
        def _():
            each(other, own, act)

    both(lambda copy: copy.start())
    return lambda: both(lambda copy: copy.wait())


def whole_section(g):
    every = slice(0, G_HALF)
    return ((0, every, g.at[:, :G_HALF]), (1, every, g.at[:, G_HALF:]))


def ada_only(g):
    return ((1, slice(G_ADA - G_HALF, G_BIAS - G_HALF), g),)


def sender(core, pack, keep, send, sems):
    started = []

    def start(half, first, last):
        n = len(started)
        cols = slice(first, last)

        def copy(slot, ref):
            return pltpu.make_async_copy(pack.at[slot, :, cols], ref.at[:, cols], sems.at[n])

        mine = copy(0, keep)
        theirs = copy(1, send)
        started.append((half, mine, theirs))

        @pl.when(core == half)
        def _():
            mine.start()

        @pl.when(core != half)
        def _():
            theirs.start()

    def finish():
        for half, mine, theirs in started:

            @pl.when(core == half)
            def _(mine=mine):
                mine.wait()

            @pl.when(core != half)
            def _(theirs=theirs):
                theirs.wait()

    return start, finish


def putter(core, pack):
    def put(half, rows, cols, value):
        slot = core if half == 0 else 1 - core
        pack[slot, rows, cols] = value

    return put


def front_kernel(place, *refs):
    blocks, (x, cond, y), refs = refs[:8], refs[8:11], refs[11:]
    saved = KEEP + WEIGHTS + MOD
    n = len(saved)
    out = named(saved, refs[:n])
    buf = named(saved, refs[n : 2 * n])
    g, low, high, order, sems, save_sems = refs[2 * n :]
    copies = []

    def save(*names):
        for name in names:
            copy = pltpu.make_async_copy(buf[name], out[name], save_sems.at[len(copies)])
            copy.start()
            copies.append(copy)

    wait = fetch(place[0], blocks, sems, whole_section(g))
    gather_selectors(low, place, 0)
    gather_selectors(high, place, 1)
    order_rows(order, place)
    wait()
    ada = unpack(g, low, place, order, buf)
    save("main", "bias", "bias2", "fc2")
    modulate(cond, g, high, ada, buf["mod"])
    save("mod")
    forward(x, buf, buf["mod"], buf, y, save)
    for copy in copies:
        copy.wait()


def turn_kernel(place, *refs):
    blocks, (x, cond, grad, y, dx, dc, keep, send), refs = refs[:8], refs[8:16], refs[16:]
    n_keep, n_w, n_t = len(KEEP), len(WEIGHTS), len(TEMPS)
    k = named(KEEP, refs[:n_keep])
    w = named(WEIGHTS, refs[n_keep : n_keep + n_w])
    t = named(TEMPS, refs[n_keep + n_w : n_keep + n_w + n_t])
    mod, g, sel, low, high, order, pack, sems = refs[n_keep + n_w + n_t :]
    core = place[0]
    wait = fetch(core, blocks, sems, whole_section(g))
    send_selectors(sel)
    gather_selectors(low, place, 0)
    gather_selectors(high, place, 1)
    order_rows(order, place)
    wait()
    ada = unpack(g, low, place, order, w)
    modulate(cond, g, high, ada, mod)
    forward(x, w, mod, k, y)
    backward(core, grad, x, cond, g, G_ADA, sel, high, w, mod, k, t, dx, dc, putter(core, pack), *sender(core, pack, keep, send, sems))


def back_kernel(place, *refs):
    blocks, (x, cond, grad), refs = refs[:8], refs[8:11], refs[11:]
    n_keep, n_w, n_t = len(KEEP), len(WEIGHTS), len(TEMPS)
    k = named(KEEP, refs[:n_keep])
    w = named(WEIGHTS, refs[n_keep : n_keep + n_w])
    mod, dx, dc, keep, send = refs[n_keep + n_w : n_keep + n_w + 5]
    refs = refs[n_keep + n_w + 5 :]
    t = named(TEMPS, refs[:n_t])
    g, sel, high, pack, sems = refs[n_t:]
    core = place[0]
    wait = fetch(core, blocks, sems, ada_only(g))
    send_selectors(sel)
    gather_selectors(high, place, 1)
    wait()
    backward(core, grad, x, cond, g, 0, sel, high, w, mod, k, t, dx, dc, putter(core, pack), *sender(core, pack, keep, send, sems))


VM = pl.BlockSpec(memory_space=pltpu.VMEM)
ANY = pl.BlockSpec(memory_space=pl.ANY)
SM = pl.BlockSpec(memory_space=pltpu.SMEM)
PARAMS = pltpu.CompilerParams(vmem_limit_bytes=60 * 1024 * 1024)
G_BUF = pltpu.VMEM((EXP, G_END), B)
ADA_BUF = pltpu.VMEM((EXP, G_BIAS - G_ADA), B)
SEL_BUF = pltpu.VMEM((4, EXP, D), B)
SELT_BUF = pltpu.VMEM((4, D, EXP), B)
ORDER_BUF = pltpu.VMEM((2, EXP, EXP), B)
SEMS = pltpu.SemaphoreType.DMA((8,))
ROWS_OUT = jax.ShapeDtypeStruct((ROWS, D), B)
COND_OUT = jax.ShapeDtypeStruct((8, D), F)
HALF_OUT = jax.ShapeDtypeStruct((EXP, P_HALF), B)
PACK_BUF = pltpu.VMEM((2, EXP, P_HALF), B)


def cost(units):
    return pl.CostEstimate(flops=units * 2_000_000_000, bytes_accessed=units * 10_000_000, transcendentals=units * 2_000_000)


def front(place, blocks, x, cond):
    outs = [ROWS_OUT] + shapes(KEEP) + shapes(WEIGHTS) + shapes(MOD)
    return pl.pallas_call(
        front_kernel,
        out_shape=outs,
        in_specs=[SM] + [ANY] * 8 + [VM] * 2,
        out_specs=[VM] + [ANY] * (len(outs) - 1),
        scratch_shapes=buffers(KEEP + WEIGHTS + MOD)
        + [G_BUF, SELT_BUF, SELT_BUF, ORDER_BUF, SEMS, pltpu.SemaphoreType.DMA((len(outs) - 1,))],
        compiler_params=PARAMS,
        cost_estimate=cost(1),
        name="front",
    )(place, *blocks, x, cond)


def turn(place, blocks, x, cond, grad):
    return pl.pallas_call(
        turn_kernel,
        out_shape=[ROWS_OUT, ROWS_OUT, COND_OUT, HALF_OUT, HALF_OUT],
        in_specs=[SM] + [ANY] * 8 + [VM] * 3,
        out_specs=[VM] * 3 + [ANY] * 2,
        scratch_shapes=buffers(KEEP) + buffers(WEIGHTS) + buffers(TEMPS) + buffers(MOD) + [G_BUF, SEL_BUF, SELT_BUF, SELT_BUF, ORDER_BUF, PACK_BUF, SEMS],
        compiler_params=PARAMS,
        cost_estimate=cost(3),
        name="turn",
    )(place, *blocks, x, cond, grad)


def back(place, blocks, x, cond, grad, kept):
    return pl.pallas_call(
        back_kernel,
        out_shape=[ROWS_OUT, COND_OUT, HALF_OUT, HALF_OUT],
        in_specs=[SM] + [ANY] * 8 + [VM] * (3 + len(kept)),
        out_specs=[VM] * 2 + [ANY] * 2,
        scratch_shapes=buffers(TEMPS) + [ADA_BUF, SEL_BUF, SELT_BUF, PACK_BUF, SEMS],
        compiler_params=PARAMS,
        cost_estimate=cost(2),
        name="back",
    )(place, *blocks, x, cond, grad, *kept)


def line_up_kernel(w_qkv, w_proj, w_fc1, w_fc2, w_ada, b_qv, b_proj, b_fc1, b_fc2, b_ada, out, main, ada, bias):
    def rows(ref, first, last):
        return ref[:, first:last].astype(F)

    main[0:6, :] = rows(w_qkv, 0, QUARTER)
    main[6:12, :384] = rows(w_qkv, QUARTER, C_PROJ)
    main[6:12, 384:] = rows(w_proj, 0, D)
    main[12:18, :] = rows(w_fc1, 0, QUARTER)
    main[18:24, :] = rows(w_fc1, QUARTER, FF)
    ada[48:56, :] = jnp.zeros((8, 256), F)
    for i in range(9):
        ada[6 * i : 6 * i + 6, :] = rows(w_ada, 256 * i, 256 * i + 256)
    for a in range(3):
        out[:, a * QUARTER : (a + 1) * QUARTER] = main[8 * a : 8 * a + 8, :].astype(B)
        out[:, G_FC2 + a * D : G_FC2 + (a + 1) * D] = w_fc2[8 * a : 8 * a + 8, :]
    for a in range(7):
        out[:, G_ADA + a * 256 : G_ADA + (a + 1) * 256] = ada[8 * a : 8 * a + 8, :].astype(B)
    bias[...] = jnp.zeros((8, 128), F)
    for ref, (lane, width) in zip((b_qv, b_proj, b_fc1, b_fc2, b_ada), BIASES):
        bias[0:1, lane : lane + width] = ref[...].astype(F)
    out[:, G_BIAS:G_END] = bias[...].astype(B)


def line_up(w_qkv, b_qv, w_proj, b_proj, w_fc1, b_fc1, w_fc2, b_fc2, w_ada, b_ada):
    biases = [b.reshape(1, -1) for b in (b_qv, b_proj, b_fc1, b_fc2, b_ada)]
    return pl.pallas_call(
        line_up_kernel,
        out_shape=jax.ShapeDtypeStruct((8, G_END), B),
        in_specs=[VM] * 10,
        out_specs=VM,
        scratch_shapes=[pltpu.VMEM((24, QUARTER), F), pltpu.VMEM((56, 256), F), pltpu.VMEM((8, 128), F)],
        name="line_up",
    )(w_qkv, w_proj, w_fc1, w_fc2, w_ada, *biases)


def swap(x):
    return lax.ppermute(x, "pipe", [(0, 1), (1, 0)])


def gather_stage(block, stage):
    def behind(by):
        pairs = []
        for core in range(2):
            stride = STRIDES[STAGES[core][stage]]
            for i in range(CHIPS):
                at = (i // stride) % 4
                pairs.append((core * CHIPS + i, core * CHIPS + i + ((at + by) % 4 - at) * stride))
        return lax.ppermute(block, ("pipe", "shard"), pairs)

    return [block] + [behind(by) for by in (1, 2, 3)]


def scatter(block):
    return lax.all_to_all(block.reshape(CHIPS, 8, P_HALF), "shard", 0, 0, tiled=True)


def shards(latents, conditions, cotangent, w_qkv, b_qv, w_proj, b_proj, w_fc1, b_fc1, w_fc2, b_fc2, w_ada, b_ada):
    p = lax.axis_index("pipe")
    j = lax.axis_index("shard")
    first = p == 0
    place = jnp.stack([p, j >> 4, (j >> 2) & 3, j & 3]).astype(jnp.int32)
    block = line_up(w_qkv[0], b_qv[0], w_proj[0], b_proj[0], w_fc1[0], b_fc1[0], w_fc2[0], b_fc2[0], w_ada[0], b_ada[0])
    block_other = swap(block)
    low = jnp.where(first, block[:, :G_HALF], block_other[:, G_HALF:])
    high = jnp.where(first, block_other[:, :G_HALF], block[:, G_HALF:])
    both = jnp.concatenate([low, high], axis=1)
    for stage in range(2):
        both = jnp.concatenate(gather_stage(both, stage), axis=0)
    own0 = gather_stage(both[:, :G_HALF], 2)
    other0 = [swap(block) for block in own0]
    high, *own0 = lax.optimization_barrier((both[:, G_HALF:], *own0))
    blocks0 = own0 + other0
    own1 = gather_stage(high, 2)
    x = lax.dynamic_index_in_dim(latents, p, 0, keepdims=False).reshape(ROWS, D)
    cot = lax.dynamic_index_in_dim(cotangent, p, 0, keepdims=False).reshape(ROWS, D)
    cond = lax.dynamic_index_in_dim(conditions, p, 0, keepdims=False).astype(F)
    cond = jnp.concatenate([cond, jnp.zeros((6, D), F)], axis=0)

    h, *kept = front(place, blocks0, x, cond)
    h, *own1 = lax.optimization_barrier((h, *own1))
    blocks1 = own1 + [swap(block) for block in own1]
    y, dx1, dc1, keep1, send1 = turn(place, blocks1, h, cond, cot)
    parts1 = scatter(keep1 + swap(send1))
    dx0, dc0, keep0, send0 = back(place, blocks0, x, cond, dx1, kept)
    parts1, send0 = lax.optimization_barrier((parts1, send0))
    parts0 = scatter(keep0 + swap(send0))

    def pair(for_first, for_second):
        keep = jnp.where(first, for_first, for_second)
        came = swap(jnp.where(first, for_second, for_first))
        both = jnp.where(first, jnp.stack([keep, came]), jnp.stack([came, keep]))
        return both.reshape(1, 2, 2, SEQ, D)

    section_outputs = pair(h, y)
    input_grads = pair(dx0, dx1)
    dc = (dc0 + dc1)[:2]
    dc_other = swap(dc)
    cond_grad = jnp.where(first, jnp.stack([dc, dc_other]), jnp.stack([dc_other, dc]))

    parts0, section_outputs, input_grads, cond_grad = lax.optimization_barrier(
        (parts0, section_outputs, input_grads, cond_grad)
    )

    def reduced(parts):
        lot = jnp.sum(parts.astype(F), axis=0)
        flat = parts.reshape(EXP, P_HALF)
        ada = lax.dot_general(
            flat[:, P_COND : P_COND + 16], flat[:, P_MOD:P_DB1], (((0,), (0,)), ((), ())), preferred_element_type=F
        )
        return jnp.concatenate([lot, ada[:8], ada[8:]], axis=1)

    lot0 = reduced(parts0)
    lot1 = reduced(parts1)
    kept_half = jnp.where(first, lot0, lot1)
    came_half = swap(jnp.where(first, lot1, lot0))
    low = jnp.where(first, kept_half, came_half)
    high = jnp.where(first, came_half, kept_half)

    rows = jnp.concatenate([low[:, a * QUARTER : (a + 1) * QUARTER] for a in range(3)], axis=0)
    quarters = [rows[6 * q : 6 * q + 6] for q in range(4)]
    db = jnp.concatenate([low[:, P_DB0 : P_DB0 + 128], low[:, P_DB0 + 128 : P_HALF], high[:, P_DB1:P_COND]], axis=0).reshape(-1)
    sums = high[:, P_MOD:P_DB1]
    db_ada = jnp.concatenate([sums[:4].sum(axis=0), sums[4:].sum(axis=0)])

    def slice_of(line, at, width):
        return lax.dynamic_slice(line, (at + width * j,), (width,))

    outs = (
        jnp.concatenate([quarters[0], quarters[1][:, :384]], axis=1),
        slice_of(db, 0, 12),
        quarters[1][:, 384:],
        slice_of(db, 768, 6),
        jnp.concatenate([quarters[2], quarters[3]], axis=1),
        slice_of(db, 1152, 24),
        jnp.concatenate([high[:, a * D : (a + 1) * D] for a in range(3)], axis=0),
        slice_of(db, 2688, 6),
        jnp.concatenate([high[:6, P_HALF : P_HALF + 1152], high[:6, P_HALF + 1152 :]], axis=1),
        slice_of(db_ada, 0, 36),
    )
    return (section_outputs, input_grads, cond_grad) + tuple(o[None] for o in outs)


def solution(mesh):
    rows = P(None, "shard", None, None)
    wide = P("pipe", "shard", None)
    thin = P("pipe", "shard")
    both = P("pipe", None, "shard", None, None)
    pairs = (wide, thin) * 5
    return jax.shard_map(
        shards,
        mesh=mesh,
        in_specs=(rows, P(None, "shard", None), rows) + pairs,
        out_specs=(both, both, P(None, "shard", None)) + pairs,
        check_vma=False,
    )
```

```python
import functools

import jax
import jax.numpy as jnp
from jax import lax
from jax.experimental import pallas as pl
from jax.experimental.pallas import tpu as pltpu
from jax.sharding import PartitionSpec as P

F = jnp.float32
B = jnp.bfloat16
D = 384
HEADS = 6
HEAD = 64
FF = 1536
SEQ = 256
EPS = 1e-06
CHIPS = 64
ROWS = 512
EXP = 512

C_QKV, C_PROJ, C_FC1, C_MAIN = 0, 1152, 1536, 3072
QUARTER = 768

G_FC2, G_ADA, G_BIAS, G_END = 2304, 3456, 5248, 5376
G_HALF = 2688
BIASES = ((0, 12), (12, 6), (18, 24), (42, 6), (48, 36))

P_HALF = 2432
P_MAIN = 2304
P_MOD, P_COND = 1152, 2304
P_BIAS = P_COND + 16
SHIFTS = (0, 6, 4, 2)

K0 = 0.7978845608028654
K1 = 0.044715

UNROLL = 6
NN = (1, 0)
NT = (1, 1)
TN = (0, 0)


def dot(a, b, dims=NN):
    return lax.dot_general(a, b, (((dims[0],), (dims[1],)), ((), ())), preferred_element_type=F)


STRIDES = {"y": 16, "x": 4, "z": 1}
STAGES = (("x", "y", "z"), ("y", "z", "x"))


def owner(block, place, core):
    total = 0
    for stage, axis in enumerate(STAGES[core]):
        here = place[1 + "yxz".index(axis)]
        behind = (block >> (2 * stage)) & 3
        total = total + STRIDES[axis] * ((here - behind) & 3)
    return total


def targets(shape, dim, shift, owner_of):
    at = lax.broadcasted_iota(jnp.int32, shape, dim)
    r = ((at & 7) + (8 - shift)) & 7
    return jnp.where(r < 6, owner_of(at >> 3) * 6 + r, -1)


def send_selectors(sel):
    col = lax.broadcasted_iota(jnp.int32, (1, D), 1)
    for i, shift in enumerate(SHIFTS):
        sel[i] = (targets((EXP, 1), 0, shift, lambda block: block) == col).astype(F).astype(B)


def gather_selectors(selt, place, core):
    row = lax.broadcasted_iota(jnp.int32, (D, 1), 0)
    for i, shift in enumerate(SHIFTS):
        found = targets((1, EXP), 1, shift, lambda block: owner(block, place, core))
        selt[i] = (row == found).astype(F).astype(B)


def row_order(place, core):
    at = lax.broadcasted_iota(jnp.int32, (1, EXP), 1)
    found = owner(at >> 3, place, core) * 8 + (at & 7)
    return (lax.broadcasted_iota(jnp.int32, (EXP, 1), 0) == found).astype(F).astype(B)


def group_of(n, width):
    return jnp.floor((n.astype(F) + 0.5) * (1.0 / width)).astype(jnp.int32)


def natural_bias(gb, lane, width):
    n = CHIPS * width
    at = lax.broadcasted_iota(jnp.int32, (1, n), 1)
    owner = group_of(at, width)
    spot = at - owner * width + lane
    pick = (lax.broadcasted_iota(jnp.int32, (128, 1), 0) == spot).astype(F).astype(B)
    wide = dot(gb, pick)
    return jnp.sum(jnp.where(lax.broadcasted_iota(jnp.int32, (CHIPS, 1), 0) == owner, wide, 0.0), axis=0, keepdims=True)


def device_lanes(row, lane, width):
    at = lax.broadcasted_iota(jnp.int32, (1, row.shape[1]), 1)
    owned_by = group_of(at, width)
    spot = at - owned_by * width + lane
    own = jnp.where(lax.broadcasted_iota(jnp.int32, (CHIPS, 1), 0) == owned_by, row, 0.0).astype(B)
    pick = (lax.broadcasted_iota(jnp.int32, (128, 1), 0) == spot).astype(F).astype(B)
    return dot(own, pick, NT)


def order_rows(order, place):
    for core in range(2):
        order[core] = row_order(place, core)


def tile_row(shape, dim):
    return lax.broadcasted_iota(jnp.int32, shape, dim) & 7


def stats(v):
    centre = v - jnp.mean(v, axis=-1, keepdims=True)
    inv = lax.rsqrt(jnp.mean(centre * centre, axis=-1, keepdims=True) + EPS)
    return centre * inv, inv


def norm_back(g, n, inv):
    mg = jnp.mean(g, axis=-1, keepdims=True)
    mgn = jnp.mean(g * n, axis=-1, keepdims=True)
    return inv * (g - mg - n * mgn)


def head_masks():
    lane = lax.broadcasted_iota(jnp.int32, (1, 128), 1)
    low = (lane < HEAD).astype(F)
    return low.astype(B), (1.0 - low).astype(B)


def unpack(g, selt, place, order, w):
    r8 = tile_row((EXP, 1), 0)

    def piece(a, c):
        return g[:, a * QUARTER + c : a * QUARTER + c + 384]

    def merge(edge, a, c):
        return jnp.where(r8 >= edge, piece(a, c).astype(F), piece(a + 1, c).astype(F)).astype(B)

    for c in (0, 384):
        w["main"][:, c : c + 384] = dot(selt[0], piece(0, c)).astype(B)
        w["main"][:, QUARTER + c : QUARTER + c + 384] = dot(selt[1], merge(6, 0, c)).astype(B)
        w["main"][:, 2 * QUARTER + c : 2 * QUARTER + c + 384] = dot(selt[2], merge(4, 1, c)).astype(B)
        w["main"][:, 3 * QUARTER + c : 3 * QUARTER + c + 384] = dot(selt[3], piece(2, c)).astype(B)

    lane = lax.broadcasted_iota(jnp.int32, (1, EXP), 1)
    from_device = jnp.where((lane & 7) == 0, owner(lane >> 3, place, 1), -1)
    lead = (lax.broadcasted_iota(jnp.int32, (CHIPS, 1), 0) == from_device).astype(F).astype(B)
    gb = dot(lead, g[:, G_BIAS:G_END]).astype(B)
    qv, proj, fc1, fc2, ada = (natural_bias(gb, lane, width) for lane, width in BIASES)
    w["bias"][:, :D] = qv[:, :D]
    w["bias"][:, D : 2 * D] = jnp.zeros((1, D), F)
    w["bias"][:, 2 * D : C_PROJ] = qv[:, D:]
    w["bias"][:, C_PROJ:C_FC1] = proj
    w["bias"][:, C_FC1:C_MAIN] = fc1
    w["bias2"][...] = fc2

    for i in range(4):
        rows = slice(i * 128, (i + 1) * 128)
        parts = [
            dot(order[min(a, 1), rows], g[:, G_FC2 + a * D : G_FC2 + (a + 1) * D]).reshape(16, 8, D) for a in range(3)
        ]
        w["fc2"][i * D : (i + 1) * D, :] = jnp.concatenate(parts, axis=1).reshape(D, D).astype(B)
    return ada


def ada_groups():
    return [(i % 4, (6 * i) // 8, SHIFTS[i % 4] in (6, 4)) for i in range(9)]


def modulate(cond, g, selt, ada, mod):
    c = cond[...]
    act = (c * jax.nn.sigmoid(c)).astype(B)
    r8 = tile_row((1, EXP), 1)
    wides = [dot(act, selt[i]) for i in range(4)]
    for n, (i, a, more) in enumerate(ada_groups()):
        at = G_ADA + a * 256
        first = jnp.where(r8 >= SHIFTS[i], wides[i], 0.0).astype(B)
        part = dot(first, g[:, at : at + 256])
        if more:
            part = part + dot(jnp.where(r8 < SHIFTS[i], wides[i], 0.0).astype(B), g[:, at + 256 : at + 512])
        mod[:, n * 256 : (n + 1) * 256] = part + ada[:, n * 256 : (n + 1) * 256]


def cond_back(dm, g, g_at, selt):
    r8 = tile_row((EXP, 1), 0)
    sums = [jnp.zeros((EXP, 8), F)] * 4
    for n, (i, a, more) in enumerate(ada_groups()):
        at = g_at + a * 256
        piece = dm[:, n * 256 : (n + 1) * 256]
        sums[i] = sums[i] + jnp.where(r8 >= SHIFTS[i], dot(g[:, at : at + 256], piece, NT), 0.0)
        if more:
            sums[i] = sums[i] + jnp.where(r8 < SHIFTS[i], dot(g[:, at + 256 : at + 512], piece, NT), 0.0)
    total = jnp.zeros((8, D), F)
    for i in range(4):
        rest = sums[i].T
        for _ in range(3):
            level = rest.astype(B)
            rest = rest - level.astype(F)
            total = total + dot(level, selt[i], NT)
    return total


def forward(x, w, mod, k, y, save=lambda *names: None):
    main, bias, fc2 = w["main"], w["bias"], w["fc2"]

    def ln_in(i, _):
        rows = pl.ds(pl.multiple_of(i * 128, 128), 128)
        lat = pl.ds(i // 2, 1)
        n, _ = stats(x[rows, :].astype(F))
        k["ain"][rows, :] = (n * (1.0 + mod[lat, D : 2 * D]) + mod[lat, :D]).astype(B)
        return 0

    lax.fori_loop(0, 4, ln_in, 0, unroll=True)

    for c in range(3):
        cs = slice(c * D, (c + 1) * D)
        k["qkv"][:, cs] = (dot(k["ain"][...], main[:, cs]) + bias[:, cs]).astype(B)

    low, high = head_masks()

    def attend(i, _):
        rows = pl.ds(pl.multiple_of((i // 3) * SEQ, SEQ), SEQ)
        at = (i % 3) * 128
        q = k["qkv"][rows, pl.ds(pl.multiple_of(at, 128), 128)]
        key = k["qkv"][rows, pl.ds(pl.multiple_of(D + at, 128), 128)]
        vt = k["qkv"][rows, pl.ds(pl.multiple_of(2 * D + at, 128), 128)].T
        heads = []
        for h, m in enumerate((low, high)):
            s = dot(key, q * (m * 0.125), NT)
            top = jnp.max(s, axis=0, keepdims=True)
            e = jnp.exp(s - top)
            t = jnp.sum(e, axis=0, keepdims=True)
            p = (e * (1.0 / t)).astype(B)
            k["lse"][i, h : h + 1, :] = top + jnp.log(t)
            heads.append(dot(vt[h * HEAD : (h + 1) * HEAD], p))
        k["att"][rows, pl.ds(pl.multiple_of(at, 128), 128)] = jnp.concatenate(heads, axis=0).T.astype(B)
        return 0

    lax.fori_loop(0, 6, attend, 0, unroll=UNROLL)
    save("ain", "qkv", "lse", "att")
    k["o"][...] = dot(k["att"][...], main[:, C_PROJ:C_FC1]) + bias[:, C_PROJ:C_FC1]

    def mid(i, _):
        rows = pl.ds(pl.multiple_of(i * 128, 128), 128)
        lat = pl.ds(i // 2, 1)
        x1 = x[rows, :].astype(F) + mod[lat, 2 * D : 3 * D] * k["o"][rows, :]
        k["x1"][rows, :] = x1
        n, _ = stats(x1)
        k["min"][rows, :] = (n * (1.0 + mod[lat, 4 * D : 5 * D]) + mod[lat, 3 * D : 4 * D]).astype(B)
        return 0

    lax.fori_loop(0, 4, mid, 0, unroll=True)

    def mlp(i, _):
        at = pl.multiple_of(i * 256, 256)
        cs = pl.ds(at, 256)
        ws = pl.ds(pl.multiple_of(C_FC1 + at, 256), 256)
        z = dot(k["min"][...], main[:, ws]) + bias[:, ws]
        zz = z * z
        t = jnp.tanh(z * (K0 + K0 * K1 * zz))
        half = 0.5 + 0.5 * t
        k["act"][:, cs] = (z * half).astype(B)
        k["slope"][:, cs] = half + (0.5 * z) * (1.0 - t * t) * (K0 + 3.0 * K0 * K1 * zz)
        return 0

    lax.fori_loop(0, 6, mlp, 0, unroll=True)

    save("o", "x1", "min", "slope", "act")
    k["f"][...] = dot(k["act"][...], fc2[...]) + w["bias2"][...]

    def out(i, _):
        rows = pl.ds(pl.multiple_of(i * 128, 128), 128)
        lat = pl.ds(i // 2, 1)
        y[rows, :] = (k["x1"][rows, :] + mod[lat, 5 * D : 6 * D] * k["f"][rows, :]).astype(B)
        return 0

    save("f")
    lax.fori_loop(0, 4, out, 0, unroll=True)


def token_sum(v):
    return jnp.sum(v, axis=0, keepdims=True)


def spread(sel, i, v):
    return dot(sel[i], v, NT).astype(B)


def backward(core, grad, x, cond, g, g_at, sel, selt, w, mod, k, t, dx, dc, put, ship, finish):
    main, fc2 = w["main"], w["fc2"]
    dmod = t["dmod"]
    dmod[...] = jnp.zeros_like(dmod)

    def add_mod(lat, piece, v):
        cs = slice(piece * D, (piece + 1) * D)
        dmod[lat, cs] = dmod[lat, cs] + v

    t["db"][...] = jnp.zeros_like(t["db"])
    r8 = tile_row((EXP, 1), 0)

    def add_db(at, v):
        t["db"][:, at : at + v.shape[1]] = t["db"][:, at : at + v.shape[1]] + v


    def start(i, _):
        rows = pl.ds(pl.multiple_of(i * 128, 128), 128)
        lat = pl.ds(i // 2, 1)
        gr = grad[rows, :].astype(F)
        df = (gr * mod[lat, 5 * D : 6 * D]).astype(B)
        t["df"][rows, :] = df
        add_mod(lat, 5, token_sum(gr * k["f"][rows, :]))
        add_db(2688, token_sum(df.astype(F)))
        return 0

    lax.fori_loop(0, 4, start, 0, unroll=True)

    def dmlp(i, _):
        cs = pl.ds(pl.multiple_of(i * 256, 256), 256)
        da = dot(t["df"][...], fc2[cs, :], NT)
        dz = (da * k["slope"][:, cs]).astype(B)
        t["dz"][:, cs] = dz
        ds = pl.ds(pl.multiple_of(1152 + i * 256, 128), 256)
        t["db"][:, ds] = token_sum(dz.astype(F))
        return 0

    lax.fori_loop(0, 6, dmlp, 0, unroll=True)

    t["wide2"][...] = spread(sel, 2, k["min"][...])
    t["wide"][...] = spread(sel, 3, k["min"][...])
    for c in range(0, QUARTER, 256):
        d2 = dot(t["wide2"][...], t["dz"][:, c : c + 256])
        d3 = dot(t["wide"][...], t["dz"][:, QUARTER + c : QUARTER + c + 256])
        put(0, slice(0, EXP), slice(2 * QUARTER + c, 2 * QUARTER + c + 256), jnp.where(r8 < 2, d2, d3).astype(B))
        t["part"][:, c : c + 256] = d2

    for c in range(4):
        part = dot(k["act"][:, c * D : (c + 1) * D], t["df"][...], TN).reshape(16, 24, D)
        for a in range(3):
            put(
                1,
                slice(c * 128, (c + 1) * 128),
                slice(a * D, (a + 1) * D),
                part[:, 8 * a : 8 * a + 8, :].reshape(128, D).astype(B),
            )

    t["dn"][...] = dot(t["dz"][...], main[:, C_FC1:C_MAIN], NT)

    def dmid(i, _):
        rows = pl.ds(pl.multiple_of(i * 128, 128), 128)
        lat = pl.ds(i // 2, 1)
        dmin = t["dn"][rows, :]
        n, inv = stats(k["x1"][rows, :])
        add_mod(lat, 4, token_sum(dmin * n))
        add_mod(lat, 3, token_sum(dmin))
        d1 = grad[rows, :].astype(F) + norm_back(dmin * (1.0 + mod[lat, 4 * D : 5 * D]), n, inv)
        t["dx1"][rows, :] = d1
        do = (d1 * mod[lat, 2 * D : 3 * D]).astype(B)
        add_mod(lat, 2, token_sum(d1 * k["o"][rows, :]))
        t["df"][rows, :] = do
        add_db(768, token_sum(do.astype(F)))
        return 0

    lax.fori_loop(0, 4, dmid, 0, unroll=True)
    t["datt"][...] = dot(t["df"][...], main[:, C_PROJ:C_FC1], NT).astype(B)

    t["wide2"][...] = spread(sel, 1, k["att"][...])
    d1 = dot(t["wide2"][...], t["df"][...])
    put(0, slice(0, EXP), slice(QUARTER + 384, 2 * QUARTER), jnp.where(r8 < 4, d1, t["part"][:, 384:]).astype(B))
    t["part2"][...] = d1

    low, high = head_masks()

    def dattend(i, _):
        rows = pl.ds(pl.multiple_of((i // 3) * SEQ, SEQ), SEQ)
        at = (i % 3) * 128
        qs = pl.ds(pl.multiple_of(at, 128), 128)
        ks = pl.ds(pl.multiple_of(D + at, 128), 128)
        vs = pl.ds(pl.multiple_of(2 * D + at, 128), 128)
        q = k["qkv"][rows, qs]
        key = k["qkv"][rows, ks]
        v = k["qkv"][rows, vs]
        da = t["datt"][rows, qs]
        kt = key.T
        dk = dv = None
        dqs = []
        for h, m in enumerate((low, high)):
            qm = q * (m * 0.125)
            dam = da * m
            s = dot(key, qm, NT)
            p = jnp.exp(s - k["lse"][i, h : h + 1, :])
            dp = dot(v, dam, NT)
            ds = (p * (dp - jnp.sum(p * dp, axis=0, keepdims=True))).astype(B)
            v1 = dot(p.astype(B), dam)
            k1 = dot(ds, qm)
            dqs.append(dot(kt[h * HEAD : (h + 1) * HEAD], ds))
            dv = v1 if dv is None else dv + v1
            dk = k1 if dk is None else dk + k1
        t["dqkv"][rows, qs] = (jnp.concatenate(dqs, axis=0).T * 0.125).astype(B)
        t["dqkv"][rows, ks] = dk.astype(B)
        t["dqkv"][rows, vs] = dv.astype(B)
        return 0

    lax.fori_loop(0, 6, dattend, 0, unroll=UNROLL)

    t["wide"][...] = spread(sel, 0, k["ain"][...])
    t["wide2"][...] = spread(sel, 1, k["ain"][...])
    d1 = dot(t["wide2"][...], t["dqkv"][:, QUARTER:])
    d0 = dot(t["wide"][...], t["dqkv"][:, :384])
    put(0, slice(0, EXP), slice(0, 384), jnp.where(r8 < 6, d0, d1).astype(B))
    put(0, slice(0, EXP), slice(QUARTER, QUARTER + 384), jnp.where(r8 < 4, d1, t["part"][:, :384]).astype(B))
    d0 = dot(t["wide"][...], t["dqkv"][:, 384:QUARTER])
    put(0, slice(0, EXP), slice(P_MAIN, P_HALF), jnp.zeros((EXP, P_HALF - P_MAIN), B))
    put(0, slice(0, EXP), slice(384, QUARTER), jnp.where(r8 < 6, d0, t["part2"][...]).astype(B))
    ship(0, 0, P_HALF)
    ship(1, 0, P_MOD)

    def bias_sums(i, _):
        rows = pl.ds(pl.multiple_of(i * 128, 128), 128)
        add_db(0, token_sum(t["dqkv"][rows, :D].astype(F)))
        add_db(D, token_sum(t["dqkv"][rows, 2 * D :].astype(F)))
        return 0

    lax.fori_loop(0, 4, bias_sums, 0, unroll=True)

    t["dn"][...] = dot(t["dqkv"][...], main[:, C_QKV:C_PROJ], NT)

    def dlast(i, _):
        rows = pl.ds(pl.multiple_of(i * 128, 128), 128)
        lat = pl.ds(i // 2, 1)
        dain = t["dn"][rows, :]
        n, inv = stats(x[rows, :].astype(F))
        add_mod(lat, 1, token_sum(dain * n))
        add_mod(lat, 0, token_sum(dain))
        back = norm_back(dain * (1.0 + mod[lat, D : 2 * D]), n, inv)
        dx[rows, :] = (t["dx1"][rows, :] + back).astype(B)
        return 0

    lax.fori_loop(0, 4, dlast, 0, unroll=True)

    c = cond[...]
    sig = jax.nn.sigmoid(c)
    act = c * sig
    dm = dmod[...].astype(B).astype(F)
    dc[...] = cond_back(dm.astype(B), g, g_at, selt) * (sig * (1.0 + c * (1.0 - sig)))

    mine = 2 * core
    block = pltpu.roll(dm[:, :1152], mine, 0) + pltpu.roll(dm[:, 1152:], mine + 4, 0)
    for q in range(4):
        rows = slice(q * 128, (q + 1) * 128)
        put(1, rows, slice(P_MOD, P_COND), jnp.broadcast_to(block[None], (16, 8, 1152)).reshape(128, 1152).astype(B))

    db = t["db"]
    sums = (db[:, :768], db[:, 768:1152], db[:, 1152:2688], db[:, 2688:], jnp.sum(dm, axis=0, keepdims=True))
    lanes = jnp.zeros((CHIPS, 128), F)
    for row, (at, width) in zip(sums, BIASES):
        lanes = lanes + device_lanes(row, at + 16, width)
    lanes = jnp.broadcast_to(lanes.reshape(CHIPS, 1, 128), (CHIPS, 8, 128)).reshape(EXP, 128)

    act = act.astype(B).astype(F)
    both = pltpu.roll(act, mine, 0) + pltpu.roll(act, mine + 4, 0)
    both = jnp.broadcast_to(both[None], (CHIPS, 8, D)).reshape(EXP, D)
    feature = lax.broadcasted_iota(jnp.int32, (1, D), 1)
    device = lax.broadcasted_iota(jnp.int32, (EXP, 1), 0) >> 3
    both = jnp.where(group_of(feature, 6) == device, both, 0.0).astype(B)
    feature = lax.broadcasted_iota(jnp.int32, (D, 1), 0)
    lane = lax.broadcasted_iota(jnp.int32, (1, 128), 1)
    pick = ((feature - 6 * group_of(feature, 6)) == (lane & 7)) & (lane < 16)
    found = dot(both, pick.astype(F).astype(B))
    put(1, slice(0, EXP), slice(P_COND, P_HALF), (jnp.where((r8 >> 2) == (lane >> 3), found, 0.0) + jnp.where(r8 == 0, lanes, 0.0)).astype(B))
    ship(1, P_MOD, P_HALF)
    finish()


KEEP = (
    ("ain", (ROWS, D), B),
    ("qkv", (ROWS, 3 * D), B),
    ("lse", (6, 8, SEQ), F),
    ("att", (ROWS, D), B),
    ("o", (ROWS, D), F),
    ("x1", (ROWS, D), F),
    ("min", (ROWS, D), B),
    ("slope", (ROWS, FF), F),
    ("act", (ROWS, FF), B),
    ("f", (ROWS, D), F),
)
WEIGHTS = (("main", (D, C_MAIN), B), ("bias", (1, C_MAIN), F), ("bias2", (1, D), F), ("fc2", (FF, D), B))
TEMPS = (
    ("dmod", (8, 6 * D), F),
    ("db", (1, 3072), F),
    ("part", (EXP, QUARTER), F),
    ("part2", (EXP, D), F),
    ("wide2", (EXP, ROWS), B),
    ("df", (ROWS, D), B),
    ("dz", (ROWS, FF), B),
    ("wide", (EXP, ROWS), B),
    ("dx1", (ROWS, D), F),
    ("dn", (ROWS, D), F),
    ("datt", (ROWS, D), B),
    ("dqkv", (ROWS, 3 * D), B),
)
MOD = (("mod", (8, 6 * D), F),)


def buffers(table):
    return [pltpu.VMEM(shape, dtype) for _, shape, dtype in table]


def shapes(table):
    return [jax.ShapeDtypeStruct(shape, dtype) for _, shape, dtype in table]


def named(table, refs):
    return {name: ref for (name, _, _), ref in zip(table, refs)}


def fetch(core, blocks, sems, parts):
    own, other = blocks[:4], blocks[4:]

    def each(low, high, act):
        for i in range(4):
            for n, (half, cols, into) in enumerate(parts):
                source = (low, high)[half][i].at[:, cols]
                copy = pltpu.make_async_copy(source, into.at[i * 128 : (i + 1) * 128], sems.at[n * 4 + i])
                act(copy)

    def both(act):
        @pl.when(core == 0)
        def _():
            each(own, other, act)

        @pl.when(core != 0)
        def _():
            each(other, own, act)

    both(lambda copy: copy.start())
    return lambda: both(lambda copy: copy.wait())


def whole_section(g):
    every = slice(0, G_HALF)
    return ((0, every, g.at[:, :G_HALF]), (1, every, g.at[:, G_HALF:]))


def ada_only(g):
    return ((1, slice(G_ADA - G_HALF, G_BIAS - G_HALF), g),)


def sender(core, pack, keep, send, sems):
    started = []

    def start(half, first, last):
        n = len(started)
        cols = slice(first, last)

        def copy(slot, ref):
            return pltpu.make_async_copy(pack.at[slot, :, cols], ref.at[:, cols], sems.at[n])

        mine = copy(0, keep)
        theirs = copy(1, send)
        started.append((half, mine, theirs))

        @pl.when(core == half)
        def _():
            mine.start()

        @pl.when(core != half)
        def _():
            theirs.start()

    def finish():
        for half, mine, theirs in started:

            @pl.when(core == half)
            def _(mine=mine):
                mine.wait()

            @pl.when(core != half)
            def _(theirs=theirs):
                theirs.wait()

    return start, finish


def putter(core, pack):
    def put(half, rows, cols, value):
        slot = core if half == 0 else 1 - core
        pack[slot, rows, cols] = value

    return put


def front_kernel(place, *refs):
    blocks, (x, cond, y), refs = refs[:8], refs[8:11], refs[11:]
    saved = KEEP + WEIGHTS + MOD
    n = len(saved)
    out = named(saved, refs[:n])
    buf = named(saved, refs[n : 2 * n])
    g, low, high, order, sems, save_sems = refs[2 * n :]
    copies = []

    def save(*names):
        for name in names:
            copy = pltpu.make_async_copy(buf[name], out[name], save_sems.at[len(copies)])
            copy.start()
            copies.append(copy)

    wait = fetch(place[0], blocks, sems, whole_section(g))
    gather_selectors(low, place, 0)
    gather_selectors(high, place, 1)
    order_rows(order, place)
    wait()
    ada = unpack(g, low, place, order, buf)
    save("main", "bias", "bias2", "fc2")
    modulate(cond, g, high, ada, buf["mod"])
    save("mod")
    forward(x, buf, buf["mod"], buf, y, save)
    for copy in copies:
        copy.wait()


def turn_kernel(place, *refs):
    blocks, (x, cond, grad, y, dx, dc, keep, send), refs = refs[:8], refs[8:16], refs[16:]
    n_keep, n_w, n_t = len(KEEP), len(WEIGHTS), len(TEMPS)
    k = named(KEEP, refs[:n_keep])
    w = named(WEIGHTS, refs[n_keep : n_keep + n_w])
    t = named(TEMPS, refs[n_keep + n_w : n_keep + n_w + n_t])
    mod, g, sel, low, high, order, pack, sems = refs[n_keep + n_w + n_t :]
    core = place[0]
    wait = fetch(core, blocks, sems, whole_section(g))
    send_selectors(sel)
    gather_selectors(low, place, 0)
    gather_selectors(high, place, 1)
    order_rows(order, place)
    wait()
    ada = unpack(g, low, place, order, w)
    modulate(cond, g, high, ada, mod)
    forward(x, w, mod, k, y)
    backward(core, grad, x, cond, g, G_ADA, sel, high, w, mod, k, t, dx, dc, putter(core, pack), *sender(core, pack, keep, send, sems))


def back_kernel(place, *refs):
    blocks, (x, cond, grad), refs = refs[:8], refs[8:11], refs[11:]
    n_keep, n_w, n_t = len(KEEP), len(WEIGHTS), len(TEMPS)
    k = named(KEEP, refs[:n_keep])
    w = named(WEIGHTS, refs[n_keep : n_keep + n_w])
    mod, dx, dc, keep, send = refs[n_keep + n_w : n_keep + n_w + 5]
    refs = refs[n_keep + n_w + 5 :]
    t = named(TEMPS, refs[:n_t])
    g, sel, high, pack, sems = refs[n_t:]
    core = place[0]
    wait = fetch(core, blocks, sems, ada_only(g))
    send_selectors(sel)
    gather_selectors(high, place, 1)
    wait()
    backward(core, grad, x, cond, g, 0, sel, high, w, mod, k, t, dx, dc, putter(core, pack), *sender(core, pack, keep, send, sems))


VM = pl.BlockSpec(memory_space=pltpu.VMEM)
ANY = pl.BlockSpec(memory_space=pl.ANY)
SM = pl.BlockSpec(memory_space=pltpu.SMEM)
PARAMS = pltpu.CompilerParams(vmem_limit_bytes=60 * 1024 * 1024)
G_BUF = pltpu.VMEM((EXP, G_END), B)
ADA_BUF = pltpu.VMEM((EXP, G_BIAS - G_ADA), B)
SEL_BUF = pltpu.VMEM((4, EXP, D), B)
SELT_BUF = pltpu.VMEM((4, D, EXP), B)
ORDER_BUF = pltpu.VMEM((2, EXP, EXP), B)
SEMS = pltpu.SemaphoreType.DMA((8,))
ROWS_OUT = jax.ShapeDtypeStruct((ROWS, D), B)
COND_OUT = jax.ShapeDtypeStruct((8, D), F)
HALF_OUT = jax.ShapeDtypeStruct((EXP, P_HALF), B)
PACK_BUF = pltpu.VMEM((2, EXP, P_HALF), B)


def cost(units):
    return pl.CostEstimate(flops=units * 2_000_000_000, bytes_accessed=units * 10_000_000, transcendentals=units * 2_000_000)


def front(place, blocks, x, cond):
    outs = [ROWS_OUT] + shapes(KEEP) + shapes(WEIGHTS) + shapes(MOD)
    return pl.pallas_call(
        front_kernel,
        out_shape=outs,
        in_specs=[SM] + [ANY] * 8 + [VM] * 2,
        out_specs=[VM] + [ANY] * (len(outs) - 1),
        scratch_shapes=buffers(KEEP + WEIGHTS + MOD)
        + [G_BUF, SELT_BUF, SELT_BUF, ORDER_BUF, SEMS, pltpu.SemaphoreType.DMA((len(outs) - 1,))],
        compiler_params=PARAMS,
        cost_estimate=cost(1),
        name="front",
    )(place, *blocks, x, cond)


def turn(place, blocks, x, cond, grad):
    return pl.pallas_call(
        turn_kernel,
        out_shape=[ROWS_OUT, ROWS_OUT, COND_OUT, HALF_OUT, HALF_OUT],
        in_specs=[SM] + [ANY] * 8 + [VM] * 3,
        out_specs=[VM] * 3 + [ANY] * 2,
        scratch_shapes=buffers(KEEP) + buffers(WEIGHTS) + buffers(TEMPS) + buffers(MOD) + [G_BUF, SEL_BUF, SELT_BUF, SELT_BUF, ORDER_BUF, PACK_BUF, SEMS],
        compiler_params=PARAMS,
        cost_estimate=cost(3),
        name="turn",
    )(place, *blocks, x, cond, grad)


def back(place, blocks, x, cond, grad, kept):
    return pl.pallas_call(
        back_kernel,
        out_shape=[ROWS_OUT, COND_OUT, HALF_OUT, HALF_OUT],
        in_specs=[SM] + [ANY] * 8 + [VM] * (3 + len(kept)),
        out_specs=[VM] * 2 + [ANY] * 2,
        scratch_shapes=buffers(TEMPS) + [ADA_BUF, SEL_BUF, SELT_BUF, PACK_BUF, SEMS],
        compiler_params=PARAMS,
        cost_estimate=cost(2),
        name="back",
    )(place, *blocks, x, cond, grad, *kept)


def line_up_kernel(w_qkv, w_proj, w_fc1, w_fc2, w_ada, b_qv, b_proj, b_fc1, b_fc2, b_ada, out, main, ada, bias):
    def rows(ref, first, last):
        return ref[:, first:last].astype(F)

    main[0:6, :] = rows(w_qkv, 0, QUARTER)
    main[6:12, :384] = rows(w_qkv, QUARTER, C_PROJ)
    main[6:12, 384:] = rows(w_proj, 0, D)
    main[12:18, :] = rows(w_fc1, 0, QUARTER)
    main[18:24, :] = rows(w_fc1, QUARTER, FF)
    ada[48:56, :] = jnp.zeros((8, 256), F)
    for i in range(9):
        ada[6 * i : 6 * i + 6, :] = rows(w_ada, 256 * i, 256 * i + 256)
    for a in range(3):
        out[:, a * QUARTER : (a + 1) * QUARTER] = main[8 * a : 8 * a + 8, :].astype(B)
        out[:, G_FC2 + a * D : G_FC2 + (a + 1) * D] = w_fc2[8 * a : 8 * a + 8, :]
    for a in range(7):
        out[:, G_ADA + a * 256 : G_ADA + (a + 1) * 256] = ada[8 * a : 8 * a + 8, :].astype(B)
    bias[...] = jnp.zeros((8, 128), F)
    for ref, (lane, width) in zip((b_qv, b_proj, b_fc1, b_fc2, b_ada), BIASES):
        bias[0:1, lane : lane + width] = ref[...].astype(F)
    out[:, G_BIAS:G_END] = bias[...].astype(B)


def line_up(w_qkv, b_qv, w_proj, b_proj, w_fc1, b_fc1, w_fc2, b_fc2, w_ada, b_ada):
    biases = [b.reshape(1, -1) for b in (b_qv, b_proj, b_fc1, b_fc2, b_ada)]
    return pl.pallas_call(
        line_up_kernel,
        out_shape=jax.ShapeDtypeStruct((8, G_END), B),
        in_specs=[VM] * 10,
        out_specs=VM,
        scratch_shapes=[pltpu.VMEM((24, QUARTER), F), pltpu.VMEM((56, 256), F), pltpu.VMEM((8, 128), F)],
        name="line_up",
    )(w_qkv, w_proj, w_fc1, w_fc2, w_ada, *biases)


def swap(x):
    return lax.ppermute(x, "pipe", [(0, 1), (1, 0)])


def gather_stage(block, stage):
    def behind(by):
        pairs = []
        for core in range(2):
            stride = STRIDES[STAGES[core][stage]]
            for i in range(CHIPS):
                at = (i // stride) % 4
                pairs.append((core * CHIPS + i, core * CHIPS + i + ((at + by) % 4 - at) * stride))
        return lax.ppermute(block, ("pipe", "shard"), pairs)

    return [block] + [behind(by) for by in (1, 2, 3)]


def scatter(block):
    return lax.all_to_all(block.reshape(CHIPS, 8, P_HALF), "shard", 0, 0, tiled=True)


def shards(latents, conditions, cotangent, w_qkv, b_qv, w_proj, b_proj, w_fc1, b_fc1, w_fc2, b_fc2, w_ada, b_ada):
    p = lax.axis_index("pipe")
    j = lax.axis_index("shard")
    first = p == 0
    place = jnp.stack([p, j >> 4, (j >> 2) & 3, j & 3]).astype(jnp.int32)
    block = line_up(w_qkv[0], b_qv[0], w_proj[0], b_proj[0], w_fc1[0], b_fc1[0], w_fc2[0], b_fc2[0], w_ada[0], b_ada[0])
    block_other = swap(block)
    low = jnp.where(first, block[:, :G_HALF], block_other[:, G_HALF:])
    high = jnp.where(first, block_other[:, :G_HALF], block[:, G_HALF:])
    both = jnp.concatenate([low, high], axis=1)
    for stage in range(2):
        both = jnp.concatenate(gather_stage(both, stage), axis=0)
    own0 = gather_stage(both[:, :G_HALF], 2)
    other0 = [swap(block) for block in own0]
    high, *own0 = lax.optimization_barrier((both[:, G_HALF:], *own0))
    blocks0 = own0 + other0
    own1 = gather_stage(high, 2)
    x = lax.dynamic_index_in_dim(latents, p, 0, keepdims=False).reshape(ROWS, D)
    cot = lax.dynamic_index_in_dim(cotangent, p, 0, keepdims=False).reshape(ROWS, D)
    cond = lax.dynamic_index_in_dim(conditions, p, 0, keepdims=False).astype(F)
    cond = jnp.concatenate([cond, jnp.zeros((6, D), F)], axis=0)

    h, *kept = front(place, blocks0, x, cond)
    h, *own1 = lax.optimization_barrier((h, *own1))
    blocks1 = own1 + [swap(block) for block in own1]
    y, dx1, dc1, keep1, send1 = turn(place, blocks1, h, cond, cot)
    parts1 = scatter(keep1 + swap(send1))
    dx0, dc0, keep0, send0 = back(place, blocks0, x, cond, dx1, kept)
    parts1, send0 = lax.optimization_barrier((parts1, send0))
    parts0 = scatter(keep0 + swap(send0))

    def pair(for_first, for_second):
        keep = jnp.where(first, for_first, for_second)
        came = swap(jnp.where(first, for_second, for_first))
        both = jnp.where(first, jnp.stack([keep, came]), jnp.stack([came, keep]))
        return both.reshape(1, 2, 2, SEQ, D)

    section_outputs = pair(h, y)
    input_grads = pair(dx0, dx1)
    dc = (dc0 + dc1)[:2]
    dc_other = swap(dc)
    cond_grad = jnp.where(first, jnp.stack([dc, dc_other]), jnp.stack([dc_other, dc]))

    parts0, section_outputs, input_grads, cond_grad = lax.optimization_barrier(
        (parts0, section_outputs, input_grads, cond_grad)
    )

    def reduced(parts):
        lot = jnp.sum(parts.astype(F), axis=0)
        flat = parts.reshape(EXP, P_HALF)
        ada = lax.dot_general(
            flat[:, P_COND : P_COND + 16], flat[:, P_MOD:P_COND], (((0,), (0,)), ((), ())), preferred_element_type=F
        )
        return jnp.concatenate([lot, ada[:8], ada[8:]], axis=1)

    lot0 = reduced(parts0)
    lot1 = reduced(parts1)
    kept_half = jnp.where(first, lot0, lot1)
    came_half = swap(jnp.where(first, lot1, lot0))
    low = jnp.where(first, kept_half, came_half)
    high = jnp.where(first, came_half, kept_half)

    rows = jnp.concatenate([low[:, a * QUARTER : (a + 1) * QUARTER] for a in range(3)], axis=0)
    quarters = [rows[6 * q : 6 * q + 6] for q in range(4)]
    def bias(i):
        at, width = BIASES[i]
        return high[0, P_BIAS + at : P_BIAS + at + width]

    outs = (
        jnp.concatenate([quarters[0], quarters[1][:, :384]], axis=1),
        bias(0),
        quarters[1][:, 384:],
        bias(1),
        jnp.concatenate([quarters[2], quarters[3]], axis=1),
        bias(2),
        jnp.concatenate([high[:, a * D : (a + 1) * D] for a in range(3)], axis=0),
        bias(3),
        jnp.concatenate([high[:6, P_HALF : P_HALF + 1152], high[:6, P_HALF + 1152 :]], axis=1),
        bias(4),
    )
    return (section_outputs, input_grads, cond_grad) + tuple(o[None] for o in outs)


def solution(mesh):
    rows = P(None, "shard", None, None)
    wide = P("pipe", "shard", None)
    thin = P("pipe", "shard")
    both = P("pipe", None, "shard", None, None)
    pairs = (wide, thin) * 5
    return jax.shard_map(
        shards,
        mesh=mesh,
        in_specs=(rows, P(None, "shard", None), rows) + pairs,
        out_specs=(both, both, P(None, "shard", None)) + pairs,
        check_vma=False,
    )
```
